32 devices in a mesh: ctx: 8 (over z, core), fsdp: 4 (over y, x).
Axes of the slice: x: 2, y: 2, z: 4, core: 2. Of those that a mesh axis runs over, the one named last changes fastest.
Arguments:
- x_prompt: bfloat16 [512, 1024], P('ctx'), may hold values from -6 to 6
- x_cont: bfloat16 [32, 1024, 1024], P(('ctx', 'fsdp')), may hold values from -6 to 6
- dy_prompt: bfloat16 [512, 1024], P('ctx'), may hold values from -6 to 6
- dy_cont: bfloat16 [32, 1024, 1024], P(('ctx', 'fsdp')), may hold values from -6 to 6
- adapter_ids: int32 [32], P(('ctx', 'fsdp')), may hold values from 0 to 7, as said below
- w_qkv: bfloat16 [1024, 3072], P(None, 'fsdp'), may hold values from -0.1875 to 0.1875
- w_out: bfloat16 [1024, 1024], P(None, 'fsdp'), may hold values from -1.5 to 1.5
- w_up: bfloat16 [1024, 4096], P(None, 'fsdp'), may hold values from -0.1875 to 0.1875
- w_down: bfloat16 [4096, 1024], P(None, 'fsdp'), may hold values from -0.09375 to 0.09375
- frozen_bias: float32 [9216], replicated, may hold values from -1.2 to 1.2
- norm_gain: float32 [2, 1024], replicated, may hold values from 0.5 to 1.5
- norm_shift: float32 [2, 1024], replicated, may hold values from -1.8 to 1.8
- adapters: float32 [8, 16, 16384], P('fsdp'), may hold values from -1 to 1
- first_moment: float32 [8, 16, 16384], P('fsdp'), may hold values from -0.066 to 0.066
- second_moment: float32 [8, 16, 16384], P('fsdp'), may hold values from 1e-05 to 4e-05
Outputs:
- prompt_out: float32 [512, 1024], P('ctx')
- prompt_grad: float32 [512, 1024], P('ctx')
- cont_out: float32 [32, 1024, 1024], P(('ctx', 'fsdp'))
- cont_grad: float32 [32, 1024, 1024], P(('ctx', 'fsdp'))
- grad_norm: float32 [], replicated
- new_adapters: float32 [8, 16, 16384], P('fsdp')
- new_first: float32 [8, 16, 16384], P('fsdp')
- new_second: float32 [8, 16, 16384], P('fsdp')
- adapter_copy: bfloat16 [8, 16, 16384], P('fsdp')
The draws below stay inside these ranges and needn't reach their ends.
Inputs may be any that keep to these rules, and one draw needn't show every extreme that they name: `adapter_ids`: each entry names one of the 8 adapter sets.
All inputs are finite; a program needn't handle non-finite values.
Results may differ from the reference program's by a relative error of at most 0.017.
The reference program's roundings to bfloat16 on the way count: a program that leaves them out, or rounds other values in their place, can miss the bound.
Values may be sent and summed in bfloat16 or wider, within the bound.
A program may use at most 320 MiB of HBM per device.

```python
import jax
import jax.numpy as jnp
from jax import lax

D = 1024
H = 16
HD = 64
ROT = 16
FF = 4096
R = 16
SETS = 8
L = 1024
STEP = 10
P_SIZE = 512
CONTS = 32
WTOT = 16384


def draw_adapter_ids(key, part):
    key = jax.random.fold_in(key, 7)
    rolled = jax.random.randint(key, (CONTS,), 0, SETS * (SETS + 1) // 2)
    bounds = jnp.cumsum(jnp.arange(1, SETS, dtype=jnp.int32))
    return jnp.sum((rolled[:, None] >= bounds[None, :]).astype(jnp.int32), axis=1).astype(jnp.int32)


def draw_adapters(key, part):
    key = jax.random.fold_in(key, 11)
    normals = jnp.clip(jax.random.normal(key, (SETS, R, WTOT), jnp.float32), -4.0, 4.0)
    column = jnp.arange(WTOT)
    is_up = (column >= D) & (column < 4 * D) | (column >= 5 * D) & (column < 6 * D) | (column >= 7 * D) & (column < 7 * D + FF) | (column >= 7 * D + 2 * FF)
    is_wide = (column >= 7 * D + FF) & (column < 7 * D + 2 * FF)
    column_scale = jnp.where(is_up, R ** (-0.5), jnp.where(is_wide, FF ** (-0.5), D ** (-0.5)))
    return (normals * column_scale[None, None, :]).astype(jnp.float32)


def block_scale(own_key, shape, cuts, low, largest):
    def one(dim, parts):
        draws = jax.random.uniform(jax.random.fold_in(jax.random.fold_in(own_key, 6), dim), (parts,), jnp.float32, low / len(cuts), largest / len(cuts))
        return jnp.repeat(jnp.exp(draws), shape[dim] // parts).reshape((-1,) + (1,) * (len(shape) - dim - 1))

    level = one(*cuts[0])
    for cut in cuts[1:]:
        level = level * one(*cut)
    return level


def scatter_about(rng, extent, deviation, reach, cuts=(), kind=jnp.bfloat16):
    values = jax.random.normal(rng, extent, jnp.float32) * deviation
    if len(cuts) > 0:
        values = block_scale(rng, extent, cuts, -0.22, 0.18) * values
    return jnp.clip(values, min=-reach, max=reach).astype(kind)


def setup_inputs(seed: int = 0) -> dict:
    seeds = jax.random.split(jax.random.key(seed), 16)
    return {
        "x_prompt": scatter_about(seeds[0], (P_SIZE, D), 1.0, 6.0, ((0, 8),)),
        "x_cont": scatter_about(seeds[1], (CONTS, L, D), 1.0, 6.0, ((0, 32),)),
        "dy_prompt": scatter_about(seeds[2], (P_SIZE, D), 1.0, 6.0, ((0, 8),)),
        "dy_cont": scatter_about(seeds[3], (CONTS, L, D), 1.0, 6.0, ((0, 32),)),
        "adapter_ids": draw_adapter_ids(jax.random.fold_in(seeds[15], 71), 0),
        "w_qkv": scatter_about(seeds[5], (D, 3 * D), D ** -0.5, 0.1875, ((1, 4),)),
        "w_out": scatter_about(seeds[6], (D, D), (D // 64) ** -0.5, 1.5, ((1, 4),)),
        "w_up": scatter_about(seeds[7], (D, FF), D ** -0.5, 0.1875, ((1, 4),)),
        "w_down": scatter_about(seeds[8], (FF, D), FF ** -0.5, 0.09375, ((1, 4),)),
        "frozen_bias": scatter_about(seeds[9], (5 * D + FF,), 0.2, 1.2, (), jnp.float32),
        "norm_gain": jnp.clip(1.0 + 0.1 * jax.random.normal(seeds[10], (2, D), jnp.float32), 0.5, 1.5),
        "norm_shift": scatter_about(seeds[11], (2, D), 0.3, 1.8, (), jnp.float32),
        "adapters": draw_adapters(jax.random.fold_in(seeds[15], 71), 0),
        "first_moment": scatter_about(seeds[13], (SETS, R, WTOT), 0.011, 0.066, ((0, 4),), jnp.float32),
        "second_moment": jnp.clip(9.999999747378752e-06 + 2.9999999242136255e-05 * jax.random.uniform(seeds[14], (SETS, R, WTOT), jnp.float32) ** block_scale(seeds[14], (SETS, R, WTOT), ((0, 4),), -0.2, 0.2), 9.999999747378752e-06, 3.9999998989515007e-05),
    }


@jax.custom_vjp
def low(v):
    return lax.optimization_barrier(v.astype(jnp.bfloat16)).astype(jnp.float32)

@jax.custom_vjp
def low_back(v):
    return v

def low_keep(v):
    return (low(v), None)

def low_pass(kept, grad):
    return (grad,)

def back_keep(v):
    return (v, None)

def back_low(kept, grad):
    return (low(grad),)
low.defvjp(low_keep, low_pass)
low_back.defvjp(back_keep, back_low)
highest = lax.Precision.HIGHEST
beta_one = 0.9
beta_two = 0.999
adam_eps = 1e-08
weight_decay = 0.01
rate_down = 0.05
rate_up = 0.5

def matmul(left, right):
    return jnp.dot(left, right, precision=highest, preferred_element_type=jnp.float32)

def matmul_bt(left, right):
    return lax.dot_general(left, right, (((1,), (1,)), ((), ())), precision=highest, preferred_element_type=jnp.float32)

def layer_norm(values, gain_row, shift_row):
    row_mean = lax.optimization_barrier(jnp.mean(values, axis=-1, keepdims=True))
    centered = values - row_mean
    variance = lax.optimization_barrier(jnp.mean(centered * centered, axis=-1, keepdims=True))
    return centered * lax.rsqrt(variance + 1e-05) * gain_row + shift_row

def rotary(values, positions):
    heads = values.reshape(values.shape[0], H, HD)
    half_rot = ROT // 2
    frequency = 10000.0 ** (-2.0 * jnp.arange(half_rot, dtype=jnp.float32) / ROT)
    angles = positions.astype(jnp.float32)[:, None] * frequency[None, :]
    cosine = jnp.cos(angles)[:, None, :]
    sine_part = jnp.sin(angles)[:, None, :]
    first_half = heads[:, :, :half_rot]
    second_half = heads[:, :, half_rot:ROT]
    turned = jnp.concatenate([first_half * cosine - second_half * sine_part, second_half * cosine + first_half * sine_part, heads[:, :, ROT:]], axis=-1)
    return turned.reshape(values.shape[0], H * HD)

def up_columns():
    column = jnp.arange(WTOT)
    return (column >= D) & (column < 4 * D) | (column >= 5 * D) & (column < 6 * D) | (column >= 7 * D) & (column < 7 * D + FF) | (column >= 7 * D + 2 * FF)

def split_sets(packed):
    return (packed[:, :D], packed[:, D:4 * D], packed[:, 4 * D:5 * D], packed[:, 5 * D:6 * D], packed[:, 6 * D:7 * D], packed[:, 7 * D:7 * D + FF], packed[:, 7 * D + FF:7 * D + 2 * FF], packed[:, 7 * D + 2 * FF:])

def adapter_path(inputs, down_map, up_map):
    middle = low(low_back(matmul_bt(inputs, down_map)))
    return matmul(middle, up_map)

def attend(queries, key_rows, value_rows, allowed):
    query_heads = queries.reshape(queries.shape[0], H, HD)
    key_heads = key_rows.reshape(key_rows.shape[0], H, HD)
    value_heads = value_rows.reshape(value_rows.shape[0], H, HD)
    scores = low_back(jnp.einsum('qhd,khd->hqk', query_heads, key_heads, precision=highest) * HD ** (-0.5))
    scores = jnp.where(allowed[None], scores, -1e+30)
    weights = low(jax.nn.softmax(scores, axis=-1))
    mixed = jnp.einsum('hqk,khd->qhd', weights, value_heads, precision=highest)
    return mixed.reshape(queries.shape[0], H * HD)

def front_half(inputs, frozen, pieces, positions):
    w_qkv, w_out, w_up, w_down, frozen_bias, norm_gain, norm_shift = frozen
    attn_in = low(layer_norm(inputs, norm_gain[0], norm_shift[0]))
    mlp_in = low(layer_norm(inputs, norm_gain[1], norm_shift[1]))
    qkv_rows = matmul(attn_in, w_qkv) + frozen_bias[:3 * D]
    if pieces is not None:
        qkv_rows = qkv_rows + adapter_path(attn_in, pieces[0], pieces[1])
    qkv_rows = low_back(qkv_rows)
    queries = low(rotary(qkv_rows[:, :D], positions))
    key_rows = low(rotary(qkv_rows[:, D:2 * D], positions))
    value_rows = low(qkv_rows[:, 2 * D:])
    return (mlp_in, queries, key_rows, value_rows)

def back_half(inputs, mlp_in, mixed, frozen, pieces):
    w_qkv, w_out, w_up, w_down, frozen_bias, norm_gain, norm_shift = frozen
    attended = low(low_back(mixed))
    branch_attn = matmul(attended, w_out) + frozen_bias[3 * D:4 * D]
    up_proj = matmul(mlp_in, w_up) + frozen_bias[4 * D:4 * D + FF]
    if pieces is not None:
        branch_attn = branch_attn + adapter_path(attended, pieces[2], pieces[3])
        up_proj = up_proj + adapter_path(mlp_in, pieces[4], pieces[5])
    hidden = low(jax.nn.gelu(low_back(up_proj), approximate=False))
    branch_mlp = matmul(hidden, w_down) + frozen_bias[4 * D + FF:]
    if pieces is not None:
        branch_mlp = branch_mlp + adapter_path(hidden, pieces[6], pieces[7])
    return inputs + branch_attn + branch_mlp

def forward(x_prompt, x_cont, adapters, adapter_ids, frozen):
    rounded_sets = low(adapters)
    prompt_positions = jnp.arange(P_SIZE, dtype=jnp.int32)
    mlp_prompt, q_prompt, k_prompt, v_prompt = front_half(x_prompt, frozen, None, prompt_positions)
    causal = prompt_positions[None, :] <= prompt_positions[:, None]
    out_prompt = back_half(x_prompt, mlp_prompt, attend(q_prompt, k_prompt, v_prompt, causal), frozen, None)
    cont_positions = P_SIZE + jnp.arange(L, dtype=jnp.int32)
    key_positions = jnp.arange(P_SIZE + L, dtype=jnp.int32)
    allowed = key_positions[None, :] <= cont_positions[:, None]

    def one_cont(pair):
        rows_in, set_index = pair
        pieces = split_sets(lax.dynamic_index_in_dim(rounded_sets, set_index, 0, keepdims=False))
        mlp_cont, q_cont, k_cont, v_cont = front_half(rows_in, frozen, pieces, cont_positions)
        key_rows = jnp.concatenate([k_prompt, k_cont], axis=0)
        value_rows = jnp.concatenate([v_prompt, v_cont], axis=0)
        return back_half(rows_in, mlp_cont, attend(q_cont, key_rows, value_rows, allowed), frozen, pieces)
    out_cont = lax.map(jax.checkpoint(one_cont), (x_cont, adapter_ids))
    return (out_prompt, out_cont)

def reference(x_prompt, x_cont, dy_prompt, dy_cont, adapter_ids, w_qkv, w_out, w_up, w_down, frozen_bias, norm_gain, norm_shift, adapters, first_moment, second_moment):
    frozen = (w_qkv.astype(jnp.float32), w_out.astype(jnp.float32), w_up.astype(jnp.float32), w_down.astype(jnp.float32), frozen_bias, norm_gain, norm_shift)

    def wrapped(prompt_in, cont_in, packed):
        return forward(prompt_in, cont_in, packed, adapter_ids, frozen)
    (prompt_out, cont_out), pullback = jax.vjp(wrapped, x_prompt.astype(jnp.float32), x_cont.astype(jnp.float32), adapters)
    prompt_grad, cont_grad, gradient = pullback((dy_prompt.astype(jnp.float32), dy_cont.astype(jnp.float32)))
    grad_norm = jnp.sqrt(jnp.sum(gradient * gradient))
    limit = 0.1 * jnp.sqrt(jnp.float32(SETS * R * WTOT))
    clipped = gradient * (limit / jnp.maximum(grad_norm, limit))
    new_first = beta_one * first_moment + (1.0 - beta_one) * clipped
    new_second = beta_two * second_moment + (1.0 - beta_two) * clipped * clipped
    corrected_first = new_first / (1.0 - beta_one ** STEP)
    corrected_second = new_second / (1.0 - beta_two ** STEP)
    step_rates = jnp.where(up_columns(), rate_up, rate_down)
    new_adapters = adapters - step_rates * (corrected_first / (jnp.sqrt(corrected_second) + adam_eps) + weight_decay * adapters)
    return (prompt_out, prompt_grad, cont_out, cont_grad, grad_norm, new_adapters, new_first, new_second, new_adapters.astype(jnp.bfloat16))
```

```python
import functools
import math

import jax
import jax.numpy as jnp
import numpy as np
from jax import lax
from jax.experimental import pallas as pl
from jax.experimental.pallas import tpu as pltpu
from jax.sharding import PartitionSpec as P

D = 1024
H = 16
HD = 64
ROT = 16
FF = 4096
R = 16
SETS = 8
STEP = 10
WTOT = 16384


beta_one = 0.9
beta_two = 0.999
adam_eps = 1e-08
weight_decay = 0.01
rate_down = 0.05
rate_up = 0.5
masked_score = -1e30
KEY_TILE = 256
QUERY_TILE = 256
SPAN = 768
PIECE = 64
LINES = 32
MLP_ROWS = 272
ROW_TILE = 512
OUT_TILE = 272
VMEM_BYTES = 62 * 1024 * 1024


def matmul(left, right):
    return jnp.dot(left, right, preferred_element_type=jnp.float32)


def matmul_bt(left, right):
    return lax.dot_general(
        left, right, (((1,), (1,)), ((), ())), preferred_element_type=jnp.float32
    )


def matmul_at(left, right):
    return lax.dot_general(
        left, right, (((0,), (0,)), ((), ())), preferred_element_type=jnp.float32
    )


def up_columns():
    column = np.arange(WTOT)
    return (
        (column >= D) & (column < 4 * D)
        | (column >= 5 * D) & (column < 6 * D)
        | (column >= 7 * D) & (column < 7 * D + FF)
        | (column >= 7 * D + 2 * FF)
    )


def pair_turn(values, cosine, low_sine, high_sine):
    return (
        values * cosine
        + pltpu.roll(values, 2 * HD - ROT // 2, 1) * low_sine
        + pltpu.roll(values, ROT // 2, 1) * high_sine
    )


def pair_turn_back(values, cosine, low_sine, high_sine):
    return (
        values * cosine
        - pltpu.roll(values, 2 * HD - ROT // 2, 1) * low_sine
        - pltpu.roll(values, ROT // 2, 1) * high_sine
    )


MESH = pl.DeviceIdType.MESH


def flip(place, mask):
    bit = 1
    while bit <= mask:
        if mask & bit:
            place = place + bit - 2 * bit * ((place // bit) % 2)
        bit *= 2
    return place


class Relay:
    def __init__(self, count):
        bits = [1 << index for index in range(count.bit_length() - 1)]
        self.count = count
        self.orders = (bits, bits[1:] + bits[:1])
        self.masks = []
        for order in self.orders:
            masks = [0]
            for bit in order:
                masks += [mask ^ bit for mask in masks]
            self.masks.append(masks)
        self.levels = [
            [held for held in range(1, count) if bin(held).count("1") == level]
            for level in range(1, count.bit_length())
        ]
        self.ctx, self.me = lax.axis_index("ctx"), lax.axis_index("fsdp")
        self.parity = self.ctx % 2
        self.sibling = self.ctx + 1 - 2 * self.parity

    def blend(self, even, odd, other):
        side = 1 - self.parity if other else self.parity
        return even + side * (odd - even)

    def partner(self, turn, stage):
        even, odd = (flip(self.me, self.orders[order][stage]) for order in (turn, 1 - turn))
        return self.blend(even, odd, False)

    def slot(self, turn, held, other=False):
        even, odd = (flip(self.me, self.masks[order][held]) for order in (turn, 1 - turn))
        return self.blend(even, odd, other)

    def greet(self, others=()):
        barrier = pltpu.get_barrier_semaphore()
        peers = [(self.ctx, flip(self.me, bit)) for bit in self.orders[0]]
        peers += [(self.sibling, self.me)] + list(others)
        for peer in peers:
            pl.semaphore_signal(barrier, inc=1, device_id=peer, device_id_type=MESH)
        pl.semaphore_wait(barrier, len(peers))


class Gathered:
    def __init__(self, relay, shard, slots, cut, sems, resident=False):
        self.resident = resident
        self.relay, self.shard, self.slots, self.cut = relay, shard, slots, cut
        self.send_sems, self.recv_sems, self.give_sems, self.take_sems, self.own_sem = sems

    def part(self, slot, turn, parity):
        return self.cut(self.slots.at[slot], 2 * parity + turn)

    def own(self):
        return pltpu.make_async_copy(self.shard, self.slots.at[self.relay.me], self.own_sem)

    def remote(self, source, target, sems, turn, held, device):
        index = turn * (self.relay.count - 1) + held - 1
        return pltpu.make_async_remote_copy(
            src_ref=source,
            dst_ref=target,
            send_sem=sems[0].at[index],
            recv_sem=sems[1].at[index],
            device_id=device,
            device_id_type=MESH,
        )

    def message(self, turn, held):
        relay = self.relay
        stage = held.bit_length() - 1
        before = held - (1 << stage)
        target = self.part(relay.slot(turn, before), turn, relay.parity)
        outside = before == 0 and not self.resident
        source = self.cut(self.shard, 2 * relay.parity + turn) if outside else target
        device = (relay.ctx, relay.partner(turn, stage))
        return self.remote(source, target, (self.send_sems, self.recv_sems), turn, held, device)

    def arrival(self, turn, held):
        relay = self.relay
        part = self.part(relay.slot(turn, held), turn, relay.parity)
        device = (relay.ctx, relay.partner(turn, held.bit_length() - 1))
        return self.remote(part, part, (self.send_sems, self.recv_sems), turn, held, device)

    def gift(self, turn, held, taken=False):
        relay = self.relay
        side = 1 - relay.parity if taken else relay.parity
        part = self.part(relay.slot(turn, held, taken), turn, side)
        device = (relay.sibling, relay.me)
        return self.remote(part, part, (self.give_sems, self.take_sems), turn, held, device)

    def start(self):
        if self.resident:
            self.own().wait()
        for held in self.relay.levels[0]:
            for turn in range(2):
                self.message(turn, held).start()
        if not self.resident:
            self.own().start()

    def forward(self, level):
        for held in self.relay.levels[level]:
            for turn in range(2):
                self.arrival(turn, held).wait_recv()
                for stage in range(held.bit_length(), len(self.relay.orders[0])):
                    self.message(turn, (1 << stage) + held).start()

    def give(self, level):
        for held in self.relay.levels[level]:
            for turn in range(2):
                self.gift(turn, held).start()

    def advance(self, level):
        self.forward(level)
        self.give(level)

    def places(self, level):
        masks = [mask for mask in range(self.relay.count) if bin(mask).count("1") == level + 1]
        return [flip(self.relay.me, mask) for mask in masks]

    def take(self, level):
        for held in self.relay.levels[level]:
            for turn in range(2):
                self.gift(turn, held, taken=True).wait_recv()

    def finish(self):
        for held in range(1, self.relay.count):
            for turn in range(2):
                self.message(turn, held).wait_send()
                self.gift(turn, held).wait_send()


def relay_sems(arrays, count):
    return [pltpu.SemaphoreType.DMA((arrays, 2 * (count - 1))) for _ in range(4)] + [
        pltpu.SemaphoreType.DMA((arrays,))
    ]


def sems_of(sems, index):
    return [sem.at[index] for sem in sems]


def row_quarter(ref, index):
    size = ref.shape[0] // 4
    return ref.at[pl.ds(pl.multiple_of(index * size, size), size)]


def lane_quarter(ref, index):
    size = ref.shape[-1] // 4
    return ref.at[:, :, pl.ds(pl.multiple_of(index * size, size), size)]


def remote_copy(source, target, sems, index, device):
    return pltpu.make_async_remote_copy(
        src_ref=source,
        dst_ref=target,
        send_sem=sems[0].at[index],
        recv_sem=sems[1].at[index],
        device_id=device,
        device_id_type=MESH,
    )


def greet_all(peers):
    barrier = pltpu.get_barrier_semaphore()
    for peer in peers:
        pl.semaphore_signal(barrier, inc=1, device_id=peer, device_id_type=MESH)
    pl.semaphore_wait(barrier, len(peers))


def ring(place, count, offset):
    return (place + offset) % count


class Trade:
    def __init__(self, axis, count, source, slots, sems):
        self.axis, self.count, self.source, self.slots = axis, count, source, slots
        self.places = {name: lax.axis_index(name) for name in ("ctx", "fsdp")}
        self.me = self.places[axis]
        self.sems = sems

    def device(self, place):
        return tuple(place if name == self.axis else self.places[name] for name in self.places)

    def send(self, offset):
        place = ring(self.me, self.count, offset)
        return remote_copy(
            self.source(place), self.slots.at[self.me], self.sems, offset - 1, self.device(place)
        )

    def start(self):
        for offset in range(1, self.count):
            self.send(offset).start()

    def wait(self):
        for offset in range(1, self.count):
            place = ring(self.me, self.count, self.count - offset)
            part = self.slots.at[place]
            remote_copy(part, part, self.sems, offset - 1, self.device(place)).wait_recv()

    def finish(self):
        for offset in range(1, self.count):
            self.send(offset).wait_send()


def trade_sems(count):
    return [pltpu.SemaphoreType.DMA((count - 1,)) for _ in range(2)]


def together(main, main_count, side, side_count):
    done = 0
    for index in range(main_count):
        next(main, None)
        while done < (index + 1) * side_count // main_count:
            next(side, None)
            done += 1
    for generator in (main, side):
        for _ in generator:
            pass


def chain(*generators):
    for generator in generators:
        yield from generator


def front_kernel(
    length,
    ids_ref,
    x_ref,
    xp_ref,
    dy_ref,
    dyp_ref,
    wq_ref,
    wo_ref,
    sets_ref,
    bias_ref,
    gain_ref,
    shift_ref,
    cos_ref,
    low_ref,
    high_ref,
    qkv_out,
    a1_out,
    a2_out,
    dob_out,
    g_out,
    wq_out,
    wo_out,
    low_out,
    picked,
    mid_ref,
    d_mid_ref,
    wq,
    wo,
    ad,
    sets,
    low_sets,
    xp,
    a1,
    a2,
    g,
    qkv,
    dob,
    mid_keys,
    *sems,
):
    wq_sems, wo_sems, ad_sems = (sems_of(sems[:5], index) for index in range(3))
    xp_send, xp_recv, xp_give, xp_take, load_sems, store_sems, column_sems = sems[5:]
    slots, _, share = wq.shape
    chunk = math.gcd(share, 256)
    per = share // chunk
    owned = ad.shape[1]
    prompt_rows = xp_ref.shape[0]
    prompt_total = xp.shape[0]
    keys = a1.shape[0]
    rows = g.shape[0]
    relay = Relay(slots)
    ctx, parity = relay.ctx, relay.parity
    lines = prompt_total // prompt_rows // 2
    line = ctx // 2

    def line_place(offset, side):
        return ((line + offset) % lines) * 2 + side

    def prompt_piece(place):
        return xp.at[pl.ds(pl.multiple_of(place * prompt_rows, prompt_rows), prompt_rows)]

    loads = [
        pltpu.make_async_copy(x_ref, dob.at[pl.ds(0, length)], load_sems.at[0]),
        pltpu.make_async_copy(dy_ref, g.at[pl.ds(0, length)], load_sems.at[1]),
        pltpu.make_async_copy(dyp_ref, g.at[pl.ds(length, prompt_rows)], load_sems.at[2]),
        pltpu.make_async_copy(xp_ref, prompt_piece(ctx), load_sems.at[3]),
        pltpu.make_async_copy(sets_ref, sets, load_sems.at[4]),
    ]
    for load in reversed(loads):
        load.start()

    adapters = Gathered(relay, low_sets.at[:, :, pl.ds(0, 6 * D)], ad, lane_quarter, ad_sems)
    qkv_weights = Gathered(relay, wq_ref, wq, row_quarter, wq_sems, True)
    out_weights = Gathered(relay, wo_ref, wo, row_quarter, wo_sems, True)
    qkv_weights.own().start()
    out_weights.own().start()
    loads[4].wait()
    for index in range(owned):
        low_sets[index] = sets[index].astype(jnp.bfloat16)
    relay.greet([(line_place(step, parity), relay.me) for step in range(1, lines)])
    adapters.start()
    qkv_weights.start()

    def prompt_send(step):
        return pltpu.make_async_remote_copy(
            src_ref=xp_ref,
            dst_ref=prompt_piece(ctx),
            send_sem=xp_send.at[step],
            recv_sem=xp_recv.at[step],
            device_id=(line_place(step, parity), relay.me),
            device_id_type=MESH,
        )

    def prompt_landed(step):
        piece = prompt_piece(line_place(lines - step, parity))
        return pltpu.make_async_remote_copy(
            src_ref=piece,
            dst_ref=piece,
            send_sem=xp_send.at[step],
            recv_sem=xp_recv.at[step],
            device_id=(line_place(step, parity), relay.me),
            device_id_type=MESH,
        )

    def prompt_gift(step, taken):
        piece = prompt_piece(line_place(lines - step, 1 - parity if taken else parity))
        return pltpu.make_async_remote_copy(
            src_ref=xp_ref if step == 0 and not taken else piece,
            dst_ref=piece,
            send_sem=xp_give.at[step],
            recv_sem=xp_take.at[step],
            device_id=(relay.sibling, relay.me),
            device_id_type=MESH,
        )

    for step in range(1, lines):
        prompt_send(step).start()
    prompt_gift(0, False).start()

    def unit_rows(values):
        values = values.astype(jnp.float32)
        centered = values - jnp.mean(values, axis=-1, keepdims=True)
        variance = jnp.mean(centered * centered, axis=-1, keepdims=True)
        return centered * lax.rsqrt(variance + 1e-05)

    loads[0].wait()
    tile = ROW_TILE

    @pl.loop(0, length // LINES)
    def _(index):
        start = pl.multiple_of(index * LINES, LINES)
        unit = unit_rows(dob[pl.ds(start, LINES), :])
        a1[pl.ds(prompt_total + start, LINES), :] = (
            unit * gain_ref[0:1, :] + shift_ref[0:1, :]
        ).astype(jnp.bfloat16)
        a2[pl.ds(start, LINES), :] = (unit * gain_ref[1:2, :] + shift_ref[1:2, :]).astype(
            jnp.bfloat16
        )

    loads[3].wait()
    unit = unit_rows(prompt_piece(ctx)[...])
    a2[pl.ds(length, prompt_rows), :] = (unit * gain_ref[1:2, :] + shift_ref[1:2, :]).astype(
        jnp.bfloat16
    )
    loads[1].wait()
    loads[2].wait()
    stores = [
        pltpu.make_async_copy(a2, a2_out, store_sems.at[0]),
        pltpu.make_async_copy(g, g_out, store_sems.at[1]),
        pltpu.make_async_copy(low_sets, low_out, store_sems.at[6]),
    ]
    for store in stores:
        store.start()

    last = len(relay.levels) - 1
    for level in range(last + 1):
        adapters.advance(level)
    qkv_weights.advance(0)
    out_weights.start()
    for step in range(1, lines):
        prompt_landed(step).wait_recv()
        prompt_gift(step, False).start()
    adapters.own().wait()
    for level in range(last + 1):
        adapters.take(level)
    mine = ids_ref[0]
    picked[...] = ad[mine // owned, mine % owned]

    mid_keys[pl.ds(0, prompt_total), :] = jnp.zeros((prompt_total, R), jnp.bfloat16)
    d_mid_ref[pl.ds(length, prompt_rows), :] = jnp.zeros((prompt_rows, R), jnp.bfloat16)
    for start in range(0, length, tile):
        at, key_at = pl.ds(start, tile), pl.ds(prompt_total + start, tile)
        middle = matmul_bt(a1[key_at, :], picked[:, :D]).astype(jnp.bfloat16)
        mid_keys[key_at, :] = middle
        mid_ref[at, :] = middle
        d_mid_ref[at, :] = matmul_bt(g[at, :], picked[:, 5 * D : 6 * D]).astype(jnp.bfloat16)
    for step in range(lines):
        prompt_gift(step, True).wait_recv()

    @pl.loop(0, prompt_total // LINES)
    def _(index):
        at = pl.ds(pl.multiple_of(index * LINES, LINES), LINES)
        a1[at, :] = (unit_rows(xp[at, :]) * gain_ref[0:1, :] + shift_ref[0:1, :]).astype(
            jnp.bfloat16
        )

    stores.append(pltpu.make_async_copy(a1, a1_out, store_sems.at[2]))
    stores[-1].start()

    columns = []

    def project(slot):
        for index in range(per):
            col = pl.multiple_of(slot * share + index * chunk, chunk)
            turned = col < 2 * D
            scale = jnp.where(col < D, HD ** (-0.5), 1.0)
            weights = wq[slot, :, index * chunk : (index + 1) * chunk]
            b_part = picked[:, pl.ds(pl.multiple_of(col + D, chunk), chunk)]
            bias = bias_ref[:, pl.ds(col, chunk)]
            for start in range(0, keys, tile):
                at = pl.ds(start, tile)
                result = matmul(a1[at, :], weights) + matmul(mid_keys[at, :], b_part) + bias
                for row in range(0, tile, 128):
                    row_at = pl.ds(start + row, 128)
                    cosine = jnp.where(turned, cos_ref[row_at, :], 1.0)
                    low_sine = jnp.where(turned, low_ref[row_at, :], 0.0)
                    high_sine = jnp.where(turned, high_ref[row_at, :], 0.0)
                    for lane in range(0, chunk, 2 * HD):
                        part = pair_turn(
                            result[row : row + 128, lane : lane + 2 * HD],
                            cosine,
                            low_sine,
                            high_sine,
                        )
                        lane_at = pl.ds(pl.multiple_of(col + lane, 2 * HD), 2 * HD)
                        qkv[row_at, lane_at] = (part * scale).astype(jnp.bfloat16)
            column_at = pl.ds(col, chunk)
            copy = pltpu.make_async_copy(
                qkv.at[:, column_at], qkv_out.at[:, column_at], column_sems.at[len(columns)]
            )
            copy.start()
            columns.append(copy)

    project(relay.me)
    for level in range(last + 1):
        if level < last:
            qkv_weights.advance(level + 1)
        else:
            out_weights.advance(0)
        qkv_weights.take(level)
        for mask in range(1, slots):
            if bin(mask).count("1") == level + 1:
                project(flip(relay.me, mask))
    stores.append(pltpu.make_async_copy(wq, wq_out, store_sems.at[3]))
    stores[-1].start()

    for level in range(1, last + 1):
        out_weights.advance(level)
    for level in range(last + 1):
        out_weights.take(level)
    stores.append(pltpu.make_async_copy(wo, wo_out, store_sems.at[4]))
    stores[-1].start()
    out_share = wo.shape[2]
    for start in range(0, rows, OUT_TILE):
        at = pl.ds(start, min(OUT_TILE, rows - start))
        total = matmul(d_mid_ref[at, :], picked[:, 4 * D : 5 * D])
        for slot in range(slots):
            total += matmul_bt(g[at, pl.ds(slot * out_share, out_share)], wo[slot])
        dob[at, :] = total.astype(jnp.bfloat16)
    stores.append(pltpu.make_async_copy(dob, dob_out, store_sems.at[5]))
    stores[-1].start()

    for array in (adapters, qkv_weights, out_weights):
        array.finish()
    for step in range(1, lines):
        prompt_send(step).wait_send()
    for step in range(lines):
        prompt_gift(step, False).wait_send()
    for copy in columns + stores:
        copy.wait()


def front(ids, x_cont, x_prompt, dy_cont, dy_prompt, w_qkv, w_out, adapters, bias, gain, shift):
    slots = lax.axis_size("fsdp")
    places = lax.axis_size("ctx")
    length, prompt_rows = x_cont.shape[0], x_prompt.shape[0]
    rows, prompt_total = length + prompt_rows, prompt_rows * places
    keys = prompt_total + length
    share, out_share = w_qkv.shape[1], w_out.shape[1]
    owned, wide = adapters.shape[0], 6 * D
    columns = slots * (share // math.gcd(share, 256))
    low = jnp.bfloat16
    anywhere = pl.BlockSpec(memory_space=pl.ANY)
    on_chip = pl.BlockSpec(memory_space=pltpu.VMEM)
    return pl.pallas_call(
        functools.partial(front_kernel, length),
        in_specs=[pl.BlockSpec(memory_space=pltpu.SMEM)] + [anywhere] * 7 + [on_chip] * 6,
        out_specs=[anywhere] * 8 + [on_chip] * 3,
        out_shape=[
            jax.ShapeDtypeStruct((keys, 3 * D), low),
            jax.ShapeDtypeStruct((keys, D), low),
            jax.ShapeDtypeStruct((rows, D), low),
            jax.ShapeDtypeStruct((rows, D), low),
            jax.ShapeDtypeStruct((rows, D), low),
            jax.ShapeDtypeStruct((slots, D, share), low),
            jax.ShapeDtypeStruct((slots, D, out_share), low),
            jax.ShapeDtypeStruct(adapters.shape, low),
            jax.ShapeDtypeStruct((R, wide), low),
            jax.ShapeDtypeStruct((length, R), low),
            jax.ShapeDtypeStruct((rows, R), low),
        ],
        scratch_shapes=[
            pltpu.VMEM((slots, D, share), low),
            pltpu.VMEM((slots, D, out_share), low),
            pltpu.VMEM((slots, owned, R, wide), low),
            pltpu.VMEM(adapters.shape, jnp.float32),
            pltpu.VMEM(adapters.shape, low),
            pltpu.VMEM((prompt_total, D), low),
            pltpu.VMEM((keys, D), low),
            pltpu.VMEM((rows, D), low),
            pltpu.VMEM((rows, D), low),
            pltpu.VMEM((keys, 3 * D), low),
            pltpu.VMEM((rows, D), low),
            pltpu.VMEM((keys, R), low),
        ]
        + relay_sems(3, slots)
        + [pltpu.SemaphoreType.DMA((places // 2,)) for _ in range(4)]
        + [
            pltpu.SemaphoreType.DMA((5,)),
            pltpu.SemaphoreType.DMA((7,)),
            pltpu.SemaphoreType.DMA((columns,)),
        ],
        compiler_params=pltpu.CompilerParams(
            collective_id=1, has_side_effects=True, vmem_limit_bytes=VMEM_BYTES
        ),
        cost_estimate=pl.CostEstimate(
            flops=2 * keys * D * 3 * D + 2 * rows * D * D,
            bytes_accessed=50 * 1024 * 1024,
            transcendentals=rows,
        ),
    )(
        ids,
        x_cont,
        x_prompt,
        dy_cont,
        dy_prompt,
        w_qkv,
        w_out,
        adapters,
        bias,
        gain,
        shift,
        *turn_tables(keys),
    )


def attention_kernel(
    length,
    prompt_total,
    prompt_rows,
    ids_ref,
    q_ref,
    k_ref,
    v_ref,
    do_ref,
    cos_ref,
    low_ref,
    high_ref,
    up_ref,
    down_ref,
    ad_ref,
    picked,
    mid_qkv,
    d_mid_out,
    a1_ref,
    g_ref,
    o_ref,
    dq_ref,
    dk_ref,
    dv_ref,
    kvp_ref,
    up_out,
    down_out,
    chosen_ref,
    grads_ref,
    mid_out_ref,
    d_mid_ref,
    ad_slots,
    up_slots,
    down_slots,
    queries_ref,
    keys_ref,
    values_ref,
    outer_ref,
    keys_t_ref,
    values_t_ref,
    dk_sum,
    dv_sum,
    a1,
    g,
    mid_sum,
    d_mid_sum,
    *sems,
):
    score_scale = HD ** (-0.5)
    key_count = prompt_total + length
    tile = KEY_TILE
    piece_rows = PIECE
    step = pl.program_id(0)
    last_step = H // 2 - 1
    relay = Relay(up_out.shape[0])
    ctx_place = relay.ctx
    first_member = jnp.where(relay.me == 0, 1.0, 0.0)
    back_sets = ad_ref.at[:, :, pl.ds(6 * D, WTOT - 6 * D)]
    resident = len(up_slots.shape) > 2
    if not resident:
        up_slots, down_slots = up_out, down_out
    adapters = Gathered(relay, back_sets, ad_slots, lane_quarter, sems_of(sems[:5], 0), True)
    up_weights = Gathered(relay, up_ref, up_slots, row_quarter, sems_of(sems[:5], 1), resident)
    down_weights = Gathered(relay, down_ref, down_slots, row_quarter, sems_of(sems[:5], 2), resident)
    arrays = (adapters, up_weights, down_weights)
    store_sems, load_sems = sems[5:]
    loads = [
        pltpu.make_async_copy(
            a1_ref.at[pl.ds(prompt_total, length)], a1, load_sems.at[0]
        ),
        pltpu.make_async_copy(g_ref.at[pl.ds(0, length)], g, load_sems.at[1]),
    ]
    levels = len(relay.levels)

    def stores(level):
        if not resident:
            return []
        return [
            pltpu.make_async_copy(array.slots.at[place], out.at[place], store_sems.at[index, place])
            for index, (array, out) in enumerate(((up_weights, up_out), (down_weights, down_out)))
            for place in up_weights.places(level)
        ]

    def store(level):
        for copy in stores(level):
            copy.start()

    late = []

    def at_step(when, action):
        if when > last_step:
            late.append((when, action))
        else:
            pl.when(step == when)(action)

    def begin():
        for load in loads:
            load.start()
        mid_sum[...] = jnp.zeros_like(mid_sum)
        d_mid_sum[...] = jnp.zeros_like(d_mid_sum)
        for array in arrays:
            if array.resident:
                array.own().start()
        relay.greet()
        for array in arrays:
            array.start()

    def settle(level):
        for array in arrays:
            array.take(level)
        store(level)

    def first_arrays(level):
        for array in arrays[:2]:
            array.forward(level)
        for array in arrays[:2]:
            array.give(level)

    at_step(0, begin)
    at_step(2, functools.partial(store, -1))
    for level in range(levels):
        at_step(3 + 3 * level, functools.partial(first_arrays, level))
        at_step(5 + 2 * level, functools.partial(down_weights.advance, level))
        at_step(7 if level < levels - 1 else 20, functools.partial(settle, level))

    wide, low = jnp.float32, jnp.bfloat16
    for start in range(0, key_count, tile):
        at = pl.ds(start, tile)
        queries_ref[at, :] = q_ref[at, :].astype(wide).astype(low)
        piece = k_ref[at, :].astype(wide)
        keys_ref[at, :] = piece.astype(low)
        keys_t_ref[:, at] = piece.T.astype(low)
        piece = v_ref[at, :].astype(wide)
        values_ref[at, :] = piece.astype(low)
        values_t_ref[:, at] = piece.T.astype(low)
    outer_ref[...] = do_ref[...].astype(wide).astype(low)

    class Unit:
        def __init__(self, row_start, rows, position_at, last_key, first, weight, head):
            self.at, self.position_at, self.rows = pl.ds(row_start, rows), position_at, rows
            self.head, self.weight, self.first = head, weight, first
            self.first_row = prompt_total + row_start
            if weight is not None:
                self.first_row = ctx_place * prompt_rows
            self.unmasked = 0 if weight is not None else prompt_total + row_start
            tiles = last_key // tile
            count = -(-last_key // SPAN)
            edges = [tile * (tiles * index // count) for index in range(count + 1)]
            self.spans = list(zip(edges[:-1], edges[1:]))
            self.tiles = range(0, last_key, piece_rows)
            self.scores, self.d_probs, self.raised, self.rounded, self.slopes = {}, {}, {}, {}, {}

        def enter(self):
            lane = lax.broadcasted_iota(jnp.int32, (self.rows, 2 * HD), 1)
            mine = (lane >= self.head * HD) & (lane < (self.head + 1) * HD)
            queries, cotangent = queries_ref[self.position_at, :], outer_ref[self.at, :]
            self.q_head = jnp.where(mine, queries, jnp.zeros_like(queries))
            self.do_head = jnp.where(mine, cotangent, jnp.zeros_like(cotangent))
            for low_edge, high_edge in self.spans:
                at = pl.ds(low_edge, high_edge - low_edge)
                whole = matmul_bt(keys_ref[at, :], self.q_head)
                for start in range(low_edge, high_edge, piece_rows):
                    piece = whole[start - low_edge : start - low_edge + piece_rows]
                    if start + piece_rows > self.unmasked:
                        key_at = start + lax.broadcasted_iota(jnp.int32, piece.shape, 0)
                        row_at = lax.broadcasted_iota(jnp.int32, piece.shape, 1)
                        piece = jnp.where(key_at <= self.first_row + row_at, piece, masked_score)
                    self.scores[start] = piece
                yield
                whole = matmul_bt(values_ref[at, :], self.do_head)
                for start in range(low_edge, high_edge, piece_rows):
                    self.d_probs[start] = whole[start - low_edge : start - low_edge + piece_rows]
                yield

        def soften(self):
            top = None
            for start in self.tiles:
                piece = self.scores[start]
                top = piece if top is None else jnp.maximum(top, piece)
                yield
            top = jnp.max(top, axis=0, keepdims=True)
            total = None
            for start in self.tiles:
                piece = jnp.exp(self.scores[start] - top)
                self.raised[start] = piece
                total = piece if total is None else total + piece
                yield
            inverse = 1.0 / jnp.sum(total, axis=0, keepdims=True)
            delta = None
            for start in self.tiles:
                soft = self.raised[start] * inverse
                self.rounded[start] = soft.astype(low)
                part = soft * self.d_probs[start]
                delta = part if delta is None else delta + part
                yield
            delta = jnp.sum(delta, axis=0, keepdims=True)
            for start in self.tiles:
                soft = self.raised[start] * inverse
                self.slopes[start] = (soft * (self.d_probs[start] - delta)).astype(low)
                yield
            if self.weight is not None:
                self.q_head = (self.q_head.astype(wide) * self.weight).astype(low)
                self.do_head = (self.do_head.astype(wide) * self.weight).astype(low)

        def span_of(self, pieces, span):
            return jnp.concatenate([pieces[start] for start in range(*span, piece_rows)], axis=0)

        def leave(self, partner=None):
            head_at = pl.ds(self.head * HD, HD)
            self.out_t, self.dq_t = None, None
            for span in self.spans:
                at = pl.ds(span[0], span[1] - span[0])
                part = matmul(values_t_ref[head_at, at], self.span_of(self.rounded, span))
                self.out_t = part if self.out_t is None else self.out_t + part
                yield
                part = matmul(keys_t_ref[head_at, at], self.span_of(self.slopes, span))
                self.dq_t = part if self.dq_t is None else self.dq_t + part
                yield
            if partner is None:
                return
            both_do = jnp.concatenate([partner.do_head, self.do_head], axis=0)
            both_q = jnp.concatenate([partner.q_head, self.q_head], axis=0)
            for span in self.spans:
                at = pl.ds(span[0], span[1] - span[0])
                for total, name, right in (
                    (dv_sum, "rounded", both_do),
                    (dk_sum, "slopes", both_q),
                ):
                    left = [
                        unit.span_of(getattr(unit, name), span) for unit in (partner, self)
                    ]
                    part = matmul(jnp.concatenate(left, axis=1), right)
                    total[at, :] = part if self.first else total[at, :] + part
                    yield

    blocks = [
        (
            row_start,
            QUERY_TILE,
            pl.ds(prompt_total + row_start, QUERY_TILE),
            prompt_total + row_start + QUERY_TILE,
            None,
        )
        for row_start in reversed(range(0, length, QUERY_TILE))
    ]
    own_at = pl.ds(pl.multiple_of(ctx_place * prompt_rows, prompt_rows), prompt_rows)
    blocks.append((length, prompt_rows, own_at, prompt_total, first_member))
    units = []
    for index, (row_start, rows, position_at, last_key, weight) in enumerate(blocks):
        for head in range(2):
            first = index == 0
            units.append(Unit(row_start, rows, position_at, last_key, first, weight, head))

    def close(index):
        if index % 2 == 0:
            return
        pair = units[index - 1 : index + 1]
        at, position_at = pair[0].at, pair[0].position_at
        o_ref[at, :] = jnp.concatenate([unit.out_t for unit in pair], axis=0).T.astype(o_ref.dtype)
        d_queries = jnp.concatenate([unit.dq_t for unit in pair], axis=0).T * score_scale
        turn = [table[position_at, :] for table in (cos_ref, low_ref, high_ref)]
        dq_ref[at, :] = pair_turn_back(d_queries, *turn).astype(dq_ref.dtype)

    for _ in units[0].enter():
        pass
    def leaving(index):
        unit = units[index]
        partner = units[index - 1] if unit.head == 1 else None
        return unit.leave(partner), (4 if partner else 2) * len(unit.spans)

    for index, unit in enumerate(units):
        side, side_count = [], 0
        if index > 0:
            generator, count = leaving(index - 1)
            side.append(generator)
            side_count += count
        if index + 1 < len(units):
            side.append(units[index + 1].enter())
            side_count += 2 * len(units[index + 1].spans)
        together(unit.soften(), 4 * len(unit.tiles), chain(*side), side_count)
        if index > 0:
            close(index - 1)
    for _ in leaving(len(units) - 1)[0]:
        pass
    close(len(units) - 1)

    prompt_at = pl.ds(0, prompt_total)
    kvp_ref[0] = dk_sum[prompt_at, :].astype(kvp_ref.dtype)
    kvp_ref[1] = dv_sum[prompt_at, :].astype(kvp_ref.dtype)
    own_at = pl.ds(prompt_total, length)
    turned_back = pair_turn_back(
        dk_sum[own_at, :], cos_ref[own_at, :], low_ref[own_at, :], high_ref[own_at, :]
    )
    dk_ref[...] = turned_back.astype(dk_ref.dtype)
    dv_ref[...] = dv_sum[own_at, :].astype(dv_ref.dtype)

    own_rows = pl.ds(0, length)
    col = step * 2 * HD

    def lanes(start):
        return pl.ds(pl.multiple_of(start + col, 2 * HD), 2 * HD)

    out_pair = o_ref[own_rows, :]
    mid_sum[...] += matmul_bt(out_pair, picked[:, lanes(4 * D)])
    grads_ref[:, lanes(4 * D)] = matmul_at(d_mid_out[own_rows, :], out_pair).astype(low)
    for start, pair in ((D, dq_ref[own_rows, :]), (2 * D, dk_ref[...]), (3 * D, dv_ref[...])):
        d_mid_sum[...] += matmul_bt(pair, picked[:, lanes(start)])
        grads_ref[:, lanes(start)] = matmul_at(mid_qkv[...], pair).astype(low)

    @pl.when(step == last_step)
    def _():
        rest = pl.ds(length, prompt_rows)
        mid_out_ref[rest, :] = jnp.zeros((prompt_rows, R), low)
        d_mid_ref[rest, :] = jnp.zeros((prompt_rows, R), low)
        mid_out_ref[own_rows, :] = mid_sum[...].astype(low)
        d_mid_ref[own_rows, :] = d_mid_sum[...].astype(low)
        for load in loads:
            load.wait()
        grads_ref[:, :D] = matmul_at(d_mid_ref[own_rows, :], a1[...]).astype(low)
        grads_ref[:, 5 * D :] = matmul_at(mid_out_ref[own_rows, :], g[...]).astype(low)

    @pl.when(step == last_step)
    def _():
        for _, action in sorted(late, key=lambda item: item[0]):
            action()
        for array in arrays:
            if not array.resident:
                array.own().wait()
            array.finish()
        for level in range(-1, levels):
            for copy in stores(level):
                copy.wait()
        mine, owned = ids_ref[0], ad_slots.shape[1]
        chosen_ref[...] = ad_slots[mine // owned, mine % owned]


def turn_tables(count):
    half_rot = ROT // 2
    place = np.arange(half_rot, dtype=np.float32)
    frequency = np.float32(10000.0) ** (np.float32(-2.0) * place / np.float32(ROT))
    angles = np.arange(count, dtype=np.float32)[:, None] * frequency[None, :]
    cosine, sine_part = np.cos(angles), np.sin(angles)
    rest = np.zeros((count, HD - ROT), np.float32)
    gap = np.zeros((count, half_rot), np.float32)

    def pair(parts):
        return np.concatenate(parts + parts, axis=1).astype(np.float32)

    return (
        pair([cosine, cosine, rest + 1.0]),
        pair([-sine_part, gap, rest]),
        pair([gap, sine_part, rest]),
    )


def attention(
    ids,
    qkv,
    d_attended,
    w_up,
    w_down,
    low_sets,
    picked,
    mid_qkv,
    d_mid_out,
    attn_in,
    grad_rows,
    length,
):
    slots = lax.axis_size("fsdp")
    row_count = d_attended.shape[0]
    prompt_rows = row_count - length
    key_count = qkv.shape[0]
    prompt_total = key_count - length
    wide = 2 * HD
    low = jnp.bfloat16
    resident = key_count <= 2048

    def column(rows, start=0):
        return pl.BlockSpec((rows, wide), lambda pair: (0, start // wide + pair))

    def fixed(shape):
        return pl.BlockSpec(shape, lambda pair: (0, 0))

    down_shape = (slots,) + w_down.shape
    table = pl.BlockSpec((key_count, wide), lambda pair: (0, 0))
    anywhere = pl.BlockSpec(memory_space=pl.ANY)
    area = row_count * key_count * 0.75
    return pl.pallas_call(
        functools.partial(attention_kernel, length, prompt_total, prompt_rows),
        grid=(H // 2,),
        in_specs=[
            pl.BlockSpec(memory_space=pltpu.SMEM),
            column(key_count),
            column(key_count, D),
            column(key_count, 2 * D),
            column(row_count),
            table,
            table,
            table,
            anywhere,
            anywhere,
            anywhere,
            fixed(picked.shape),
            fixed(mid_qkv.shape),
            fixed(d_mid_out.shape),
            anywhere,
            anywhere,
        ],
        out_specs=[
            column(row_count),
            column(row_count),
            column(length),
            column(length),
            pl.BlockSpec((2, prompt_total, wide), lambda pair: (0, 0, pair)),
            anywhere,
            anywhere,
            fixed((R, WTOT - 6 * D)),
            fixed(picked.shape),
            fixed((row_count, R)),
            fixed((row_count, R)),
        ],
        out_shape=[
            jax.ShapeDtypeStruct((row_count, D), low),
            jax.ShapeDtypeStruct((row_count, D), low),
            jax.ShapeDtypeStruct((length, D), low),
            jax.ShapeDtypeStruct((length, D), low),
            jax.ShapeDtypeStruct((2, prompt_total, D), low),
            jax.ShapeDtypeStruct((slots,) + w_up.shape, low),
            jax.ShapeDtypeStruct(down_shape, low),
            jax.ShapeDtypeStruct((R, WTOT - 6 * D), low),
            jax.ShapeDtypeStruct(picked.shape, low),
            jax.ShapeDtypeStruct((row_count, R), low),
            jax.ShapeDtypeStruct((row_count, R), low),
        ],
        scratch_shapes=[
            pltpu.VMEM((slots,) + low_sets.shape[:2] + (WTOT - 6 * D,), low),
            pltpu.VMEM((slots,) + w_up.shape if resident else (16, 128), low),
            pltpu.VMEM(down_shape if resident else (16, 128), low),
            pltpu.VMEM((key_count, wide), low),
            pltpu.VMEM((key_count, wide), low),
            pltpu.VMEM((key_count, wide), low),
            pltpu.VMEM((row_count, wide), low),
            pltpu.VMEM((wide, key_count), low),
            pltpu.VMEM((wide, key_count), low),
            pltpu.VMEM((key_count, wide), jnp.float32),
            pltpu.VMEM((key_count, wide), jnp.float32),
            pltpu.VMEM((length, D), low),
            pltpu.VMEM((length, D), low),
            pltpu.VMEM((length, R), jnp.float32),
            pltpu.VMEM((length, R), jnp.float32),
        ]
        + relay_sems(3, slots)
        + [pltpu.SemaphoreType.DMA((2, slots)), pltpu.SemaphoreType.DMA((2,))],
        compiler_params=pltpu.CompilerParams(
            collective_id=2, has_side_effects=True, vmem_limit_bytes=VMEM_BYTES
        ),
        cost_estimate=pl.CostEstimate(
            flops=int(12 * area * D), bytes_accessed=32 * 1024 * 1024, transcendentals=int(area * H)
        ),
    )(
        ids,
        qkv,
        qkv,
        qkv,
        d_attended,
        *turn_tables(key_count),
        w_up,
        w_down,
        low_sets,
        picked,
        mid_qkv,
        d_mid_out,
        attn_in,
        grad_rows,
    )


def mlp_kernel(
    length,
    a_ref,
    g_ref,
    up_ref,
    down_ref,
    a_up_ref,
    b_up_ref,
    a_down_ref,
    b_down_ref,
    bias_ref,
    kvp_ref,
    ids_ref,
    cos_ref,
    low_ref,
    high_ref,
    out_ref,
    d_in_ref,
    grads_ref,
    share_ref,
    ids_out,
    mid_up,
    d_mid_down,
    mid_down_sum,
    d_mid_up_sum,
    first,
    first_sum,
    second,
    third,
    id_tiles,
    a,
    g,
    w_up,
    w_down,
    own_sem,
    load_sems,
    *sems,
):
    step = pl.program_id(0)
    last_step = pl.num_programs(0) - 1
    members, prompt_total, part = first.shape
    places, prompt_rows, _ = second.shape
    ctx, me = lax.axis_index("ctx"), lax.axis_index("fsdp")
    halves = members // 2

    def prompt_part(place):
        columns = pl.ds(pl.multiple_of((place % halves) * part, part), part)
        return kvp_ref.at[place // halves, :, columns]

    def owned_rows(place):
        return first_sum.at[pl.ds(pl.multiple_of(place * prompt_rows, prompt_rows), prompt_rows)]

    over_members = Trade("fsdp", members, prompt_part, first, sems[0:2])
    over_places = Trade("ctx", places, owned_rows, second, sems[2:4])
    to_members = Trade("fsdp", members, lambda place: third.at[me], third, sems[4:6])
    id_trade = Trade("ctx", places, lambda place: id_tiles.at[ctx], id_tiles, sems[6:8])
    own_part = pltpu.make_async_copy(prompt_part(me), first.at[me], own_sem)
    loads = [
        pltpu.make_async_copy(a_ref, a, load_sems.at[0]),
        pltpu.make_async_copy(g_ref, g, load_sems.at[1]),
    ]

    @pl.when(step == 0)
    def _():
        for load in loads:
            load.start()
        own_part.start()
        id_tiles[ctx] = jnp.full(id_tiles.shape[1:], ids_ref[0].astype(jnp.float32))
        greet_all(
            [(ctx, ring(me, members, offset)) for offset in range(1, members)]
            + [(ring(ctx, places, offset), me) for offset in range(1, places)]
        )
        over_members.start()
        id_trade.start()

    @pl.when(step == last_step // 2 + 1)
    def _():
        own_part.wait()
        over_members.wait()
        total = first[0].astype(jnp.float32)
        for member in range(1, members):
            total += first[member].astype(jnp.float32)
        first_sum[...] = total.astype(jnp.bfloat16)
        over_places.start()

    @pl.when(step == last_step - 1)
    def _():
        over_places.wait()
        second[ctx] = owned_rows(ctx)[...]
        total = second[0].astype(jnp.float32)
        for place in range(1, places):
            total += second[place].astype(jnp.float32)
        is_key = me < halves
        own_at = pl.ds(pl.multiple_of(ctx * prompt_rows, prompt_rows), prompt_rows)
        cosine = jnp.where(is_key, cos_ref[own_at, :], 1.0)
        low_sine = jnp.where(is_key, low_ref[own_at, :], 0.0)
        high_sine = jnp.where(is_key, high_ref[own_at, :], 0.0)
        for lane in range(0, part, 2 * HD):
            third[me, :, lane : lane + 2 * HD] = pair_turn_back(
                total[:, lane : lane + 2 * HD], cosine, low_sine, high_sine
            ).astype(jnp.bfloat16)
        to_members.start()

    rows = a.shape[0]
    slots, wide, share = down_ref.shape
    low = jnp.bfloat16
    chunk = min(256, wide)
    parts = range(0, wide, chunk)
    tiles = [pl.ds(start, min(MLP_ROWS, rows - start)) for start in range(0, rows, MLP_ROWS)]

    def masked(values):
        row = lax.broadcasted_iota(jnp.int32, values.shape, 0)
        return jnp.where(row < length, values, 0.0).astype(low)

    @pl.when(step == 0)
    def _():
        for load in loads:
            load.wait()
        mid_up[...] = masked(matmul_bt(a[...], a_up_ref[...]))
        d_mid_down[...] = masked(matmul_bt(g[...], b_down_ref[...]))
        mid_down_sum[...] = jnp.zeros_like(mid_down_sum)
        d_mid_up_sum[...] = jnp.zeros_like(d_mid_up_sum)
        out_ref[...] = jnp.zeros_like(out_ref)
        d_in_ref[...] = jnp.zeros_like(d_in_ref)

    w_up[...] = up_ref[0].astype(jnp.float32).astype(low)
    for slot in range(slots):
        piece = down_ref[slot].astype(jnp.float32).astype(low)
        w_down[:, slot * share : (slot + 1) * share] = piece
    b_up, a_down = b_up_ref[...], a_down_ref[...]
    bias = bias_ref[...]

    class Unit:
        def __init__(self, at):
            self.at = at
            self.up, self.d_hidden, self.hidden, self.d_up = [], [], [], []

        def enter(self):
            for start in parts:
                lanes = slice(start, start + chunk)
                up = matmul(a[self.at, :], w_up[:, lanes])
                self.up.append(up + matmul(mid_up[self.at, :], b_up[:, lanes]) + bias[:, lanes])
                yield
                d_hidden = matmul_bt(g[self.at, :], w_down[lanes, :])
                self.d_hidden.append(d_hidden + matmul(d_mid_down[self.at, :], a_down[:, lanes]))
                yield

        def bend(self):
            for up, d_hidden in zip(self.up, self.d_hidden):
                height = up.shape[0]
                edges = [0, height // 32 * 16 + height % 32, height]
                hidden, d_up = [], []
                for lane in range(0, chunk, 128):
                    hidden_rows, d_rows = [], []
                    for low_edge, high_edge in zip(edges[:-1], edges[1:]):
                        u = up[low_edge:high_edge, lane : lane + 128]
                        cdf = 0.5 + 0.5 * lax.erf(u * (0.5**0.5))
                        density = jnp.exp(-0.5 * (u * u)) * ((2.0 * math.pi) ** -0.5)
                        hidden_rows.append((u * cdf).astype(low))
                        d_piece = d_hidden[low_edge:high_edge, lane : lane + 128]
                        d_rows.append((d_piece * (cdf + u * density)).astype(low))
                        yield
                    hidden.append(jnp.concatenate(hidden_rows, axis=0))
                    d_up.append(jnp.concatenate(d_rows, axis=0))
                self.hidden.append(jnp.concatenate(hidden, axis=1))
                self.d_up.append(jnp.concatenate(d_up, axis=1))

        def leave(self):
            at = self.at
            for column in range(0, D, 256):
                lanes = slice(column, column + 256)
                total = out_ref[at, lanes]
                for start, hidden in zip(parts, self.hidden):
                    total += matmul(hidden, w_down[start : start + chunk, lanes])
                out_ref[at, lanes] = total
                yield
                total = d_in_ref[at, lanes]
                for start, d_up in zip(parts, self.d_up):
                    total += matmul_bt(d_up, w_up[lanes, start : start + chunk])
                d_in_ref[at, lanes] = total
                yield
            self.grads = []
            middle, d_middle = mid_down_sum[at, :], d_mid_up_sum[at, :]
            for start, hidden, d_up in zip(parts, self.hidden, self.d_up):
                middle += matmul_bt(hidden, a_down[:, start : start + chunk])
                d_middle += matmul_bt(d_up, b_up[:, start : start + chunk])
                self.grads.append(
                    (matmul_at(mid_up[at, :], d_up), matmul_at(d_mid_down[at, :], hidden))
                )
                yield
            mid_down_sum[at, :] = middle
            d_mid_up_sum[at, :] = d_middle

    units = [Unit(at) for at in tiles]
    enters, leaves, bends = 2 * len(parts), 8 + len(parts), 2 * len(parts) * (chunk // 128)
    for _ in units[0].enter():
        pass
    for index, unit in enumerate(units):
        side, side_count = [], 0
        if index > 0:
            side.append(units[index - 1].leave())
            side_count += leaves
        if index + 1 < len(units):
            side.append(units[index + 1].enter())
            side_count += enters
        together(unit.bend(), bends, chain(*side), side_count)
    for _ in units[-1].leave():
        pass
    grad_b_up = jnp.concatenate(
        [sum(unit.grads[index][0] for unit in units) for index in range(len(parts))], axis=1
    )
    grad_a_down = jnp.concatenate(
        [sum(unit.grads[index][1] for unit in units) for index in range(len(parts))], axis=1
    )
    for start, value in ((D, grad_b_up), (D + FF, grad_a_down)):
        columns = pl.ds(pl.multiple_of(start + step * wide, wide), wide)
        grads_ref[:, columns] = value.astype(jnp.bfloat16)

    @pl.when(step == last_step)
    def _():
        mid_down = masked(mid_down_sum[...])
        d_mid_up = masked(d_mid_up_sum[...])
        out_ref[...] += matmul(mid_down, b_down_ref[...])
        d_in_ref[...] += matmul(d_mid_up, a_up_ref[...])
        grads_ref[:, :D] = matmul_at(d_mid_up, a[...]).astype(jnp.bfloat16)
        grads_ref[:, D + 2 * FF :] = matmul_at(mid_down, g[...]).astype(jnp.bfloat16)
        to_members.wait()
        id_trade.wait()
        share_ref[...] = third[...]
        ids_out[...] = id_tiles[...]
        for trade in (over_members, over_places, to_members, id_trade):
            trade.finish()


def mlp(mlp_in, grad_rows, up_slots, down_slots, chosen, frozen_bias, kvp, ids, length):
    rows = mlp_in.shape[0]
    prompt_total, prompt_rows = kvp.shape[1], rows - length
    places = lax.axis_size("ctx")
    slots, _, up_share = up_slots.shape
    down_share = down_slots.shape[2]
    wide = math.gcd(up_share, 512)
    per = up_share // wide

    def whole(shape):
        return pl.BlockSpec(shape, lambda step: (0,) * len(shape))

    def columns(start, width):
        return pl.BlockSpec((R, width), lambda step: (0, start // width))

    def moving(height, start):
        return pl.BlockSpec((height, wide), lambda step: (0, start // wide + step))

    return pl.pallas_call(
        functools.partial(mlp_kernel, length),
        grid=(FF // wide,),
        in_specs=[
            pl.BlockSpec(memory_space=pl.ANY),
            pl.BlockSpec(memory_space=pl.ANY),
            pl.BlockSpec((1, D, wide), lambda step: (step // per, 0, step % per)),
            pl.BlockSpec((slots, wide, down_share), lambda step: (0, step, 0)),
            columns(0, D),
            moving(R, D),
            moving(R, D + FF),
            columns(D + 2 * FF, D),
            moving(1, 4 * D),
            pl.BlockSpec(memory_space=pl.ANY),
            pl.BlockSpec(memory_space=pltpu.SMEM),
        ]
        + [whole((prompt_total, 2 * HD))] * 3,
        out_specs=[
            whole((rows, D)),
            whole((rows, D)),
            whole((R, 2 * D + 2 * FF)),
            whole((slots, prompt_rows, 2 * D // slots)),
            whole((places, 8, 2 * HD)),
        ],
        out_shape=[
            jax.ShapeDtypeStruct((rows, D), jnp.float32),
            jax.ShapeDtypeStruct((rows, D), jnp.float32),
            jax.ShapeDtypeStruct((R, 2 * D + 2 * FF), jnp.bfloat16),
            jax.ShapeDtypeStruct((slots, prompt_rows, 2 * D // slots), jnp.bfloat16),
            jax.ShapeDtypeStruct((places, 8, 2 * HD), jnp.float32),
        ],
        scratch_shapes=[
            pltpu.VMEM((rows, R), jnp.bfloat16),
            pltpu.VMEM((rows, R), jnp.bfloat16),
            pltpu.VMEM((rows, R), jnp.float32),
            pltpu.VMEM((rows, R), jnp.float32),
            pltpu.VMEM((slots, prompt_total, 2 * D // slots), jnp.bfloat16),
            pltpu.VMEM((prompt_total, 2 * D // slots), jnp.bfloat16),
            pltpu.VMEM((places, prompt_rows, 2 * D // slots), jnp.bfloat16),
            pltpu.VMEM((slots, prompt_rows, 2 * D // slots), jnp.bfloat16),
            pltpu.VMEM((places, 8, 2 * HD), jnp.float32),
            pltpu.VMEM((rows, D), jnp.bfloat16),
            pltpu.VMEM((rows, D), jnp.bfloat16),
            pltpu.VMEM((D, wide), jnp.bfloat16),
            pltpu.VMEM((wide, D), jnp.bfloat16),
            pltpu.SemaphoreType.DMA,
            pltpu.SemaphoreType.DMA((2,)),
        ]
        + trade_sems(slots)
        + trade_sems(places)
        + trade_sems(slots)
        + trade_sems(places),
        compiler_params=pltpu.CompilerParams(
            collective_id=3, has_side_effects=True, vmem_limit_bytes=VMEM_BYTES
        ),
        cost_estimate=pl.CostEstimate(
            flops=8 * rows * D * FF,
            bytes_accessed=30 * 1024 * 1024,
            transcendentals=2 * rows * FF,
        ),
    )(
        mlp_in,
        grad_rows,
        up_slots,
        down_slots,
        chosen,
        chosen,
        chosen,
        chosen,
        frozen_bias[None],
        kvp,
        ids,
        *turn_tables(prompt_total),
    )


def tail_kernel(
    length,
    x_ref,
    xp_ref,
    g_ref,
    ob_ref,
    dq_ref,
    dk_ref,
    dv_ref,
    share_ref,
    mlp_ref,
    d_mlp_ref,
    wq_ref,
    wo_ref,
    picked,
    mid_out,
    d_mid_qkv,
    front_ref,
    back_ref,
    ids_ref,
    bias_ref,
    gain_ref,
    cont_out,
    prompt_out,
    cont_grad,
    prompt_grad,
    sums_ref,
    norm_ref,
    x,
    g,
    ob,
    dqkv,
    result,
    d_rows,
    wq,
    wo,
    grads,
    first,
    bins,
    second,
    full,
    norm_members,
    norm_places,
    load_sems,
    store_sems,
    *sems,
):
    rows = x.shape[0]
    prompt_rows = rows - length
    places, members, owned = full.shape[0], second.shape[0], full.shape[1]
    width = first.shape[2]
    part = 2 * D // members
    slots, _, share = wq.shape
    out_share = wo.shape[2]
    ctx, me = lax.axis_index("ctx"), lax.axis_index("fsdp")
    parity, line, lines = ctx % 2, ctx // 2, places // 2
    sibling = ctx + 1 - 2 * parity
    own_rows, prompt_at = pl.ds(0, length), pl.ds(length, prompt_rows)

    pairs = [
        (front_ref, grads.at[:, pl.ds(0, 6 * D)]),
        (back_ref, grads.at[:, pl.ds(6 * D, WTOT - 6 * D)]),
        (ob_ref, ob),
        (wo_ref, wo),
        (x_ref, x.at[own_rows]),
        (xp_ref, x.at[prompt_at]),
        (mlp_ref, result),
        (dq_ref, dqkv.at[:, pl.ds(0, D)]),
        (dk_ref, dqkv.at[own_rows, pl.ds(D, D)]),
        (dv_ref, dqkv.at[own_rows, pl.ds(2 * D, D)]),
        (g_ref, g),
        (wq_ref, wq),
        (d_mlp_ref, d_rows),
    ] + [
        (share_ref.at[slot], dqkv.at[prompt_at, pl.ds(D + slot * part, part)])
        for slot in range(members)
    ]
    loads = [
        pltpu.make_async_copy(source, target, load_sems.at[index])
        for index, (source, target) in enumerate(pairs)
    ]
    for load in loads:
        load.start()

    def grad_part(place):
        return grads.at[:, pl.ds(pl.multiple_of(place * width, width), width)]

    def line_place(offset, side):
        return ((line + offset) % lines) * 2 + side

    over_places = Trade("ctx", places, grad_part, first, sems[0:2])
    over_members = Trade(
        "fsdp", members, lambda place: bins.at[pl.ds(place * owned, owned)], second, sems[2:4]
    )
    norm_a = Trade("fsdp", members, lambda place: norm_members.at[me], norm_members, sems[4:6])
    norm_b = Trade("ctx", places, lambda place: norm_places.at[ctx], norm_places, sems[6:8])
    line_sems, gift_sems = sems[8:10], sems[10:12]

    def line_send(offset):
        part_ref = full.at[ctx]
        return remote_copy(
            part_ref, part_ref, line_sems, offset, (line_place(offset, parity), me)
        )

    def line_landed(offset):
        part_ref = full.at[line_place(lines - offset, parity)]
        return remote_copy(
            part_ref, part_ref, line_sems, offset, (line_place(offset, parity), me)
        )

    def gift(offset, taken=False):
        side = 1 - parity if taken else parity
        part_ref = full.at[line_place(lines - offset, side)]
        return remote_copy(part_ref, part_ref, gift_sems, offset, (sibling, me))

    greet_all(
        [(ctx, ring(me, members, offset)) for offset in range(1, members)]
        + [(ring(ctx, places, offset), me) for offset in range(1, places)]
    )

    for load in loads[:2]:
        load.wait()
    over_places.start()

    for load in loads[2:7]:
        load.wait()
    low = jnp.bfloat16
    tiles = [(start, min(OUT_TILE, rows - start)) for start in range(0, rows, OUT_TILE)]
    def out_rows(start, size):
        at = pl.ds(start, size)
        adapted = matmul(mid_out[at, :], picked[:, 5 * D : 6 * D])
        for slot in range(slots):
            lanes = slice(slot * out_share, (slot + 1) * out_share)
            first_bias = bias_ref[:, 3 * D + slot * out_share : 3 * D + (slot + 1) * out_share]
            second_start = 4 * D + FF + slot * out_share
            second_bias = bias_ref[:, second_start : second_start + out_share]
            result[at, lanes] += (
                x[at, lanes].astype(jnp.float32)
                + matmul(ob[at, :], wo[slot])
                + adapted[:, lanes]
                + first_bias
                + second_bias
            )

    def back_rows(start, size):
        at = pl.ds(start, size)
        d_attn_in = matmul(d_mid_qkv[at, :], picked[:, :D])
        for slot in range(slots):
            d_attn_in += matmul_bt(dqkv[at, slot * share : (slot + 1) * share], wq[slot])
        for row in range(0, size, 16):
            row_at = pl.ds(start + row, 16)
            values = x[row_at, :].astype(jnp.float32)
            centered = values - jnp.mean(values, axis=-1, keepdims=True)
            variance = jnp.mean(centered * centered, axis=-1, keepdims=True)
            scale = lax.rsqrt(variance + 1e-05)
            unit = centered * scale
            d_unit = d_attn_in[row : row + 16] * gain_ref[0:1, :]
            d_unit += d_rows[row_at, :] * gain_ref[1:2, :]
            mean_d = jnp.mean(d_unit, axis=-1, keepdims=True)
            mean_du = jnp.mean(d_unit * unit, axis=-1, keepdims=True)
            d_rows[row_at, :] = g[row_at, :].astype(jnp.float32) + scale * (
                d_unit - mean_d - unit * mean_du
            )

    half = len(tiles) // 2
    for start, size in tiles[:half]:
        out_rows(start, size)

    over_places.wait()
    first[ctx] = grad_part(ctx)[...]
    for index in range(members * owned):
        total = None
        for place in range(places):
            matches = ids_ref[place, 0:1, 0:1] == float(index)
            piece = jnp.where(matches, first[place].astype(jnp.float32), 0.0)
            total = piece if total is None else total + piece
        bins[index] = total.astype(low)
    over_members.start()

    for start, size in tiles[half:]:
        out_rows(start, size)
    stores = [
        pltpu.make_async_copy(result.at[own_rows], cont_out, store_sems.at[0]),
        pltpu.make_async_copy(result.at[prompt_at], prompt_out, store_sems.at[1]),
    ]
    for store in stores:
        store.start()
    for load in loads[7:]:
        load.wait()

    over_members.wait()
    second[me] = bins[pl.ds(me * owned, owned)]
    total = second[0].astype(jnp.float32)
    for member in range(1, members):
        total += second[member].astype(jnp.float32)
    full[ctx] = total.astype(low)
    for offset in range(1, lines):
        line_send(offset).start()
    gift(0).start()
    norm_members[me] = jnp.full(norm_members.shape[1:], jnp.sum(total * total))
    norm_a.start()

    for start, size in tiles[:1]:
        back_rows(start, size)
    norm_a.wait()
    square = norm_members[0]
    for member in range(1, members):
        square = square + norm_members[member]
    norm_places[ctx] = square
    norm_b.start()
    for start, size in tiles[1 : half + 1]:
        back_rows(start, size)
    for offset in range(1, lines):
        line_landed(offset).wait_recv()
        gift(offset).start()
    for start, size in tiles[half + 1 :]:
        back_rows(start, size)
    stores += [
        pltpu.make_async_copy(d_rows.at[own_rows], cont_grad, store_sems.at[2]),
        pltpu.make_async_copy(d_rows.at[prompt_at], prompt_grad, store_sems.at[3]),
    ]
    for store in stores[2:]:
        store.start()
    norm_b.wait()
    square = norm_places[0]
    for place in range(1, places):
        square = square + norm_places[place]
    norm_ref[...] = jnp.sqrt(square)
    for offset in range(lines):
        gift(offset, taken=True).wait_recv()
    sums_ref[...] = full[...]
    for trade in (over_places, over_members, norm_a, norm_b):
        trade.finish()
    for offset in range(1, lines):
        line_send(offset).wait_send()
    for offset in range(lines):
        gift(offset).wait_send()
    for store in stores:
        store.wait()


def tail(
    x_cont,
    x_prompt,
    grad_rows,
    attended,
    dq_rows,
    dk_own,
    dv_own,
    prompt_share,
    mlp_out,
    d_mlp_in,
    qkv_slots,
    out_slots,
    picked,
    mid_out,
    d_mid_qkv,
    front_grads,
    back_grads,
    id_tiles,
    frozen_bias,
    norm_gain,
    owned,
):
    rows, length, prompt_rows = attended.shape[0], x_cont.shape[0], x_prompt.shape[0]
    places, members = lax.axis_size("ctx"), lax.axis_size("fsdp")
    width = WTOT // places
    low, wide = jnp.bfloat16, jnp.float32
    anywhere = pl.BlockSpec(memory_space=pl.ANY)
    on_chip = pl.BlockSpec(memory_space=pltpu.VMEM)
    return pl.pallas_call(
        functools.partial(tail_kernel, length),
        in_specs=[anywhere] * 12 + [on_chip] * 3 + [anywhere] * 2 + [on_chip] * 3,
        out_specs=[anywhere] * 4 + [on_chip] * 2,
        out_shape=[
            jax.ShapeDtypeStruct((length, D), wide),
            jax.ShapeDtypeStruct((prompt_rows, D), wide),
            jax.ShapeDtypeStruct((length, D), wide),
            jax.ShapeDtypeStruct((prompt_rows, D), wide),
            jax.ShapeDtypeStruct((places, owned, R, width), low),
            jax.ShapeDtypeStruct((8, 2 * HD), wide),
        ],
        scratch_shapes=[
            pltpu.VMEM((rows, D), low),
            pltpu.VMEM((rows, D), low),
            pltpu.VMEM((rows, D), low),
            pltpu.VMEM((rows, 3 * D), low),
            pltpu.VMEM((rows, D), wide),
            pltpu.VMEM((rows, D), wide),
            pltpu.VMEM(qkv_slots.shape, low),
            pltpu.VMEM(out_slots.shape, low),
            pltpu.VMEM((R, WTOT), low),
            pltpu.VMEM((places, R, width), low),
            pltpu.VMEM((members * owned, R, width), low),
            pltpu.VMEM((members, owned, R, width), low),
            pltpu.VMEM((places, owned, R, width), low),
            pltpu.VMEM((members, 8, 2 * HD), wide),
            pltpu.VMEM((places, 8, 2 * HD), wide),
            pltpu.SemaphoreType.DMA((13 + members,)),
            pltpu.SemaphoreType.DMA((4,)),
        ]
        + trade_sems(places)
        + trade_sems(members)
        + trade_sems(members)
        + trade_sems(places)
        + [pltpu.SemaphoreType.DMA((places // 2,)) for _ in range(4)],
        compiler_params=pltpu.CompilerParams(
            collective_id=4, has_side_effects=True, vmem_limit_bytes=VMEM_BYTES
        ),
        cost_estimate=pl.CostEstimate(
            flops=2 * rows * D * 4 * D, bytes_accessed=50 * 1024 * 1024, transcendentals=rows
        ),
    )(
        x_cont,
        x_prompt,
        grad_rows,
        attended,
        dq_rows,
        dk_own,
        dv_own,
        prompt_share,
        mlp_out,
        d_mlp_in,
        qkv_slots,
        out_slots,
        picked,
        mid_out,
        d_mid_qkv,
        front_grads,
        back_grads,
        id_tiles,
        frozen_bias[None],
        norm_gain,
    )


def update_kernel(
    sums_ref,
    norm_ref,
    sets_ref,
    first_ref,
    second_ref,
    rate_ref,
    cont_out_ref,
    cont_grad_ref,
    prompt_out_ref,
    prompt_grad_ref,
    new_sets,
    new_first,
    new_second,
    low_sets,
    cont_out,
    cont_grad,
    prompt_out,
    prompt_grad,
    norm_out,
):
    cont_out[...] = cont_out_ref[...]
    cont_grad[...] = cont_grad_ref[...]
    prompt_out[...] = prompt_out_ref[...]
    prompt_grad[...] = prompt_grad_ref[...]
    norm_out[0] = norm_ref[0, 0]
    limit = 0.1 * math.sqrt(SETS * R * WTOT)
    norm = norm_ref[0:1, 0:1]
    ratio = limit / jnp.maximum(norm, limit)
    rate = rate_ref[...]
    for index in range(sets_ref.shape[0]):
        clipped = sums_ref[0, index].astype(jnp.float32) * ratio
        first = beta_one * first_ref[index] + (1.0 - beta_one) * clipped
        second = beta_two * second_ref[index] + (1.0 - beta_two) * clipped * clipped
        corrected_first = first / (1.0 - beta_one**STEP)
        corrected_second = second / (1.0 - beta_two**STEP)
        old = sets_ref[index]
        new = old - rate * (
            corrected_first / (jnp.sqrt(corrected_second) + adam_eps) + weight_decay * old
        )
        new_first[index] = first
        new_second[index] = second
        new_sets[index] = new
        low_sets[index] = new.astype(jnp.bfloat16)


def update(sums, norm, adapters, first_moment, second_moment, rows_out):
    places, owned, _, width = sums.shape
    rates = np.where(up_columns(), rate_up, rate_down).astype(np.float32)[None]
    length, prompt_rows = rows_out[0].shape[0], rows_out[2].shape[0]

    def columns():
        return pl.BlockSpec((owned, R, width), lambda place: (0, 0, place))

    def shaped(kind):
        return jax.ShapeDtypeStruct(adapters.shape, kind)

    moving = [pl.BlockSpec((length // places, D), lambda place: (place, 0))] * 2
    moving += [pl.BlockSpec((prompt_rows, D), lambda place: (0, 0))] * 2
    return pl.pallas_call(
        update_kernel,
        grid=(places,),
        in_specs=[
            pl.BlockSpec((1, owned, R, width), lambda place: (place, 0, 0, 0)),
            pl.BlockSpec((8, 2 * HD), lambda place: (0, 0)),
            columns(),
            columns(),
            columns(),
            pl.BlockSpec((1, width), lambda place: (0, place)),
        ]
        + moving,
        out_specs=[columns()] * 4 + moving + [pl.BlockSpec(memory_space=pltpu.SMEM)],
        out_shape=[shaped(jnp.float32)] * 3
        + [shaped(jnp.bfloat16)]
        + [jax.ShapeDtypeStruct(row.shape, jnp.float32) for row in rows_out]
        + [jax.ShapeDtypeStruct((1,), jnp.float32)],
        compiler_params=pltpu.CompilerParams(vmem_limit_bytes=VMEM_BYTES),
    )(sums, norm, adapters, first_moment, second_moment, rates, *rows_out)


def per_device(
    x_prompt,
    x_cont,
    dy_prompt,
    dy_cont,
    adapter_ids,
    w_qkv,
    w_out,
    w_up,
    w_down,
    frozen_bias,
    norm_gain,
    norm_shift,
    adapters,
    first_moment,
    second_moment,
):
    length = x_cont.shape[1]
    (
        qkv,
        attn_in,
        mlp_in,
        d_attended,
        grad_rows,
        qkv_slots,
        out_slots,
        low_sets,
        picked,
        mid_qkv,
        d_mid_out,
    ) = front(
        adapter_ids,
        x_cont[0],
        x_prompt,
        dy_cont[0],
        dy_prompt,
        w_qkv,
        w_out,
        adapters,
        frozen_bias[None],
        norm_gain,
        norm_shift,
    )
    (
        attended,
        dq_rows,
        dk_own,
        dv_own,
        kv_prompt,
        up_slots,
        down_slots,
        chosen,
        front_grads,
        mid_out,
        d_mid_qkv,
    ) = attention(
        adapter_ids,
        qkv,
        d_attended,
        w_up,
        w_down,
        low_sets,
        picked,
        mid_qkv,
        d_mid_out,
        attn_in,
        grad_rows,
        length,
    )
    mlp_out, d_mlp_in, back_grads, prompt_share, id_tiles = mlp(
        mlp_in,
        grad_rows,
        up_slots,
        down_slots,
        chosen,
        frozen_bias,
        kv_prompt,
        adapter_ids,
        length,
    )
    cont_out, prompt_out, cont_grad, prompt_grad, sums, norm = tail(
        x_cont[0],
        x_prompt,
        grad_rows,
        attended,
        dq_rows,
        dk_own,
        dv_own,
        prompt_share,
        mlp_out,
        d_mlp_in,
        qkv_slots,
        out_slots,
        picked,
        mid_out,
        d_mid_qkv,
        front_grads,
        back_grads,
        id_tiles,
        frozen_bias,
        norm_gain,
        adapters.shape[0],
    )
    new_sets, new_first, new_second, low_new, cont_out, cont_grad, prompt_out, prompt_grad, norm = (
        update(
            sums,
            norm,
            adapters,
            first_moment,
            second_moment,
            (cont_out, cont_grad, prompt_out, prompt_grad),
        )
    )
    return (
        prompt_out,
        prompt_grad,
        cont_out[None],
        cont_grad[None],
        norm.reshape(()),
        new_sets,
        new_first,
        new_second,
        low_new,
    )


def solution(mesh):
    in_specs = (
        P("ctx", None),
        P(("ctx", "fsdp"), None, None),
        P("ctx", None),
        P(("ctx", "fsdp"), None, None),
        P(("ctx", "fsdp")),
        P(None, "fsdp"),
        P(None, "fsdp"),
        P(None, "fsdp"),
        P(None, "fsdp"),
        P(),
        P(),
        P(),
        P("fsdp", None, None),
        P("fsdp", None, None),
        P("fsdp", None, None),
    )
    out_specs = (
        P("ctx", None),
        P("ctx", None),
        P(("ctx", "fsdp"), None, None),
        P(("ctx", "fsdp"), None, None),
        P(),
        P("fsdp", None, None),
        P("fsdp", None, None),
        P("fsdp", None, None),
        P("fsdp", None, None),
    )
    return jax.shard_map(
        per_device, mesh=mesh, in_specs=in_specs, out_specs=out_specs, check_vma=False
    )
```

```python
import functools
import math

import jax
import jax.numpy as jnp
import numpy as np
from jax import lax
from jax.experimental import pallas as pl
from jax.experimental.pallas import tpu as pltpu
from jax.sharding import PartitionSpec as P

D = 1024
H = 16
HD = 64
ROT = 16
FF = 4096
R = 16
SETS = 8
STEP = 10
WTOT = 16384


beta_one = 0.9
beta_two = 0.999
adam_eps = 1e-08
weight_decay = 0.01
rate_down = 0.05
rate_up = 0.5
masked_score = -1e30
KEY_TILE = 256
QUERY_TILE = 256
SPAN = 768
PIECE = 64
LINES = 32
MLP_ROWS = 272
ROW_TILE = 512
OUT_TILE = 272
VMEM_BYTES = 62 * 1024 * 1024


def matmul(left, right):
    return jnp.dot(left, right, preferred_element_type=jnp.float32)


def matmul_bt(left, right):
    return lax.dot_general(
        left, right, (((1,), (1,)), ((), ())), preferred_element_type=jnp.float32
    )


def matmul_at(left, right):
    return lax.dot_general(
        left, right, (((0,), (0,)), ((), ())), preferred_element_type=jnp.float32
    )


def up_columns():
    column = np.arange(WTOT)
    return (
        (column >= D) & (column < 4 * D)
        | (column >= 5 * D) & (column < 6 * D)
        | (column >= 7 * D) & (column < 7 * D + FF)
        | (column >= 7 * D + 2 * FF)
    )


def pair_turn(values, cosine, low_sine, high_sine):
    return (
        values * cosine
        + pltpu.roll(values, 2 * HD - ROT // 2, 1) * low_sine
        + pltpu.roll(values, ROT // 2, 1) * high_sine
    )


def pair_turn_back(values, cosine, low_sine, high_sine):
    return (
        values * cosine
        - pltpu.roll(values, 2 * HD - ROT // 2, 1) * low_sine
        - pltpu.roll(values, ROT // 2, 1) * high_sine
    )


MESH = pl.DeviceIdType.MESH


def flip(place, mask):
    bit = 1
    while bit <= mask:
        if mask & bit:
            place = place + bit - 2 * bit * ((place // bit) % 2)
        bit *= 2
    return place


class Relay:
    def __init__(self, count):
        bits = [1 << index for index in range(count.bit_length() - 1)]
        self.count = count
        self.orders = (bits, bits[1:] + bits[:1])
        self.masks = []
        for order in self.orders:
            masks = [0]
            for bit in order:
                masks += [mask ^ bit for mask in masks]
            self.masks.append(masks)
        self.levels = [
            [held for held in range(1, count) if bin(held).count("1") == level]
            for level in range(1, count.bit_length())
        ]
        self.ctx, self.me = lax.axis_index("ctx"), lax.axis_index("fsdp")
        self.parity = self.ctx % 2
        self.sibling = self.ctx + 1 - 2 * self.parity

    def blend(self, even, odd, other):
        side = 1 - self.parity if other else self.parity
        return even + side * (odd - even)

    def partner(self, turn, stage):
        even, odd = (flip(self.me, self.orders[order][stage]) for order in (turn, 1 - turn))
        return self.blend(even, odd, False)

    def slot(self, turn, held, other=False):
        even, odd = (flip(self.me, self.masks[order][held]) for order in (turn, 1 - turn))
        return self.blend(even, odd, other)

    def greet(self, others=()):
        barrier = pltpu.get_barrier_semaphore()
        peers = [(self.ctx, flip(self.me, bit)) for bit in self.orders[0]]
        peers += [(self.sibling, self.me)] + list(others)
        for peer in peers:
            pl.semaphore_signal(barrier, inc=1, device_id=peer, device_id_type=MESH)
        pl.semaphore_wait(barrier, len(peers))


class Gathered:
    def __init__(self, relay, shard, slots, cut, sems, resident=False):
        self.resident = resident
        self.relay, self.shard, self.slots, self.cut = relay, shard, slots, cut
        self.send_sems, self.recv_sems, self.give_sems, self.take_sems, self.own_sem = sems

    def part(self, slot, turn, parity):
        return self.cut(self.slots.at[slot], 2 * parity + turn)

    def own(self):
        return pltpu.make_async_copy(self.shard, self.slots.at[self.relay.me], self.own_sem)

    def remote(self, source, target, sems, turn, held, device):
        index = turn * (self.relay.count - 1) + held - 1
        return pltpu.make_async_remote_copy(
            src_ref=source,
            dst_ref=target,
            send_sem=sems[0].at[index],
            recv_sem=sems[1].at[index],
            device_id=device,
            device_id_type=MESH,
        )

    def message(self, turn, held):
        relay = self.relay
        stage = held.bit_length() - 1
        before = held - (1 << stage)
        target = self.part(relay.slot(turn, before), turn, relay.parity)
        outside = before == 0 and not self.resident
        source = self.cut(self.shard, 2 * relay.parity + turn) if outside else target
        device = (relay.ctx, relay.partner(turn, stage))
        return self.remote(source, target, (self.send_sems, self.recv_sems), turn, held, device)

    def arrival(self, turn, held):
        relay = self.relay
        part = self.part(relay.slot(turn, held), turn, relay.parity)
        device = (relay.ctx, relay.partner(turn, held.bit_length() - 1))
        return self.remote(part, part, (self.send_sems, self.recv_sems), turn, held, device)

    def gift(self, turn, held, taken=False):
        relay = self.relay
        side = 1 - relay.parity if taken else relay.parity
        part = self.part(relay.slot(turn, held, taken), turn, side)
        device = (relay.sibling, relay.me)
        return self.remote(part, part, (self.give_sems, self.take_sems), turn, held, device)

    def start(self):
        if self.resident:
            self.own().wait()
        for held in self.relay.levels[0]:
            for turn in range(2):
                self.message(turn, held).start()
        if not self.resident:
            self.own().start()

    def forward(self, level):
        for held in self.relay.levels[level]:
            for turn in range(2):
                self.arrival(turn, held).wait_recv()
                for stage in range(held.bit_length(), len(self.relay.orders[0])):
                    self.message(turn, (1 << stage) + held).start()

    def give(self, level):
        for held in self.relay.levels[level]:
            for turn in range(2):
                self.gift(turn, held).start()

    def advance(self, level):
        self.forward(level)
        self.give(level)

    def places(self, level):
        masks = [mask for mask in range(self.relay.count) if bin(mask).count("1") == level + 1]
        return [flip(self.relay.me, mask) for mask in masks]

    def take(self, level):
        for held in self.relay.levels[level]:
            for turn in range(2):
                self.gift(turn, held, taken=True).wait_recv()

    def finish(self):
        for held in range(1, self.relay.count):
            for turn in range(2):
                self.message(turn, held).wait_send()
                self.gift(turn, held).wait_send()


def relay_sems(arrays, count):
    return [pltpu.SemaphoreType.DMA((arrays, 2 * (count - 1))) for _ in range(4)] + [
        pltpu.SemaphoreType.DMA((arrays,))
    ]


def sems_of(sems, index):
    return [sem.at[index] for sem in sems]


def row_quarter(ref, index):
    size = ref.shape[0] // 4
    return ref.at[pl.ds(pl.multiple_of(index * size, size), size)]


def lane_quarter(ref, index):
    size = ref.shape[-1] // 4
    return ref.at[:, :, pl.ds(pl.multiple_of(index * size, size), size)]


def remote_copy(source, target, sems, index, device):
    return pltpu.make_async_remote_copy(
        src_ref=source,
        dst_ref=target,
        send_sem=sems[0].at[index],
        recv_sem=sems[1].at[index],
        device_id=device,
        device_id_type=MESH,
    )


def greet_all(peers):
    barrier = pltpu.get_barrier_semaphore()
    for peer in peers:
        pl.semaphore_signal(barrier, inc=1, device_id=peer, device_id_type=MESH)
    pl.semaphore_wait(barrier, len(peers))


class Trade:
    def __init__(self, axis, count, source, slots, sems):
        self.axis, self.count, self.source, self.slots = axis, count, source, slots
        self.places = {name: lax.axis_index(name) for name in ("ctx", "fsdp")}
        self.me = self.places[axis]
        self.sems = sems

    def device(self, place):
        return tuple(place if name == self.axis else self.places[name] for name in self.places)

    def send(self, offset):
        place = flip(self.me, offset)
        return remote_copy(
            self.source(place), self.slots.at[self.me], self.sems, offset - 1, self.device(place)
        )

    def start(self):
        for offset in reversed(range(1, self.count)):
            self.send(offset).start()

    def wait(self):
        for offset in reversed(range(1, self.count)):
            place = flip(self.me, offset)
            part = self.slots.at[place]
            remote_copy(part, part, self.sems, offset - 1, self.device(place)).wait_recv()

    def finish(self):
        for offset in range(1, self.count):
            self.send(offset).wait_send()


def trade_sems(count):
    return [pltpu.SemaphoreType.DMA((count - 1,)) for _ in range(2)]


def together(main, main_count, side, side_count):
    done = 0
    for index in range(main_count):
        next(main, None)
        while done < (index + 1) * side_count // main_count:
            next(side, None)
            done += 1
    for generator in (main, side):
        for _ in generator:
            pass


def chain(*generators):
    for generator in generators:
        yield from generator


def front_kernel(
    length,
    ids_ref,
    x_ref,
    xp_ref,
    dy_ref,
    dyp_ref,
    wq_ref,
    wo_ref,
    sets_ref,
    bias_ref,
    gain_ref,
    shift_ref,
    cos_ref,
    low_ref,
    high_ref,
    qkv_out,
    a1_out,
    a2_out,
    dob_out,
    g_out,
    wq_out,
    wo_out,
    low_out,
    picked,
    mid_ref,
    d_mid_ref,
    wq,
    wo,
    ad,
    sets,
    low_sets,
    xp,
    a1,
    a2,
    g,
    qkv,
    dob,
    mid_keys,
    *sems,
):
    wq_sems, wo_sems, ad_sems = (sems_of(sems[:5], index) for index in range(3))
    xp_send, xp_recv, xp_give, xp_take, load_sems, store_sems, column_sems = sems[5:]
    slots, _, share = wq.shape
    chunk = math.gcd(share, 256)
    per = share // chunk
    owned = ad.shape[1]
    prompt_rows = xp_ref.shape[0]
    prompt_total = xp.shape[0]
    keys = a1.shape[0]
    rows = g.shape[0]
    relay = Relay(slots)
    ctx, parity = relay.ctx, relay.parity
    lines = prompt_total // prompt_rows // 2
    line = ctx // 2

    def line_place(offset, side):
        return flip(line, offset) * 2 + side

    def prompt_piece(place):
        return xp.at[pl.ds(pl.multiple_of(place * prompt_rows, prompt_rows), prompt_rows)]

    loads = [
        pltpu.make_async_copy(x_ref, dob.at[pl.ds(0, length)], load_sems.at[0]),
        pltpu.make_async_copy(dy_ref, g.at[pl.ds(0, length)], load_sems.at[1]),
        pltpu.make_async_copy(dyp_ref, g.at[pl.ds(length, prompt_rows)], load_sems.at[2]),
        pltpu.make_async_copy(xp_ref, prompt_piece(ctx), load_sems.at[3]),
        pltpu.make_async_copy(sets_ref, sets, load_sems.at[4]),
    ]
    for load in reversed(loads):
        load.start()

    adapters = Gathered(relay, low_sets.at[:, :, pl.ds(0, 6 * D)], ad, lane_quarter, ad_sems)
    qkv_weights = Gathered(relay, wq_ref, wq, row_quarter, wq_sems, True)
    out_weights = Gathered(relay, wo_ref, wo, row_quarter, wo_sems, True)
    qkv_weights.own().start()
    out_weights.own().start()
    loads[4].wait()
    for index in range(owned):
        low_sets[index] = sets[index].astype(jnp.bfloat16)
    relay.greet([(line_place(step, parity), relay.me) for step in range(1, lines)])
    adapters.start()
    qkv_weights.start()

    def prompt_send(step):
        return pltpu.make_async_remote_copy(
            src_ref=xp_ref,
            dst_ref=prompt_piece(ctx),
            send_sem=xp_send.at[step],
            recv_sem=xp_recv.at[step],
            device_id=(line_place(step, parity), relay.me),
            device_id_type=MESH,
        )

    def prompt_landed(step):
        piece = prompt_piece(line_place(step, parity))
        return pltpu.make_async_remote_copy(
            src_ref=piece,
            dst_ref=piece,
            send_sem=xp_send.at[step],
            recv_sem=xp_recv.at[step],
            device_id=(line_place(step, parity), relay.me),
            device_id_type=MESH,
        )

    def prompt_gift(step, taken):
        piece = prompt_piece(line_place(step, 1 - parity if taken else parity))
        return pltpu.make_async_remote_copy(
            src_ref=xp_ref if step == 0 and not taken else piece,
            dst_ref=piece,
            send_sem=xp_give.at[step],
            recv_sem=xp_take.at[step],
            device_id=(relay.sibling, relay.me),
            device_id_type=MESH,
        )

    for step in reversed(range(1, lines)):
        prompt_send(step).start()
    prompt_gift(0, False).start()

    def unit_rows(values):
        values = values.astype(jnp.float32)
        centered = values - jnp.mean(values, axis=-1, keepdims=True)
        variance = jnp.mean(centered * centered, axis=-1, keepdims=True)
        return centered * lax.rsqrt(variance + 1e-05)

    loads[0].wait()
    tile = ROW_TILE

    @pl.loop(0, length // LINES)
    def _(index):
        start = pl.multiple_of(index * LINES, LINES)
        unit = unit_rows(dob[pl.ds(start, LINES), :])
        a1[pl.ds(prompt_total + start, LINES), :] = (
            unit * gain_ref[0:1, :] + shift_ref[0:1, :]
        ).astype(jnp.bfloat16)
        a2[pl.ds(start, LINES), :] = (unit * gain_ref[1:2, :] + shift_ref[1:2, :]).astype(
            jnp.bfloat16
        )

    loads[3].wait()
    unit = unit_rows(prompt_piece(ctx)[...])
    a2[pl.ds(length, prompt_rows), :] = (unit * gain_ref[1:2, :] + shift_ref[1:2, :]).astype(
        jnp.bfloat16
    )
    loads[1].wait()
    loads[2].wait()
    stores = [
        pltpu.make_async_copy(a2, a2_out, store_sems.at[0]),
        pltpu.make_async_copy(g, g_out, store_sems.at[1]),
        pltpu.make_async_copy(low_sets, low_out, store_sems.at[6]),
    ]
    for store in stores:
        store.start()

    last = len(relay.levels) - 1
    for level in range(last + 1):
        adapters.advance(level)
    qkv_weights.advance(0)
    out_weights.start()
    for step in reversed(range(1, lines)):
        prompt_landed(step).wait_recv()
        prompt_gift(step, False).start()
    adapters.own().wait()
    for level in range(last + 1):
        adapters.take(level)
    mine = ids_ref[0]
    picked[...] = ad[mine // owned, mine % owned]

    mid_keys[pl.ds(0, prompt_total), :] = jnp.zeros((prompt_total, R), jnp.bfloat16)
    d_mid_ref[pl.ds(length, prompt_rows), :] = jnp.zeros((prompt_rows, R), jnp.bfloat16)
    for start in range(0, length, tile):
        at, key_at = pl.ds(start, tile), pl.ds(prompt_total + start, tile)
        middle = matmul_bt(a1[key_at, :], picked[:, :D]).astype(jnp.bfloat16)
        mid_keys[key_at, :] = middle
        mid_ref[at, :] = middle
        d_mid_ref[at, :] = matmul_bt(g[at, :], picked[:, 5 * D : 6 * D]).astype(jnp.bfloat16)
    for step in range(lines):
        prompt_gift(step, True).wait_recv()

    @pl.loop(0, prompt_total // LINES)
    def _(index):
        at = pl.ds(pl.multiple_of(index * LINES, LINES), LINES)
        a1[at, :] = (unit_rows(xp[at, :]) * gain_ref[0:1, :] + shift_ref[0:1, :]).astype(
            jnp.bfloat16
        )

    stores.append(pltpu.make_async_copy(a1, a1_out, store_sems.at[2]))
    stores[-1].start()

    columns = []

    def project(slot):
        for index in range(per):
            col = pl.multiple_of(slot * share + index * chunk, chunk)
            turned = col < 2 * D
            scale = jnp.where(col < D, HD ** (-0.5), 1.0)
            weights = wq[slot, :, index * chunk : (index + 1) * chunk]
            b_part = picked[:, pl.ds(pl.multiple_of(col + D, chunk), chunk)]
            bias = bias_ref[:, pl.ds(col, chunk)]
            for start in range(0, keys, tile):
                at = pl.ds(start, tile)
                result = matmul(a1[at, :], weights) + matmul(mid_keys[at, :], b_part) + bias
                for row in range(0, tile, 128):
                    row_at = pl.ds(start + row, 128)
                    cosine = jnp.where(turned, cos_ref[row_at, :], 1.0)
                    low_sine = jnp.where(turned, low_ref[row_at, :], 0.0)
                    high_sine = jnp.where(turned, high_ref[row_at, :], 0.0)
                    for lane in range(0, chunk, 2 * HD):
                        part = pair_turn(
                            result[row : row + 128, lane : lane + 2 * HD],
                            cosine,
                            low_sine,
                            high_sine,
                        )
                        lane_at = pl.ds(pl.multiple_of(col + lane, 2 * HD), 2 * HD)
                        qkv[row_at, lane_at] = (part * scale).astype(jnp.bfloat16)
            column_at = pl.ds(col, chunk)
            copy = pltpu.make_async_copy(
                qkv.at[:, column_at], qkv_out.at[:, column_at], column_sems.at[len(columns)]
            )
            copy.start()
            columns.append(copy)

    project(relay.me)
    for level in range(last + 1):
        if level < last:
            qkv_weights.advance(level + 1)
        else:
            out_weights.advance(0)
        qkv_weights.take(level)
        for mask in range(1, slots):
            if bin(mask).count("1") == level + 1:
                project(flip(relay.me, mask))
    stores.append(pltpu.make_async_copy(wq, wq_out, store_sems.at[3]))
    stores[-1].start()

    for level in range(1, last + 1):
        out_weights.advance(level)
    for level in range(last + 1):
        out_weights.take(level)
    stores.append(pltpu.make_async_copy(wo, wo_out, store_sems.at[4]))
    stores[-1].start()
    out_share = wo.shape[2]
    for start in range(0, rows, OUT_TILE):
        at = pl.ds(start, min(OUT_TILE, rows - start))
        total = matmul(d_mid_ref[at, :], picked[:, 4 * D : 5 * D])
        for slot in range(slots):
            total += matmul_bt(g[at, pl.ds(slot * out_share, out_share)], wo[slot])
        dob[at, :] = total.astype(jnp.bfloat16)
    stores.append(pltpu.make_async_copy(dob, dob_out, store_sems.at[5]))
    stores[-1].start()

    for array in (adapters, qkv_weights, out_weights):
        array.finish()
    for step in range(1, lines):
        prompt_send(step).wait_send()
    for step in range(lines):
        prompt_gift(step, False).wait_send()
    for copy in columns + stores:
        copy.wait()


def front(ids, x_cont, x_prompt, dy_cont, dy_prompt, w_qkv, w_out, adapters, bias, gain, shift):
    slots = lax.axis_size("fsdp")
    places = lax.axis_size("ctx")
    length, prompt_rows = x_cont.shape[0], x_prompt.shape[0]
    rows, prompt_total = length + prompt_rows, prompt_rows * places
    keys = prompt_total + length
    share, out_share = w_qkv.shape[1], w_out.shape[1]
    owned, wide = adapters.shape[0], 6 * D
    columns = slots * (share // math.gcd(share, 256))
    low = jnp.bfloat16
    anywhere = pl.BlockSpec(memory_space=pl.ANY)
    on_chip = pl.BlockSpec(memory_space=pltpu.VMEM)
    return pl.pallas_call(
        functools.partial(front_kernel, length),
        in_specs=[pl.BlockSpec(memory_space=pltpu.SMEM)] + [anywhere] * 7 + [on_chip] * 6,
        out_specs=[anywhere] * 8 + [on_chip] * 3,
        out_shape=[
            jax.ShapeDtypeStruct((keys, 3 * D), low),
            jax.ShapeDtypeStruct((keys, D), low),
            jax.ShapeDtypeStruct((rows, D), low),
            jax.ShapeDtypeStruct((rows, D), low),
            jax.ShapeDtypeStruct((rows, D), low),
            jax.ShapeDtypeStruct((slots, D, share), low),
            jax.ShapeDtypeStruct((slots, D, out_share), low),
            jax.ShapeDtypeStruct(adapters.shape, low),
            jax.ShapeDtypeStruct((R, wide), low),
            jax.ShapeDtypeStruct((length, R), low),
            jax.ShapeDtypeStruct((rows, R), low),
        ],
        scratch_shapes=[
            pltpu.VMEM((slots, D, share), low),
            pltpu.VMEM((slots, D, out_share), low),
            pltpu.VMEM((slots, owned, R, wide), low),
            pltpu.VMEM(adapters.shape, jnp.float32),
            pltpu.VMEM(adapters.shape, low),
            pltpu.VMEM((prompt_total, D), low),
            pltpu.VMEM((keys, D), low),
            pltpu.VMEM((rows, D), low),
            pltpu.VMEM((rows, D), low),
            pltpu.VMEM((keys, 3 * D), low),
            pltpu.VMEM((rows, D), low),
            pltpu.VMEM((keys, R), low),
        ]
        + relay_sems(3, slots)
        + [pltpu.SemaphoreType.DMA((places // 2,)) for _ in range(4)]
        + [
            pltpu.SemaphoreType.DMA((5,)),
            pltpu.SemaphoreType.DMA((7,)),
            pltpu.SemaphoreType.DMA((columns,)),
        ],
        compiler_params=pltpu.CompilerParams(
            collective_id=1, has_side_effects=True, vmem_limit_bytes=VMEM_BYTES
        ),
        cost_estimate=pl.CostEstimate(
            flops=2 * keys * D * 3 * D + 2 * rows * D * D,
            bytes_accessed=50 * 1024 * 1024,
            transcendentals=rows,
        ),
    )(
        ids,
        x_cont,
        x_prompt,
        dy_cont,
        dy_prompt,
        w_qkv,
        w_out,
        adapters,
        bias,
        gain,
        shift,
        *turn_tables(keys),
    )


def attention_kernel(
    length,
    prompt_total,
    prompt_rows,
    ids_ref,
    q_ref,
    k_ref,
    v_ref,
    do_ref,
    cos_ref,
    low_ref,
    high_ref,
    up_ref,
    down_ref,
    ad_ref,
    o_ref,
    dq_ref,
    dk_ref,
    dv_ref,
    kvp_ref,
    up_out,
    down_out,
    chosen_ref,
    ad_slots,
    up_slots,
    down_slots,
    queries_ref,
    keys_ref,
    values_ref,
    outer_ref,
    keys_t_ref,
    values_t_ref,
    dk_sum,
    dv_sum,
    *sems,
):
    score_scale = HD ** (-0.5)
    key_count = prompt_total + length
    tile = KEY_TILE
    piece_rows = PIECE
    step = pl.program_id(0)
    last_step = H // 2 - 1
    relay = Relay(up_out.shape[0])
    ctx_place = relay.ctx
    first_member = jnp.where(relay.me == 0, 1.0, 0.0)
    back_sets = ad_ref.at[:, :, pl.ds(6 * D, WTOT - 6 * D)]
    resident = len(up_slots.shape) > 2
    if not resident:
        up_slots, down_slots = up_out, down_out
    adapters = Gathered(relay, back_sets, ad_slots, lane_quarter, sems_of(sems[:5], 0), True)
    up_weights = Gathered(relay, up_ref, up_slots, row_quarter, sems_of(sems[:5], 1), resident)
    early = down_ref.at[pl.ds(0, down_slots.shape[1])]
    down_weights = Gathered(relay, early, down_slots, row_quarter, sems_of(sems[:5], 2), resident)
    arrays = (adapters, up_weights, down_weights)
    store_sems = sems[5]
    levels = len(relay.levels)

    def stores(level):
        if not resident:
            return []
        return [
            pltpu.make_async_copy(array.slots.at[place], out.at[place], store_sems.at[index, place])
            for index, (array, out) in enumerate(((up_weights, up_out), (down_weights, down_out)))
            for place in up_weights.places(level)
        ]

    def store(level):
        for copy in stores(level):
            copy.start()

    late = []

    def at_step(when, action):
        if when > last_step:
            late.append((when, action))
        else:
            pl.when(step == when)(action)

    def begin():
        for array in arrays:
            if array.resident:
                array.own().start()
        relay.greet()
        for array in arrays:
            array.start()

    def settle(level):
        for array in arrays:
            array.take(level)
        store(level)

    def first_arrays(level):
        for array in arrays[:2]:
            array.forward(level)
        for array in arrays[:2]:
            array.give(level)

    at_step(0, begin)
    at_step(2, functools.partial(store, -1))
    for level in range(levels):
        at_step(3 + 3 * level, functools.partial(first_arrays, level))
        at_step(5 + 2 * level, functools.partial(down_weights.advance, level))
    for level in range(levels):
        at_step(7 if level < levels - 1 else 20, functools.partial(settle, level))

    wide, low = jnp.float32, jnp.bfloat16
    for start in range(0, key_count, tile):
        at = pl.ds(start, tile)
        queries_ref[at, :] = q_ref[at, :].astype(wide).astype(low)
        piece = k_ref[at, :].astype(wide)
        keys_ref[at, :] = piece.astype(low)
        keys_t_ref[:, at] = piece.T.astype(low)
        piece = v_ref[at, :].astype(wide)
        values_ref[at, :] = piece.astype(low)
        values_t_ref[:, at] = piece.T.astype(low)
    outer_ref[...] = do_ref[...].astype(wide).astype(low)

    class Unit:
        def __init__(self, row_start, rows, position_at, last_key, first, weight, head):
            self.at, self.position_at, self.rows = pl.ds(row_start, rows), position_at, rows
            self.head, self.weight, self.first = head, weight, first
            self.first_row = prompt_total + row_start
            if weight is not None:
                self.first_row = ctx_place * prompt_rows
            self.unmasked = 0 if weight is not None else prompt_total + row_start
            tiles = last_key // tile
            count = -(-last_key // SPAN)
            edges = [tile * (tiles * index // count) for index in range(count + 1)]
            self.spans = list(zip(edges[:-1], edges[1:]))
            self.tiles = range(0, last_key, piece_rows)
            self.scores, self.d_probs, self.raised, self.rounded, self.slopes = {}, {}, {}, {}, {}
            self.top = None

        def enter(self):
            lane = lax.broadcasted_iota(jnp.int32, (self.rows, 2 * HD), 1)
            mine = (lane >= self.head * HD) & (lane < (self.head + 1) * HD)
            queries, cotangent = queries_ref[self.position_at, :], outer_ref[self.at, :]
            self.q_head = jnp.where(mine, queries, jnp.zeros_like(queries))
            self.do_head = jnp.where(mine, cotangent, jnp.zeros_like(cotangent))
            for low_edge, high_edge in self.spans:
                at = pl.ds(low_edge, high_edge - low_edge)
                whole = matmul_bt(keys_ref[at, :], self.q_head)
                for start in range(low_edge, high_edge, piece_rows):
                    piece = whole[start - low_edge : start - low_edge + piece_rows]
                    if start + piece_rows > self.unmasked:
                        key_at = start + lax.broadcasted_iota(jnp.int32, piece.shape, 0)
                        row_at = lax.broadcasted_iota(jnp.int32, piece.shape, 1)
                        piece = jnp.where(key_at <= self.first_row + row_at, piece, masked_score)
                    self.scores[start] = piece
                    self.top = piece if self.top is None else jnp.maximum(self.top, piece)
                yield
                whole = matmul_bt(values_ref[at, :], self.do_head)
                for start in range(low_edge, high_edge, piece_rows):
                    self.d_probs[start] = whole[start - low_edge : start - low_edge + piece_rows]
                yield

        def soften(self):
            top = jnp.max(self.top, axis=0, keepdims=True)
            total, delta = None, None
            for start in self.tiles:
                piece = jnp.exp(self.scores[start] - top)
                part = piece * self.d_probs[start]
                self.raised[start] = piece
                total = piece if total is None else total + piece
                delta = part if delta is None else delta + part
                yield
            inverse = 1.0 / jnp.sum(total, axis=0, keepdims=True)
            delta = jnp.sum(delta, axis=0, keepdims=True) * inverse
            for start in self.tiles:
                soft = self.raised[start] * inverse
                self.rounded[start] = soft.astype(low)
                self.slopes[start] = (soft * (self.d_probs[start] - delta)).astype(low)
                yield
            if self.weight is not None:
                self.q_head = (self.q_head.astype(wide) * self.weight).astype(low)
                self.do_head = (self.do_head.astype(wide) * self.weight).astype(low)

        def span_of(self, pieces, span):
            return jnp.concatenate([pieces[start] for start in range(*span, piece_rows)], axis=0)

        def leave(self, partner=None):
            head_at = pl.ds(self.head * HD, HD)
            self.out_t, self.dq_t = None, None
            for span in self.spans:
                at = pl.ds(span[0], span[1] - span[0])
                part = matmul(values_t_ref[head_at, at], self.span_of(self.rounded, span))
                self.out_t = part if self.out_t is None else self.out_t + part
                yield
                part = matmul(keys_t_ref[head_at, at], self.span_of(self.slopes, span))
                self.dq_t = part if self.dq_t is None else self.dq_t + part
                yield
            if partner is None:
                return
            both_do = jnp.concatenate([partner.do_head, self.do_head], axis=0)
            both_q = jnp.concatenate([partner.q_head, self.q_head], axis=0)
            for span in self.spans:
                at = pl.ds(span[0], span[1] - span[0])
                for total, name, right in (
                    (dv_sum, "rounded", both_do),
                    (dk_sum, "slopes", both_q),
                ):
                    left = [
                        unit.span_of(getattr(unit, name), span) for unit in (partner, self)
                    ]
                    part = matmul(jnp.concatenate(left, axis=1), right)
                    total[at, :] = part if self.first else total[at, :] + part
                    yield

    blocks = [
        (
            row_start,
            QUERY_TILE,
            pl.ds(prompt_total + row_start, QUERY_TILE),
            prompt_total + row_start + QUERY_TILE,
            None,
        )
        for row_start in reversed(range(0, length, QUERY_TILE))
    ]
    own_at = pl.ds(pl.multiple_of(ctx_place * prompt_rows, prompt_rows), prompt_rows)
    blocks.append((length, prompt_rows, own_at, prompt_total, first_member))
    units = []
    for index, (row_start, rows, position_at, last_key, weight) in enumerate(blocks):
        for head in range(2):
            first = index == 0
            units.append(Unit(row_start, rows, position_at, last_key, first, weight, head))

    def close(index):
        if index % 2 == 0:
            return
        pair = units[index - 1 : index + 1]
        at, position_at = pair[0].at, pair[0].position_at
        o_ref[at, :] = jnp.concatenate([unit.out_t for unit in pair], axis=0).T.astype(o_ref.dtype)
        d_queries = jnp.concatenate([unit.dq_t for unit in pair], axis=0).T * score_scale
        turn = [table[position_at, :] for table in (cos_ref, low_ref, high_ref)]
        dq_ref[at, :] = pair_turn_back(d_queries, *turn).astype(dq_ref.dtype)

    for _ in units[0].enter():
        pass
    def leaving(index):
        unit = units[index]
        partner = units[index - 1] if unit.head == 1 else None
        return unit.leave(partner), (4 if partner else 2) * len(unit.spans)

    for index, unit in enumerate(units):
        side, side_count = [], 0
        if index > 0:
            generator, count = leaving(index - 1)
            side.append(generator)
            side_count += count
        if index + 1 < len(units):
            side.append(units[index + 1].enter())
            side_count += 2 * len(units[index + 1].spans)
        together(unit.soften(), 2 * len(unit.tiles), chain(*side), side_count)
        if index > 0:
            close(index - 1)
    for _ in leaving(len(units) - 1)[0]:
        pass
    close(len(units) - 1)

    prompt_at = pl.ds(0, prompt_total)
    kvp_ref[0] = dk_sum[prompt_at, :].astype(kvp_ref.dtype)
    kvp_ref[1] = dv_sum[prompt_at, :].astype(kvp_ref.dtype)
    own_at = pl.ds(prompt_total, length)
    turned_back = pair_turn_back(
        dk_sum[own_at, :], cos_ref[own_at, :], low_ref[own_at, :], high_ref[own_at, :]
    )
    dk_ref[...] = turned_back.astype(dk_ref.dtype)
    dv_ref[...] = dv_sum[own_at, :].astype(dv_ref.dtype)

    @pl.when(step == last_step)
    def _():
        for _, action in sorted(late, key=lambda item: item[0]):
            action()
        for array in arrays:
            if not array.resident:
                array.own().wait()
            array.finish()
        for level in range(-1, levels):
            for copy in stores(level):
                copy.wait()
        mine, owned = ids_ref[0], ad_slots.shape[1]
        chosen_ref[...] = ad_slots[mine // owned, mine % owned]


def turn_tables(count):
    half_rot = ROT // 2
    place = np.arange(half_rot, dtype=np.float32)
    frequency = np.float32(10000.0) ** (np.float32(-2.0) * place / np.float32(ROT))
    angles = np.arange(count, dtype=np.float32)[:, None] * frequency[None, :]
    cosine, sine_part = np.cos(angles), np.sin(angles)
    rest = np.zeros((count, HD - ROT), np.float32)
    gap = np.zeros((count, half_rot), np.float32)

    def pair(parts):
        return np.concatenate(parts + parts, axis=1).astype(np.float32)

    return (
        pair([cosine, cosine, rest + 1.0]),
        pair([-sine_part, gap, rest]),
        pair([gap, sine_part, rest]),
    )


def attention(ids, qkv, d_attended, w_up, w_down, low_sets, length):
    slots = lax.axis_size("fsdp")
    row_count = d_attended.shape[0]
    prompt_rows = row_count - length
    key_count = qkv.shape[0]
    prompt_total = key_count - length
    wide = 2 * HD
    low = jnp.bfloat16
    resident = key_count <= 2048

    def column(rows, start=0):
        return pl.BlockSpec((rows, wide), lambda pair: (0, start // wide + pair))

    down_shape = (slots, w_down.shape[0] // 4 * 3, w_down.shape[1])
    table = pl.BlockSpec((key_count, wide), lambda pair: (0, 0))
    anywhere = pl.BlockSpec(memory_space=pl.ANY)
    area = row_count * key_count * 0.75
    return pl.pallas_call(
        functools.partial(attention_kernel, length, prompt_total, prompt_rows),
        grid=(H // 2,),
        in_specs=[
            pl.BlockSpec(memory_space=pltpu.SMEM),
            column(key_count),
            column(key_count, D),
            column(key_count, 2 * D),
            column(row_count),
            table,
            table,
            table,
            anywhere,
            anywhere,
            anywhere,
        ],
        out_specs=[
            column(row_count),
            column(row_count),
            column(length),
            column(length),
            pl.BlockSpec((2, prompt_total, wide), lambda pair: (0, 0, pair)),
            anywhere,
            anywhere,
            pl.BlockSpec((R, WTOT - 6 * D), lambda pair: (0, 0)),
        ],
        out_shape=[
            jax.ShapeDtypeStruct((row_count, D), low),
            jax.ShapeDtypeStruct((row_count, D), low),
            jax.ShapeDtypeStruct((length, D), low),
            jax.ShapeDtypeStruct((length, D), low),
            jax.ShapeDtypeStruct((2, prompt_total, D), low),
            jax.ShapeDtypeStruct((slots,) + w_up.shape, low),
            jax.ShapeDtypeStruct(down_shape, low),
            jax.ShapeDtypeStruct((R, WTOT - 6 * D), low),
        ],
        scratch_shapes=[
            pltpu.VMEM((slots,) + low_sets.shape[:2] + (WTOT - 6 * D,), low),
            pltpu.VMEM((slots,) + w_up.shape if resident else (16, 128), low),
            pltpu.VMEM(down_shape if resident else (16, 128), low),
            pltpu.VMEM((key_count, wide), low),
            pltpu.VMEM((key_count, wide), low),
            pltpu.VMEM((key_count, wide), low),
            pltpu.VMEM((row_count, wide), low),
            pltpu.VMEM((wide, key_count), low),
            pltpu.VMEM((wide, key_count), low),
            pltpu.VMEM((key_count, wide), jnp.float32),
            pltpu.VMEM((key_count, wide), jnp.float32),
        ]
        + relay_sems(3, slots)
        + [pltpu.SemaphoreType.DMA((2, slots))],
        compiler_params=pltpu.CompilerParams(
            collective_id=2, has_side_effects=True, vmem_limit_bytes=VMEM_BYTES
        ),
        cost_estimate=pl.CostEstimate(
            flops=int(12 * area * D), bytes_accessed=32 * 1024 * 1024, transcendentals=int(area * H)
        ),
    )(ids, qkv, qkv, qkv, d_attended, *turn_tables(key_count), w_up, w_down, low_sets)


def mlp_kernel(
    length,
    a_ref,
    g_ref,
    up_ref,
    down_ref,
    a_up_ref,
    b_up_ref,
    a_down_ref,
    b_down_ref,
    bias_ref,
    kvp_ref,
    shard_ref,
    ids_ref,
    cos_ref,
    low_ref,
    high_ref,
    out_ref,
    d_in_ref,
    grads_ref,
    share_ref,
    ids_out,
    mid_up,
    d_mid_down,
    mid_down_sum,
    d_mid_up_sum,
    first,
    first_sum,
    second,
    third,
    id_tiles,
    a,
    g,
    w_up,
    w_down,
    late,
    kvp,
    own_sem,
    load_sems,
    *sems,
):
    step = pl.program_id(0)
    last_step = pl.num_programs(0) - 1
    members, prompt_total, part = first.shape
    places, prompt_rows, _ = second.shape
    ctx, me = lax.axis_index("ctx"), lax.axis_index("fsdp")
    halves = members // 2

    def prompt_part(place):
        columns = pl.ds(pl.multiple_of((place % halves) * part, part), part)
        return kvp.at[place // halves, :, columns]

    def owned_rows(place):
        return first_sum.at[pl.ds(pl.multiple_of(place * prompt_rows, prompt_rows), prompt_rows)]

    over_members = Trade("fsdp", members, prompt_part, first, sems[0:2])
    over_places = Trade("ctx", places, owned_rows, second, sems[2:4])
    to_members = Trade("fsdp", members, lambda place: third.at[me], third, sems[4:6])
    id_trade = Trade("ctx", places, lambda place: id_tiles.at[ctx], id_tiles, sems[6:8])
    own_part = pltpu.make_async_copy(prompt_part(me), first.at[me], own_sem)
    relay = Relay(members)
    late_rows = late.shape[1]
    late_shard = shard_ref.at[pl.ds(shard_ref.shape[0] - late_rows, late_rows)]
    late_down = Gathered(relay, late_shard, late, row_quarter, sems_of(sems[8:13], 0), True)
    levels = range(len(relay.levels))
    loads = [
        pltpu.make_async_copy(a_ref, a, load_sems.at[0]),
        pltpu.make_async_copy(g_ref, g, load_sems.at[1]),
        pltpu.make_async_copy(kvp_ref, kvp, load_sems.at[2]),
    ]

    @pl.when(step == 0)
    def _():
        for load in loads:
            load.start()
        late_down.own().start()
        id_tiles[ctx] = jnp.full(id_tiles.shape[1:], ids_ref[0].astype(jnp.float32))
        greet_all(
            [(ctx, flip(me, offset)) for offset in range(1, members)]
            + [(flip(ctx, offset), me) for offset in range(1, places)]
        )
        late_down.start()
        loads[2].wait()
        own_part.start()
        over_members.start()
        id_trade.start()

    @pl.when(step == last_step // 2 + 1)
    def _():
        own_part.wait()
        over_members.wait()
        total = first[0].astype(jnp.float32)
        for member in range(1, members):
            total += first[member].astype(jnp.float32)
        first_sum[...] = total.astype(jnp.bfloat16)
        over_places.start()

    @pl.when(step == last_step - 1)
    def _():
        over_places.wait()
        second[ctx] = owned_rows(ctx)[...]
        total = second[0].astype(jnp.float32)
        for place in range(1, places):
            total += second[place].astype(jnp.float32)
        is_key = me < halves
        own_at = pl.ds(pl.multiple_of(ctx * prompt_rows, prompt_rows), prompt_rows)
        cosine = jnp.where(is_key, cos_ref[own_at, :], 1.0)
        low_sine = jnp.where(is_key, low_ref[own_at, :], 0.0)
        high_sine = jnp.where(is_key, high_ref[own_at, :], 0.0)
        for lane in range(0, part, 2 * HD):
            third[me, :, lane : lane + 2 * HD] = pair_turn_back(
                total[:, lane : lane + 2 * HD], cosine, low_sine, high_sine
            ).astype(jnp.bfloat16)
        to_members.start()

    rows = a.shape[0]
    slots, wide, share = down_ref.shape
    low = jnp.bfloat16
    chunk = min(256, wide)
    parts = range(0, wide, chunk)
    tiles = [pl.ds(start, min(MLP_ROWS, rows - start)) for start in range(0, rows, MLP_ROWS)]

    def masked(values):
        row = lax.broadcasted_iota(jnp.int32, values.shape, 0)
        return jnp.where(row < length, values, 0.0).astype(low)

    @pl.when(step == 0)
    def _():
        for load in loads[:2]:
            load.wait()
        mid_up[...] = masked(matmul_bt(a[...], a_up_ref[...]))
        d_mid_down[...] = masked(matmul_bt(g[...], b_down_ref[...]))
        mid_down_sum[...] = jnp.zeros_like(mid_down_sum)
        d_mid_up_sum[...] = jnp.zeros_like(d_mid_up_sum)
        out_ref[...] = jnp.zeros_like(out_ref)
        d_in_ref[...] = jnp.zeros_like(d_in_ref)

    w_up[...] = up_ref[0].astype(jnp.float32).astype(low)
    early = last_step + 1 - late_rows // wide

    @pl.when(step < early)
    def _():
        for slot in range(slots):
            piece = down_ref[slot].astype(jnp.float32).astype(low)
            w_down[:, slot * share : (slot + 1) * share] = piece

    for level in levels:

        @pl.when(step == min(2 + 2 * level, early - 1))
        def _():
            late_down.advance(level)

    @pl.when(step == early)
    def _():
        for level in levels:
            late_down.take(level)

    @pl.when(step >= early)
    def _():
        lines = pl.ds(pl.multiple_of((step - early) * wide, wide), wide)
        for slot in range(slots):
            w_down[:, slot * share : (slot + 1) * share] = late[slot, lines, :]

    b_up, a_down = b_up_ref[...], a_down_ref[...]
    bias = bias_ref[...]

    class Unit:
        def __init__(self, at):
            self.at = at
            self.up, self.d_hidden, self.hidden, self.d_up = [], [], [], []

        def enter(self):
            for start in parts:
                lanes = slice(start, start + chunk)
                up = matmul(a[self.at, :], w_up[:, lanes])
                self.up.append(up + matmul(mid_up[self.at, :], b_up[:, lanes]) + bias[:, lanes])
                yield
                d_hidden = matmul_bt(g[self.at, :], w_down[lanes, :])
                self.d_hidden.append(d_hidden + matmul(d_mid_down[self.at, :], a_down[:, lanes]))
                yield

        def bend(self):
            for up, d_hidden in zip(self.up, self.d_hidden):
                height = up.shape[0]
                edges = [0, height // 32 * 16 + height % 32, height]
                hidden, d_up = [], []
                for lane in range(0, chunk, 128):
                    hidden_rows, d_rows = [], []
                    for low_edge, high_edge in zip(edges[:-1], edges[1:]):
                        u = up[low_edge:high_edge, lane : lane + 128]
                        cdf = 0.5 + 0.5 * lax.erf(u * (0.5**0.5))
                        density = jnp.exp(-0.5 * (u * u)) * ((2.0 * math.pi) ** -0.5)
                        hidden_rows.append((u * cdf).astype(low))
                        d_piece = d_hidden[low_edge:high_edge, lane : lane + 128]
                        d_rows.append((d_piece * (cdf + u * density)).astype(low))
                        yield
                    hidden.append(jnp.concatenate(hidden_rows, axis=0))
                    d_up.append(jnp.concatenate(d_rows, axis=0))
                self.hidden.append(jnp.concatenate(hidden, axis=1))
                self.d_up.append(jnp.concatenate(d_up, axis=1))

        def leave(self):
            at = self.at
            for column in range(0, D, 256):
                lanes = slice(column, column + 256)
                total = out_ref[at, lanes]
                for start, hidden in zip(parts, self.hidden):
                    total += matmul(hidden, w_down[start : start + chunk, lanes])
                out_ref[at, lanes] = total
                yield
                total = d_in_ref[at, lanes]
                for start, d_up in zip(parts, self.d_up):
                    total += matmul_bt(d_up, w_up[lanes, start : start + chunk])
                d_in_ref[at, lanes] = total
                yield
            self.grads = []
            middle, d_middle = mid_down_sum[at, :], d_mid_up_sum[at, :]
            for start, hidden, d_up in zip(parts, self.hidden, self.d_up):
                middle += matmul_bt(hidden, a_down[:, start : start + chunk])
                d_middle += matmul_bt(d_up, b_up[:, start : start + chunk])
                self.grads.append(
                    (matmul_at(mid_up[at, :], d_up), matmul_at(d_mid_down[at, :], hidden))
                )
                yield
            mid_down_sum[at, :] = middle
            d_mid_up_sum[at, :] = d_middle

    units = [Unit(at) for at in tiles]
    enters, leaves, bends = 2 * len(parts), 8 + len(parts), 2 * len(parts) * (chunk // 128)
    for _ in units[0].enter():
        pass
    for index, unit in enumerate(units):
        side, side_count = [], 0
        if index > 0:
            side.append(units[index - 1].leave())
            side_count += leaves
        if index + 1 < len(units):
            side.append(units[index + 1].enter())
            side_count += enters
        together(unit.bend(), bends, chain(*side), side_count)
    for _ in units[-1].leave():
        pass
    grad_b_up = jnp.concatenate(
        [sum(unit.grads[index][0] for unit in units) for index in range(len(parts))], axis=1
    )
    grad_a_down = jnp.concatenate(
        [sum(unit.grads[index][1] for unit in units) for index in range(len(parts))], axis=1
    )
    for start, value in ((D, grad_b_up), (D + FF, grad_a_down)):
        columns = pl.ds(pl.multiple_of(start + step * wide, wide), wide)
        grads_ref[:, columns] = value.astype(jnp.bfloat16)

    @pl.when(step == last_step)
    def _():
        mid_down = masked(mid_down_sum[...])
        d_mid_up = masked(d_mid_up_sum[...])
        out_ref[...] += matmul(mid_down, b_down_ref[...])
        d_in_ref[...] += matmul(d_mid_up, a_up_ref[...])
        grads_ref[:, :D] = matmul_at(d_mid_up, a[...]).astype(jnp.bfloat16)
        grads_ref[:, D + 2 * FF :] = matmul_at(mid_down, g[...]).astype(jnp.bfloat16)
        to_members.wait()
        id_trade.wait()
        share_ref[...] = third[...]
        ids_out[...] = id_tiles[...]
        for trade in (over_members, over_places, to_members, id_trade, late_down):
            trade.finish()


def mlp(mlp_in, grad_rows, up_slots, down_slots, chosen, frozen_bias, kvp, w_down, ids, length):
    rows = mlp_in.shape[0]
    prompt_total, prompt_rows = kvp.shape[1], rows - length
    places = lax.axis_size("ctx")
    slots, _, up_share = up_slots.shape
    down_share = down_slots.shape[2]
    wide = math.gcd(up_share, 512)
    per = up_share // wide
    early = down_slots.shape[1] // wide
    late_rows = w_down.shape[0] - down_slots.shape[1]

    def whole(shape):
        return pl.BlockSpec(shape, lambda step: (0,) * len(shape))

    def columns(start, width):
        return pl.BlockSpec((R, width), lambda step: (0, start // width))

    def moving(height, start):
        return pl.BlockSpec((height, wide), lambda step: (0, start // wide + step))

    return pl.pallas_call(
        functools.partial(mlp_kernel, length),
        grid=(FF // wide,),
        in_specs=[
            pl.BlockSpec(memory_space=pl.ANY),
            pl.BlockSpec(memory_space=pl.ANY),
            pl.BlockSpec((1, D, wide), lambda step: (step // per, 0, step % per)),
            pl.BlockSpec((slots, wide, down_share), lambda step: (0, jnp.minimum(step, early - 1), 0)),
            columns(0, D),
            moving(R, D),
            moving(R, D + FF),
            columns(D + 2 * FF, D),
            moving(1, 4 * D),
            pl.BlockSpec(memory_space=pl.ANY),
            pl.BlockSpec(memory_space=pl.ANY),
            pl.BlockSpec(memory_space=pltpu.SMEM),
        ]
        + [whole((prompt_total, 2 * HD))] * 3,
        out_specs=[
            whole((rows, D)),
            whole((rows, D)),
            whole((R, 2 * D + 2 * FF)),
            whole((slots, prompt_rows, 2 * D // slots)),
            whole((places, 8, 2 * HD)),
        ],
        out_shape=[
            jax.ShapeDtypeStruct((rows, D), jnp.float32),
            jax.ShapeDtypeStruct((rows, D), jnp.float32),
            jax.ShapeDtypeStruct((R, 2 * D + 2 * FF), jnp.bfloat16),
            jax.ShapeDtypeStruct((slots, prompt_rows, 2 * D // slots), jnp.bfloat16),
            jax.ShapeDtypeStruct((places, 8, 2 * HD), jnp.float32),
        ],
        scratch_shapes=[
            pltpu.VMEM((rows, R), jnp.bfloat16),
            pltpu.VMEM((rows, R), jnp.bfloat16),
            pltpu.VMEM((rows, R), jnp.float32),
            pltpu.VMEM((rows, R), jnp.float32),
            pltpu.VMEM((slots, prompt_total, 2 * D // slots), jnp.bfloat16),
            pltpu.VMEM((prompt_total, 2 * D // slots), jnp.bfloat16),
            pltpu.VMEM((places, prompt_rows, 2 * D // slots), jnp.bfloat16),
            pltpu.VMEM((slots, prompt_rows, 2 * D // slots), jnp.bfloat16),
            pltpu.VMEM((places, 8, 2 * HD), jnp.float32),
            pltpu.VMEM((rows, D), jnp.bfloat16),
            pltpu.VMEM((rows, D), jnp.bfloat16),
            pltpu.VMEM((D, wide), jnp.bfloat16),
            pltpu.VMEM((wide, D), jnp.bfloat16),
            pltpu.VMEM((slots, late_rows, down_share), jnp.bfloat16),
            pltpu.VMEM(kvp.shape, jnp.bfloat16),
            pltpu.SemaphoreType.DMA,
            pltpu.SemaphoreType.DMA((3,)),
        ]
        + trade_sems(slots)
        + trade_sems(places)
        + trade_sems(slots)
        + trade_sems(places)
        + relay_sems(1, slots),
        compiler_params=pltpu.CompilerParams(
            collective_id=3, has_side_effects=True, vmem_limit_bytes=VMEM_BYTES
        ),
        cost_estimate=pl.CostEstimate(
            flops=8 * rows * D * FF,
            bytes_accessed=30 * 1024 * 1024,
            transcendentals=2 * rows * FF,
        ),
    )(
        mlp_in,
        grad_rows,
        up_slots,
        down_slots,
        chosen,
        chosen,
        chosen,
        chosen,
        frozen_bias[None],
        kvp,
        w_down,
        ids,
        *turn_tables(prompt_total),
    )


def tail_kernel(
    length,
    x_ref,
    xp_ref,
    g_ref,
    ob_ref,
    dq_ref,
    dk_ref,
    dv_ref,
    share_ref,
    a1_ref,
    mlp_ref,
    d_mlp_ref,
    wq_ref,
    wo_ref,
    picked,
    mid_qkv,
    d_mid_out,
    back_ref,
    ids_ref,
    bias_ref,
    gain_ref,
    cont_out,
    prompt_out,
    cont_grad,
    prompt_grad,
    sums_ref,
    norm_ref,
    x,
    g,
    ob,
    dqkv,
    a1,
    result,
    d_rows,
    wq,
    wo,
    mid_out,
    d_mid_qkv,
    grads,
    first,
    bins,
    second,
    full,
    norm_members,
    norm_places,
    load_sems,
    store_sems,
    *sems,
):
    rows = x.shape[0]
    prompt_rows = rows - length
    places, members, owned = full.shape[0], second.shape[0], full.shape[1]
    width = first.shape[2]
    part = 2 * D // members
    slots, _, share = wq.shape
    out_share = wo.shape[2]
    ctx, me = lax.axis_index("ctx"), lax.axis_index("fsdp")
    parity, line, lines = ctx % 2, ctx // 2, places // 2
    sibling = ctx + 1 - 2 * parity
    own_rows, prompt_at = pl.ds(0, length), pl.ds(length, prompt_rows)

    front_places = 6 * D // width
    pairs = [
        (back_ref, grads.at[:, pl.ds(6 * D, WTOT - 6 * D)]),
        (dq_ref, dqkv.at[:, pl.ds(0, D)]),
        (dk_ref, dqkv.at[own_rows, pl.ds(D, D)]),
        (dv_ref, dqkv.at[own_rows, pl.ds(2 * D, D)]),
        (a1_ref.at[pl.ds(a1_ref.shape[0] - length, length)], a1),
        (ob_ref, ob),
        (g_ref, g),
        (wo_ref, wo),
        (x_ref, x.at[own_rows]),
        (xp_ref, x.at[prompt_at]),
        (mlp_ref, result),
        (wq_ref, wq),
        (d_mlp_ref, d_rows),
    ] + [
        (share_ref.at[slot], dqkv.at[prompt_at, pl.ds(D + slot * part, part)])
        for slot in range(members)
    ]
    loads = [
        pltpu.make_async_copy(source, target, load_sems.at[index])
        for index, (source, target) in enumerate(pairs)
    ]
    for load in loads:
        load.start()

    def grad_part(place):
        return grads.at[:, pl.ds(pl.multiple_of(place * width, width), width)]

    def line_place(offset, side):
        return flip(line, offset) * 2 + side

    over_places = Trade("ctx", places, grad_part, first, sems[0:2])
    over_members = Trade(
        "fsdp", members, lambda place: bins.at[pl.ds(place * owned, owned)], second, sems[2:4]
    )
    norm_a = Trade("fsdp", members, lambda place: norm_members.at[me], norm_members, sems[4:6])
    norm_b = Trade("ctx", places, lambda place: norm_places.at[ctx], norm_places, sems[6:8])
    line_sems, gift_sems = sems[8:10], sems[10:12]

    def line_send(offset):
        part_ref = full.at[ctx]
        return remote_copy(
            part_ref, part_ref, line_sems, offset, (line_place(offset, parity), me)
        )

    def line_landed(offset):
        part_ref = full.at[line_place(offset, parity)]
        return remote_copy(
            part_ref, part_ref, line_sems, offset, (line_place(offset, parity), me)
        )

    def gift(offset, taken=False):
        side = 1 - parity if taken else parity
        part_ref = full.at[line_place(offset, side)]
        return remote_copy(part_ref, part_ref, gift_sems, offset, (sibling, me))

    greet_all(
        [(ctx, flip(me, offset)) for offset in range(1, members)]
        + [(flip(ctx, offset), me) for offset in range(1, places)]
    )

    def send_grads(front):
        for offset in reversed(range(1, places)):
            is_front = flip(ctx, offset) < front_places

            @pl.when(is_front if front else jnp.logical_not(is_front))
            def _():
                over_places.send(offset).start()

    loads[0].wait()
    send_grads(False)
    for load in loads[1:7]:
        load.wait()
    low = jnp.bfloat16
    d_mid_qkv[prompt_at, :] = jnp.zeros((prompt_rows, R), low)
    mid_out[prompt_at, :] = jnp.zeros((prompt_rows, R), low)
    tile = ROW_TILE
    grad_parts = [None] * 4
    for start in range(0, length, tile):
        at = pl.ds(start, tile)
        d_middle = matmul_bt(dqkv[at, :], picked[:, D : 4 * D]).astype(low)
        middle = matmul_bt(ob[at, :], picked[:, 4 * D : 5 * D]).astype(low)
        d_mid_qkv[at, :] = d_middle
        mid_out[at, :] = middle
        parts = (
            matmul_at(d_middle, a1[at, :]),
            matmul_at(mid_qkv[at, :], dqkv[at, :]),
            matmul_at(d_mid_out[at, :], ob[at, :]),
            matmul_at(middle, g[at, :]),
        )
        grad_parts = [
            new if old is None else old + new for old, new in zip(grad_parts, parts)
        ]
    for start, value in zip((0, D, 4 * D, 5 * D), grad_parts):
        grads[:, start : start + value.shape[1]] = value.astype(low)
    send_grads(True)
    for load in loads[7:11]:
        load.wait()
    tiles = [(start, min(OUT_TILE, rows - start)) for start in range(0, rows, OUT_TILE)]
    def out_rows(start, size):
        at = pl.ds(start, size)
        adapted = matmul(mid_out[at, :], picked[:, 5 * D : 6 * D])
        for slot in range(slots):
            lanes = slice(slot * out_share, (slot + 1) * out_share)
            first_bias = bias_ref[:, 3 * D + slot * out_share : 3 * D + (slot + 1) * out_share]
            second_start = 4 * D + FF + slot * out_share
            second_bias = bias_ref[:, second_start : second_start + out_share]
            result[at, lanes] += (
                x[at, lanes].astype(jnp.float32)
                + matmul(ob[at, :], wo[slot])
                + adapted[:, lanes]
                + first_bias
                + second_bias
            )

    def back_rows(start, size):
        at = pl.ds(start, size)
        d_attn_in = matmul(d_mid_qkv[at, :], picked[:, :D])
        for slot in range(slots):
            d_attn_in += matmul_bt(dqkv[at, slot * share : (slot + 1) * share], wq[slot])
        for row in range(0, size, 16):
            row_at = pl.ds(start + row, 16)
            values = x[row_at, :].astype(jnp.float32)
            centered = values - jnp.mean(values, axis=-1, keepdims=True)
            variance = jnp.mean(centered * centered, axis=-1, keepdims=True)
            scale = lax.rsqrt(variance + 1e-05)
            unit = centered * scale
            d_unit = d_attn_in[row : row + 16] * gain_ref[0:1, :]
            d_unit += d_rows[row_at, :] * gain_ref[1:2, :]
            mean_d = jnp.mean(d_unit, axis=-1, keepdims=True)
            mean_du = jnp.mean(d_unit * unit, axis=-1, keepdims=True)
            d_rows[row_at, :] = g[row_at, :].astype(jnp.float32) + scale * (
                d_unit - mean_d - unit * mean_du
            )

    half = len(tiles) // 2
    for start, size in tiles[:half]:
        out_rows(start, size)

    over_places.wait()
    first[ctx] = grad_part(ctx)[...]
    for index in range(members * owned):
        total = None
        for place in range(places):
            matches = ids_ref[place, 0:1, 0:1] == float(index)
            piece = jnp.where(matches, first[place].astype(jnp.float32), 0.0)
            total = piece if total is None else total + piece
        bins[index] = total.astype(low)
    over_members.start()

    for start, size in tiles[half:]:
        out_rows(start, size)
    stores = [
        pltpu.make_async_copy(result.at[own_rows], cont_out, store_sems.at[0]),
        pltpu.make_async_copy(result.at[prompt_at], prompt_out, store_sems.at[1]),
    ]
    for store in stores:
        store.start()
    for load in loads[11:]:
        load.wait()

    over_members.wait()
    second[me] = bins[pl.ds(me * owned, owned)]
    total = second[0].astype(jnp.float32)
    for member in range(1, members):
        total += second[member].astype(jnp.float32)
    full[ctx] = total.astype(low)
    for offset in reversed(range(1, lines)):
        line_send(offset).start()
    gift(0).start()
    norm_members[me] = jnp.full(norm_members.shape[1:], jnp.sum(total * total))
    norm_a.start()

    for start, size in tiles[:1]:
        back_rows(start, size)
    norm_a.wait()
    square = norm_members[0]
    for member in range(1, members):
        square = square + norm_members[member]
    norm_places[ctx] = square
    norm_b.start()
    for start, size in tiles[1 : half + 1]:
        back_rows(start, size)
    for offset in reversed(range(1, lines)):
        line_landed(offset).wait_recv()
        gift(offset).start()
    for start, size in tiles[half + 1 :]:
        back_rows(start, size)
    stores += [
        pltpu.make_async_copy(d_rows.at[own_rows], cont_grad, store_sems.at[2]),
        pltpu.make_async_copy(d_rows.at[prompt_at], prompt_grad, store_sems.at[3]),
    ]
    for store in stores[2:]:
        store.start()
    norm_b.wait()
    square = norm_places[0]
    for place in range(1, places):
        square = square + norm_places[place]
    norm_ref[...] = jnp.sqrt(square)
    for offset in range(lines):
        gift(offset, taken=True).wait_recv()
    sums_ref[...] = full[...]
    for trade in (over_places, over_members, norm_a, norm_b):
        trade.finish()
    for offset in range(1, lines):
        line_send(offset).wait_send()
    for offset in range(lines):
        gift(offset).wait_send()
    for store in stores:
        store.wait()


def tail(
    x_cont,
    x_prompt,
    grad_rows,
    attended,
    dq_rows,
    dk_own,
    dv_own,
    prompt_share,
    attn_in,
    mlp_out,
    d_mlp_in,
    qkv_slots,
    out_slots,
    picked,
    mid_qkv,
    d_mid_out,
    back_grads,
    id_tiles,
    frozen_bias,
    norm_gain,
    owned,
):
    rows, length, prompt_rows = attended.shape[0], x_cont.shape[0], x_prompt.shape[0]
    places, members = lax.axis_size("ctx"), lax.axis_size("fsdp")
    width = WTOT // places
    low, wide = jnp.bfloat16, jnp.float32
    anywhere = pl.BlockSpec(memory_space=pl.ANY)
    on_chip = pl.BlockSpec(memory_space=pltpu.VMEM)
    return pl.pallas_call(
        functools.partial(tail_kernel, length),
        in_specs=[anywhere] * 13 + [on_chip] * 3 + [anywhere] + [on_chip] * 3,
        out_specs=[anywhere] * 4 + [on_chip] * 2,
        out_shape=[
            jax.ShapeDtypeStruct((length, D), wide),
            jax.ShapeDtypeStruct((prompt_rows, D), wide),
            jax.ShapeDtypeStruct((length, D), wide),
            jax.ShapeDtypeStruct((prompt_rows, D), wide),
            jax.ShapeDtypeStruct((places, owned, R, width), low),
            jax.ShapeDtypeStruct((8, 2 * HD), wide),
        ],
        scratch_shapes=[
            pltpu.VMEM((rows, D), low),
            pltpu.VMEM((rows, D), low),
            pltpu.VMEM((rows, D), low),
            pltpu.VMEM((rows, 3 * D), low),
            pltpu.VMEM((length, D), low),
            pltpu.VMEM((rows, D), wide),
            pltpu.VMEM((rows, D), wide),
            pltpu.VMEM(qkv_slots.shape, low),
            pltpu.VMEM(out_slots.shape, low),
            pltpu.VMEM((rows, R), low),
            pltpu.VMEM((rows, R), low),
            pltpu.VMEM((R, WTOT), low),
            pltpu.VMEM((places, R, width), low),
            pltpu.VMEM((members * owned, R, width), low),
            pltpu.VMEM((members, owned, R, width), low),
            pltpu.VMEM((places, owned, R, width), low),
            pltpu.VMEM((members, 8, 2 * HD), wide),
            pltpu.VMEM((places, 8, 2 * HD), wide),
            pltpu.SemaphoreType.DMA((13 + members,)),
            pltpu.SemaphoreType.DMA((4,)),
        ]
        + trade_sems(places)
        + trade_sems(members)
        + trade_sems(members)
        + trade_sems(places)
        + [pltpu.SemaphoreType.DMA((places // 2,)) for _ in range(4)],
        compiler_params=pltpu.CompilerParams(
            collective_id=4, has_side_effects=True, vmem_limit_bytes=VMEM_BYTES
        ),
        cost_estimate=pl.CostEstimate(
            flops=2 * rows * D * 4 * D, bytes_accessed=50 * 1024 * 1024, transcendentals=rows
        ),
    )(
        x_cont,
        x_prompt,
        grad_rows,
        attended,
        dq_rows,
        dk_own,
        dv_own,
        prompt_share,
        attn_in,
        mlp_out,
        d_mlp_in,
        qkv_slots,
        out_slots,
        picked,
        mid_qkv,
        d_mid_out,
        back_grads,
        id_tiles,
        frozen_bias[None],
        norm_gain,
    )


def update_kernel(
    sums_ref,
    norm_ref,
    sets_ref,
    first_ref,
    second_ref,
    rate_ref,
    cont_out_ref,
    cont_grad_ref,
    prompt_out_ref,
    prompt_grad_ref,
    new_sets,
    new_first,
    new_second,
    low_sets,
    cont_out,
    cont_grad,
    prompt_out,
    prompt_grad,
    norm_out,
):
    cont_out[...] = cont_out_ref[...]
    cont_grad[...] = cont_grad_ref[...]
    prompt_out[...] = prompt_out_ref[...]
    prompt_grad[...] = prompt_grad_ref[...]
    norm_out[0] = norm_ref[0, 0]
    limit = 0.1 * math.sqrt(SETS * R * WTOT)
    norm = norm_ref[0:1, 0:1]
    ratio = limit / jnp.maximum(norm, limit)
    rate = rate_ref[...]
    for index in range(sets_ref.shape[0]):
        clipped = sums_ref[0, index].astype(jnp.float32) * ratio
        first = beta_one * first_ref[index] + (1.0 - beta_one) * clipped
        second = beta_two * second_ref[index] + (1.0 - beta_two) * clipped * clipped
        corrected_first = first / (1.0 - beta_one**STEP)
        corrected_second = second / (1.0 - beta_two**STEP)
        old = sets_ref[index]
        new = old - rate * (
            corrected_first / (jnp.sqrt(corrected_second) + adam_eps) + weight_decay * old
        )
        new_first[index] = first
        new_second[index] = second
        new_sets[index] = new
        low_sets[index] = new.astype(jnp.bfloat16)


def update(sums, norm, adapters, first_moment, second_moment, rows_out):
    places, owned, _, width = sums.shape
    rates = np.where(up_columns(), rate_up, rate_down).astype(np.float32)[None]
    length, prompt_rows = rows_out[0].shape[0], rows_out[2].shape[0]

    def columns():
        return pl.BlockSpec((owned, R, width), lambda place: (0, 0, place))

    def shaped(kind):
        return jax.ShapeDtypeStruct(adapters.shape, kind)

    moving = [pl.BlockSpec((length // places, D), lambda place: (place, 0))] * 2
    moving += [pl.BlockSpec((prompt_rows, D), lambda place: (0, 0))] * 2
    return pl.pallas_call(
        update_kernel,
        grid=(places,),
        in_specs=[
            pl.BlockSpec((1, owned, R, width), lambda place: (place, 0, 0, 0)),
            pl.BlockSpec((8, 2 * HD), lambda place: (0, 0)),
            columns(),
            columns(),
            columns(),
            pl.BlockSpec((1, width), lambda place: (0, place)),
        ]
        + moving,
        out_specs=[columns()] * 4 + moving + [pl.BlockSpec(memory_space=pltpu.SMEM)],
        out_shape=[shaped(jnp.float32)] * 3
        + [shaped(jnp.bfloat16)]
        + [jax.ShapeDtypeStruct(row.shape, jnp.float32) for row in rows_out]
        + [jax.ShapeDtypeStruct((1,), jnp.float32)],
        compiler_params=pltpu.CompilerParams(vmem_limit_bytes=VMEM_BYTES),
    )(sums, norm, adapters, first_moment, second_moment, rates, *rows_out)


def per_device(
    x_prompt,
    x_cont,
    dy_prompt,
    dy_cont,
    adapter_ids,
    w_qkv,
    w_out,
    w_up,
    w_down,
    frozen_bias,
    norm_gain,
    norm_shift,
    adapters,
    first_moment,
    second_moment,
):
    length = x_cont.shape[1]
    (
        qkv,
        attn_in,
        mlp_in,
        d_attended,
        grad_rows,
        qkv_slots,
        out_slots,
        low_sets,
        picked,
        mid_qkv,
        d_mid_out,
    ) = front(
        adapter_ids,
        x_cont[0],
        x_prompt,
        dy_cont[0],
        dy_prompt,
        w_qkv,
        w_out,
        adapters,
        frozen_bias[None],
        norm_gain,
        norm_shift,
    )
    attended, dq_rows, dk_own, dv_own, kv_prompt, up_slots, down_slots, chosen = attention(
        adapter_ids, qkv, d_attended, w_up, w_down, low_sets, length
    )
    mlp_out, d_mlp_in, back_grads, prompt_share, id_tiles = mlp(
        mlp_in,
        grad_rows,
        up_slots,
        down_slots,
        chosen,
        frozen_bias,
        kv_prompt,
        w_down,
        adapter_ids,
        length,
    )
    cont_out, prompt_out, cont_grad, prompt_grad, sums, norm = tail(
        x_cont[0],
        x_prompt,
        grad_rows,
        attended,
        dq_rows,
        dk_own,
        dv_own,
        prompt_share,
        attn_in,
        mlp_out,
        d_mlp_in,
        qkv_slots,
        out_slots,
        picked,
        mid_qkv,
        d_mid_out,
        back_grads,
        id_tiles,
        frozen_bias,
        norm_gain,
        adapters.shape[0],
    )
    new_sets, new_first, new_second, low_new, cont_out, cont_grad, prompt_out, prompt_grad, norm = (
        update(
            sums,
            norm,
            adapters,
            first_moment,
            second_moment,
            (cont_out, cont_grad, prompt_out, prompt_grad),
        )
    )
    return (
        prompt_out,
        prompt_grad,
        cont_out[None],
        cont_grad[None],
        norm.reshape(()),
        new_sets,
        new_first,
        new_second,
        low_new,
    )


def solution(mesh):
    in_specs = (
        P("ctx", None),
        P(("ctx", "fsdp"), None, None),
        P("ctx", None),
        P(("ctx", "fsdp"), None, None),
        P(("ctx", "fsdp")),
        P(None, "fsdp"),
        P(None, "fsdp"),
        P(None, "fsdp"),
        P(None, "fsdp"),
        P(),
        P(),
        P(),
        P("fsdp", None, None),
        P("fsdp", None, None),
        P("fsdp", None, None),
    )
    out_specs = (
        P("ctx", None),
        P("ctx", None),
        P(("ctx", "fsdp"), None, None),
        P(("ctx", "fsdp"), None, None),
        P(),
        P("fsdp", None, None),
        P("fsdp", None, None),
        P("fsdp", None, None),
        P("fsdp", None, None),
    )
    return jax.shard_map(
        per_device, mesh=mesh, in_specs=in_specs, out_specs=out_specs, check_vma=False
    )
```

```python
import functools
import math

import jax
import jax.numpy as jnp
import numpy as np
from jax import lax
from jax.experimental import pallas as pl
from jax.experimental.pallas import tpu as pltpu
from jax.sharding import PartitionSpec as P

D = 1024
H = 16
HD = 64
ROT = 16
FF = 4096
R = 16
SETS = 8
STEP = 10
WTOT = 16384


beta_one = 0.9
beta_two = 0.999
adam_eps = 1e-08
weight_decay = 0.01
rate_down = 0.05
rate_up = 0.5
masked_score = -1e30
KEY_TILE = 256
QUERY_TILE = 256
SPAN = 768
PIECE = 64
LINES = 32
MLP_ROWS = 272
ROW_TILE = 512
OUT_TILE = 272
VMEM_BYTES = 62 * 1024 * 1024


def matmul(left, right):
    return jnp.dot(left, right, preferred_element_type=jnp.float32)


def matmul_bt(left, right):
    return lax.dot_general(
        left, right, (((1,), (1,)), ((), ())), preferred_element_type=jnp.float32
    )


def matmul_at(left, right):
    return lax.dot_general(
        left, right, (((0,), (0,)), ((), ())), preferred_element_type=jnp.float32
    )


def up_columns():
    column = np.arange(WTOT)
    return (
        (column >= D) & (column < 4 * D)
        | (column >= 5 * D) & (column < 6 * D)
        | (column >= 7 * D) & (column < 7 * D + FF)
        | (column >= 7 * D + 2 * FF)
    )


def pair_turn(values, cosine, low_sine, high_sine):
    return (
        values * cosine
        + pltpu.roll(values, 2 * HD - ROT // 2, 1) * low_sine
        + pltpu.roll(values, ROT // 2, 1) * high_sine
    )


def pair_turn_back(values, cosine, low_sine, high_sine):
    return (
        values * cosine
        - pltpu.roll(values, 2 * HD - ROT // 2, 1) * low_sine
        - pltpu.roll(values, ROT // 2, 1) * high_sine
    )


MESH = pl.DeviceIdType.MESH


def flip(place, mask):
    bit = 1
    while bit <= mask:
        if mask & bit:
            place = place + bit - 2 * bit * ((place // bit) % 2)
        bit *= 2
    return place


class Relay:
    def __init__(self, count):
        bits = [1 << index for index in range(count.bit_length() - 1)]
        self.count = count
        self.orders = (bits, bits[1:] + bits[:1])
        self.masks = []
        for order in self.orders:
            masks = [0]
            for bit in order:
                masks += [mask ^ bit for mask in masks]
            self.masks.append(masks)
        self.levels = [
            [held for held in range(1, count) if bin(held).count("1") == level]
            for level in range(1, count.bit_length())
        ]
        self.ctx, self.me = lax.axis_index("ctx"), lax.axis_index("fsdp")
        self.parity = self.ctx % 2
        self.sibling = self.ctx + 1 - 2 * self.parity

    def blend(self, even, odd, other):
        side = 1 - self.parity if other else self.parity
        return even + side * (odd - even)

    def partner(self, turn, stage):
        even, odd = (flip(self.me, self.orders[order][stage]) for order in (turn, 1 - turn))
        return self.blend(even, odd, False)

    def slot(self, turn, held, other=False):
        even, odd = (flip(self.me, self.masks[order][held]) for order in (turn, 1 - turn))
        return self.blend(even, odd, other)

    def greet(self, others=()):
        barrier = pltpu.get_barrier_semaphore()
        peers = [(self.ctx, flip(self.me, bit)) for bit in self.orders[0]]
        peers += [(self.sibling, self.me)] + list(others)
        for peer in peers:
            pl.semaphore_signal(barrier, inc=1, device_id=peer, device_id_type=MESH)
        pl.semaphore_wait(barrier, len(peers))


class Gathered:
    def __init__(self, relay, shard, slots, cut, sems, resident=False):
        self.resident = resident
        self.relay, self.shard, self.slots, self.cut = relay, shard, slots, cut
        self.send_sems, self.recv_sems, self.give_sems, self.take_sems, self.own_sem = sems

    def part(self, slot, turn, parity):
        return self.cut(self.slots.at[slot], 2 * parity + turn)

    def own(self):
        return pltpu.make_async_copy(self.shard, self.slots.at[self.relay.me], self.own_sem)

    def remote(self, source, target, sems, turn, held, device):
        index = turn * (self.relay.count - 1) + held - 1
        return pltpu.make_async_remote_copy(
            src_ref=source,
            dst_ref=target,
            send_sem=sems[0].at[index],
            recv_sem=sems[1].at[index],
            device_id=device,
            device_id_type=MESH,
        )

    def message(self, turn, held):
        relay = self.relay
        stage = held.bit_length() - 1
        before = held - (1 << stage)
        target = self.part(relay.slot(turn, before), turn, relay.parity)
        outside = before == 0 and not self.resident
        source = self.cut(self.shard, 2 * relay.parity + turn) if outside else target
        device = (relay.ctx, relay.partner(turn, stage))
        return self.remote(source, target, (self.send_sems, self.recv_sems), turn, held, device)

    def arrival(self, turn, held):
        relay = self.relay
        part = self.part(relay.slot(turn, held), turn, relay.parity)
        device = (relay.ctx, relay.partner(turn, held.bit_length() - 1))
        return self.remote(part, part, (self.send_sems, self.recv_sems), turn, held, device)

    def gift(self, turn, held, taken=False):
        relay = self.relay
        side = 1 - relay.parity if taken else relay.parity
        part = self.part(relay.slot(turn, held, taken), turn, side)
        device = (relay.sibling, relay.me)
        return self.remote(part, part, (self.give_sems, self.take_sems), turn, held, device)

    def start(self):
        if self.resident:
            self.own().wait()
        for held in self.relay.levels[0]:
            for turn in range(2):
                self.message(turn, held).start()
        if not self.resident:
            self.own().start()

    def forward(self, level):
        for held in self.relay.levels[level]:
            for turn in range(2):
                self.arrival(turn, held).wait_recv()
                for stage in range(held.bit_length(), len(self.relay.orders[0])):
                    self.message(turn, (1 << stage) + held).start()

    def give(self, level):
        for held in self.relay.levels[level]:
            for turn in range(2):
                self.gift(turn, held).start()

    def advance(self, level):
        self.forward(level)
        self.give(level)

    def places(self, level):
        masks = [mask for mask in range(self.relay.count) if bin(mask).count("1") == level + 1]
        return [flip(self.relay.me, mask) for mask in masks]

    def take(self, level):
        for held in self.relay.levels[level]:
            for turn in range(2):
                self.gift(turn, held, taken=True).wait_recv()

    def finish(self):
        for held in range(1, self.relay.count):
            for turn in range(2):
                self.message(turn, held).wait_send()
                self.gift(turn, held).wait_send()


def relay_sems(arrays, count):
    return [pltpu.SemaphoreType.DMA((arrays, 2 * (count - 1))) for _ in range(4)] + [
        pltpu.SemaphoreType.DMA((arrays,))
    ]


def sems_of(sems, index):
    return [sem.at[index] for sem in sems]


def row_quarter(ref, index):
    size = ref.shape[0] // 4
    return ref.at[pl.ds(pl.multiple_of(index * size, size), size)]


def lane_quarter(ref, index):
    size = ref.shape[-1] // 4
    return ref.at[:, :, pl.ds(pl.multiple_of(index * size, size), size)]


def remote_copy(source, target, sems, index, device):
    return pltpu.make_async_remote_copy(
        src_ref=source,
        dst_ref=target,
        send_sem=sems[0].at[index],
        recv_sem=sems[1].at[index],
        device_id=device,
        device_id_type=MESH,
    )


def greet_all(peers):
    barrier = pltpu.get_barrier_semaphore()
    for peer in peers:
        pl.semaphore_signal(barrier, inc=1, device_id=peer, device_id_type=MESH)
    pl.semaphore_wait(barrier, len(peers))


class Trade:
    def __init__(self, axis, count, source, slots, sems):
        self.axis, self.count, self.source, self.slots = axis, count, source, slots
        self.places = {name: lax.axis_index(name) for name in ("ctx", "fsdp")}
        self.me = self.places[axis]
        self.sems = sems

    def device(self, place):
        return tuple(place if name == self.axis else self.places[name] for name in self.places)

    def send(self, offset):
        place = flip(self.me, offset)
        return remote_copy(
            self.source(place), self.slots.at[self.me], self.sems, offset - 1, self.device(place)
        )

    def start(self):
        for offset in reversed(range(1, self.count)):
            self.send(offset).start()

    def wait(self):
        for offset in reversed(range(1, self.count)):
            place = flip(self.me, offset)
            part = self.slots.at[place]
            remote_copy(part, part, self.sems, offset - 1, self.device(place)).wait_recv()

    def finish(self):
        for offset in range(1, self.count):
            self.send(offset).wait_send()


def trade_sems(count):
    return [pltpu.SemaphoreType.DMA((count - 1,)) for _ in range(2)]


def together(main, main_count, side, side_count):
    done = 0
    for index in range(main_count):
        next(main, None)
        while done < (index + 1) * side_count // main_count:
            next(side, None)
            done += 1
    for generator in (main, side):
        for _ in generator:
            pass


def chain(*generators):
    for generator in generators:
        yield from generator


def front_kernel(
    length,
    ids_ref,
    x_ref,
    xp_ref,
    dy_ref,
    dyp_ref,
    wq_ref,
    wo_ref,
    sets_ref,
    bias_ref,
    gain_ref,
    shift_ref,
    cos_ref,
    low_ref,
    high_ref,
    qkv_out,
    a1_out,
    a2_out,
    dob_out,
    g_out,
    wq_out,
    wo_out,
    low_out,
    picked,
    mid_ref,
    d_mid_ref,
    wq,
    wo,
    ad,
    sets,
    low_sets,
    xp,
    a1,
    a2,
    g,
    qkv,
    dob,
    mid_keys,
    *sems,
):
    wq_sems, wo_sems, ad_sems = (sems_of(sems[:5], index) for index in range(3))
    xp_send, xp_recv, xp_give, xp_take, load_sems, store_sems, column_sems = sems[5:]
    slots, _, share = wq.shape
    chunk = math.gcd(share, 256)
    per = share // chunk
    owned = ad.shape[1]
    prompt_rows = xp_ref.shape[0]
    prompt_total = xp.shape[0]
    keys = a1.shape[0]
    rows = g.shape[0]
    relay = Relay(slots)
    ctx, parity = relay.ctx, relay.parity
    lines = prompt_total // prompt_rows // 2
    line = ctx // 2

    def line_place(offset, side):
        return flip(line, offset) * 2 + side

    def prompt_piece(place):
        return xp.at[pl.ds(pl.multiple_of(place * prompt_rows, prompt_rows), prompt_rows)]

    loads = [
        pltpu.make_async_copy(x_ref, dob.at[pl.ds(0, length)], load_sems.at[0]),
        pltpu.make_async_copy(dy_ref, g.at[pl.ds(0, length)], load_sems.at[1]),
        pltpu.make_async_copy(dyp_ref, g.at[pl.ds(length, prompt_rows)], load_sems.at[2]),
        pltpu.make_async_copy(xp_ref, prompt_piece(ctx), load_sems.at[3]),
        pltpu.make_async_copy(sets_ref, sets, load_sems.at[4]),
    ]
    for load in reversed(loads):
        load.start()

    adapters = Gathered(relay, low_sets.at[:, :, pl.ds(0, 6 * D)], ad, lane_quarter, ad_sems)
    qkv_weights = Gathered(relay, wq_ref, wq, row_quarter, wq_sems, True)
    out_weights = Gathered(relay, wo_ref, wo, row_quarter, wo_sems, True)
    qkv_weights.own().start()
    out_weights.own().start()
    loads[4].wait()
    for index in range(owned):
        low_sets[index] = sets[index].astype(jnp.bfloat16)
    relay.greet([(line_place(step, parity), relay.me) for step in range(1, lines)])
    adapters.start()
    qkv_weights.start()

    def prompt_send(step):
        return pltpu.make_async_remote_copy(
            src_ref=xp_ref,
            dst_ref=prompt_piece(ctx),
            send_sem=xp_send.at[step],
            recv_sem=xp_recv.at[step],
            device_id=(line_place(step, parity), relay.me),
            device_id_type=MESH,
        )

    def prompt_landed(step):
        piece = prompt_piece(line_place(step, parity))
        return pltpu.make_async_remote_copy(
            src_ref=piece,
            dst_ref=piece,
            send_sem=xp_send.at[step],
            recv_sem=xp_recv.at[step],
            device_id=(line_place(step, parity), relay.me),
            device_id_type=MESH,
        )

    def prompt_gift(step, taken):
        piece = prompt_piece(line_place(step, 1 - parity if taken else parity))
        return pltpu.make_async_remote_copy(
            src_ref=xp_ref if step == 0 and not taken else piece,
            dst_ref=piece,
            send_sem=xp_give.at[step],
            recv_sem=xp_take.at[step],
            device_id=(relay.sibling, relay.me),
            device_id_type=MESH,
        )

    for step in reversed(range(1, lines)):
        prompt_send(step).start()
    prompt_gift(0, False).start()

    def unit_rows(values):
        values = values.astype(jnp.float32)
        centered = values - jnp.mean(values, axis=-1, keepdims=True)
        variance = jnp.mean(centered * centered, axis=-1, keepdims=True)
        return centered * lax.rsqrt(variance + 1e-05)

    loads[0].wait()
    tile = ROW_TILE

    @pl.loop(0, length // LINES)
    def _(index):
        start = pl.multiple_of(index * LINES, LINES)
        unit = unit_rows(dob[pl.ds(start, LINES), :])
        a1[pl.ds(prompt_total + start, LINES), :] = (
            unit * gain_ref[0:1, :] + shift_ref[0:1, :]
        ).astype(jnp.bfloat16)
        a2[pl.ds(start, LINES), :] = (unit * gain_ref[1:2, :] + shift_ref[1:2, :]).astype(
            jnp.bfloat16
        )

    loads[3].wait()
    unit = unit_rows(prompt_piece(ctx)[...])
    a2[pl.ds(length, prompt_rows), :] = (unit * gain_ref[1:2, :] + shift_ref[1:2, :]).astype(
        jnp.bfloat16
    )
    loads[1].wait()
    loads[2].wait()
    stores = [
        pltpu.make_async_copy(a2, a2_out, store_sems.at[0]),
        pltpu.make_async_copy(g, g_out, store_sems.at[1]),
        pltpu.make_async_copy(low_sets, low_out, store_sems.at[6]),
    ]
    for store in stores:
        store.start()

    last = len(relay.levels) - 1
    for level in range(last + 1):
        adapters.advance(level)
    qkv_weights.advance(0)
    out_weights.start()
    for step in reversed(range(1, lines)):
        prompt_landed(step).wait_recv()
        prompt_gift(step, False).start()
    adapters.own().wait()
    for level in range(last + 1):
        adapters.take(level)
    mine = ids_ref[0]
    picked[...] = ad[mine // owned, mine % owned]

    mid_keys[pl.ds(0, prompt_total), :] = jnp.zeros((prompt_total, R), jnp.bfloat16)
    d_mid_ref[pl.ds(length, prompt_rows), :] = jnp.zeros((prompt_rows, R), jnp.bfloat16)
    for start in range(0, length, tile):
        at, key_at = pl.ds(start, tile), pl.ds(prompt_total + start, tile)
        middle = matmul_bt(a1[key_at, :], picked[:, :D]).astype(jnp.bfloat16)
        mid_keys[key_at, :] = middle
        mid_ref[at, :] = middle
        d_mid_ref[at, :] = matmul_bt(g[at, :], picked[:, 5 * D : 6 * D]).astype(jnp.bfloat16)
    for step in range(lines):
        prompt_gift(step, True).wait_recv()

    @pl.loop(0, prompt_total // LINES)
    def _(index):
        at = pl.ds(pl.multiple_of(index * LINES, LINES), LINES)
        a1[at, :] = (unit_rows(xp[at, :]) * gain_ref[0:1, :] + shift_ref[0:1, :]).astype(
            jnp.bfloat16
        )

    stores.append(pltpu.make_async_copy(a1, a1_out, store_sems.at[2]))
    stores[-1].start()

    columns = []

    def project(slot):
        for index in range(per):
            col = pl.multiple_of(slot * share + index * chunk, chunk)
            turned = col < 2 * D
            scale = jnp.where(col < D, HD ** (-0.5), 1.0)
            weights = wq[slot, :, index * chunk : (index + 1) * chunk]
            b_part = picked[:, pl.ds(pl.multiple_of(col + D, chunk), chunk)]
            bias = bias_ref[:, pl.ds(col, chunk)]
            for start in range(0, keys, tile):
                at = pl.ds(start, tile)
                result = matmul(a1[at, :], weights) + matmul(mid_keys[at, :], b_part) + bias
                for row in range(0, tile, 128):
                    row_at = pl.ds(start + row, 128)
                    cosine = jnp.where(turned, cos_ref[row_at, :], 1.0)
                    low_sine = jnp.where(turned, low_ref[row_at, :], 0.0)
                    high_sine = jnp.where(turned, high_ref[row_at, :], 0.0)
                    for lane in range(0, chunk, 2 * HD):
                        part = pair_turn(
                            result[row : row + 128, lane : lane + 2 * HD],
                            cosine,
                            low_sine,
                            high_sine,
                        )
                        lane_at = pl.ds(pl.multiple_of(col + lane, 2 * HD), 2 * HD)
                        qkv[row_at, lane_at] = (part * scale).astype(jnp.bfloat16)
            column_at = pl.ds(col, chunk)
            copy = pltpu.make_async_copy(
                qkv.at[:, column_at], qkv_out.at[:, column_at], column_sems.at[len(columns)]
            )
            copy.start()
            columns.append(copy)

    project(relay.me)
    for level in range(last + 1):
        if level < last:
            qkv_weights.advance(level + 1)
        else:
            out_weights.advance(0)
        qkv_weights.take(level)
        for mask in range(1, slots):
            if bin(mask).count("1") == level + 1:
                project(flip(relay.me, mask))
    stores.append(pltpu.make_async_copy(wq, wq_out, store_sems.at[3]))
    stores[-1].start()

    for level in range(1, last + 1):
        out_weights.advance(level)
    for level in range(last + 1):
        out_weights.take(level)
    stores.append(pltpu.make_async_copy(wo, wo_out, store_sems.at[4]))
    stores[-1].start()
    out_share = wo.shape[2]
    for start in range(0, rows, OUT_TILE):
        at = pl.ds(start, min(OUT_TILE, rows - start))
        total = matmul(d_mid_ref[at, :], picked[:, 4 * D : 5 * D])
        for slot in range(slots):
            total += matmul_bt(g[at, pl.ds(slot * out_share, out_share)], wo[slot])
        dob[at, :] = total.astype(jnp.bfloat16)
    stores.append(pltpu.make_async_copy(dob, dob_out, store_sems.at[5]))
    stores[-1].start()

    for array in (adapters, qkv_weights, out_weights):
        array.finish()
    for step in range(1, lines):
        prompt_send(step).wait_send()
    for step in range(lines):
        prompt_gift(step, False).wait_send()
    for copy in columns + stores:
        copy.wait()


def front(ids, x_cont, x_prompt, dy_cont, dy_prompt, w_qkv, w_out, adapters, bias, gain, shift):
    slots = lax.axis_size("fsdp")
    places = lax.axis_size("ctx")
    length, prompt_rows = x_cont.shape[0], x_prompt.shape[0]
    rows, prompt_total = length + prompt_rows, prompt_rows * places
    keys = prompt_total + length
    share, out_share = w_qkv.shape[1], w_out.shape[1]
    owned, wide = adapters.shape[0], 6 * D
    columns = slots * (share // math.gcd(share, 256))
    low = jnp.bfloat16
    anywhere = pl.BlockSpec(memory_space=pl.ANY)
    on_chip = pl.BlockSpec(memory_space=pltpu.VMEM)
    return pl.pallas_call(
        functools.partial(front_kernel, length),
        in_specs=[pl.BlockSpec(memory_space=pltpu.SMEM)] + [anywhere] * 7 + [on_chip] * 6,
        out_specs=[anywhere] * 8 + [on_chip] * 3,
        out_shape=[
            jax.ShapeDtypeStruct((keys, 3 * D), low),
            jax.ShapeDtypeStruct((keys, D), low),
            jax.ShapeDtypeStruct((rows, D), low),
            jax.ShapeDtypeStruct((rows, D), low),
            jax.ShapeDtypeStruct((rows, D), low),
            jax.ShapeDtypeStruct((slots, D, share), low),
            jax.ShapeDtypeStruct((slots, D, out_share), low),
            jax.ShapeDtypeStruct(adapters.shape, low),
            jax.ShapeDtypeStruct((R, wide), low),
            jax.ShapeDtypeStruct((length, R), low),
            jax.ShapeDtypeStruct((rows, R), low),
        ],
        scratch_shapes=[
            pltpu.VMEM((slots, D, share), low),
            pltpu.VMEM((slots, D, out_share), low),
            pltpu.VMEM((slots, owned, R, wide), low),
            pltpu.VMEM(adapters.shape, jnp.float32),
            pltpu.VMEM(adapters.shape, low),
            pltpu.VMEM((prompt_total, D), low),
            pltpu.VMEM((keys, D), low),
            pltpu.VMEM((rows, D), low),
            pltpu.VMEM((rows, D), low),
            pltpu.VMEM((keys, 3 * D), low),
            pltpu.VMEM((rows, D), low),
            pltpu.VMEM((keys, R), low),
        ]
        + relay_sems(3, slots)
        + [pltpu.SemaphoreType.DMA((places // 2,)) for _ in range(4)]
        + [
            pltpu.SemaphoreType.DMA((5,)),
            pltpu.SemaphoreType.DMA((7,)),
            pltpu.SemaphoreType.DMA((columns,)),
        ],
        compiler_params=pltpu.CompilerParams(
            collective_id=1, has_side_effects=True, vmem_limit_bytes=VMEM_BYTES
        ),
        cost_estimate=pl.CostEstimate(
            flops=2 * keys * D * 3 * D + 2 * rows * D * D,
            bytes_accessed=50 * 1024 * 1024,
            transcendentals=rows,
        ),
    )(
        ids,
        x_cont,
        x_prompt,
        dy_cont,
        dy_prompt,
        w_qkv,
        w_out,
        adapters,
        bias,
        gain,
        shift,
        *turn_tables(keys),
    )


def attention_kernel(
    length,
    prompt_total,
    prompt_rows,
    ids_ref,
    q_ref,
    k_ref,
    v_ref,
    do_ref,
    cos_ref,
    low_ref,
    high_ref,
    up_ref,
    down_ref,
    ad_ref,
    o_ref,
    dq_ref,
    dk_ref,
    dv_ref,
    kvp_ref,
    up_out,
    down_out,
    chosen_ref,
    ad_slots,
    up_slots,
    down_slots,
    queries_ref,
    keys_ref,
    values_ref,
    outer_ref,
    keys_t_ref,
    values_t_ref,
    dk_sum,
    dv_sum,
    *sems,
):
    score_scale = HD ** (-0.5)
    key_count = prompt_total + length
    tile = KEY_TILE
    piece_rows = PIECE
    step = pl.program_id(0)
    last_step = H // 2 - 1
    relay = Relay(up_out.shape[0])
    ctx_place = relay.ctx
    first_member = jnp.where(relay.me == 0, 1.0, 0.0)
    back_sets = ad_ref.at[:, :, pl.ds(6 * D, WTOT - 6 * D)]
    resident = len(up_slots.shape) > 2
    if not resident:
        up_slots, down_slots = up_out, down_out
    adapters = Gathered(relay, back_sets, ad_slots, lane_quarter, sems_of(sems[:5], 0), True)
    up_weights = Gathered(relay, up_ref, up_slots, row_quarter, sems_of(sems[:5], 1), resident)
    early = down_ref.at[pl.ds(0, down_slots.shape[1])]
    down_weights = Gathered(relay, early, down_slots, row_quarter, sems_of(sems[:5], 2), resident)
    arrays = (adapters, up_weights, down_weights)
    store_sems = sems[5]
    levels = len(relay.levels)

    def stores(level):
        if not resident:
            return []
        return [
            pltpu.make_async_copy(array.slots.at[place], out.at[place], store_sems.at[index, place])
            for index, (array, out) in enumerate(((up_weights, up_out), (down_weights, down_out)))
            for place in up_weights.places(level)
        ]

    def store(level):
        for copy in stores(level):
            copy.start()

    late = []

    def at_step(when, action):
        if when > last_step:
            late.append((when, action))
        else:
            pl.when(step == when)(action)

    def begin():
        for array in arrays:
            if array.resident:
                array.own().start()
        relay.greet()
        for array in arrays:
            array.start()

    def settle(level):
        for array in arrays:
            array.take(level)
        store(level)

    def first_arrays(level):
        for array in arrays[:2]:
            array.forward(level)
        for array in arrays[:2]:
            array.give(level)

    at_step(0, begin)
    at_step(2, functools.partial(store, -1))
    for level in range(levels):
        at_step(3 + 3 * level, functools.partial(first_arrays, level))
        at_step(5 + 2 * level, functools.partial(down_weights.advance, level))
    for level in range(levels):
        at_step(7 if level < levels - 1 else 20, functools.partial(settle, level))

    wide, low = jnp.float32, jnp.bfloat16
    for start in range(0, key_count, tile):
        at = pl.ds(start, tile)
        queries_ref[at, :] = q_ref[at, :].astype(wide).astype(low)
        piece = k_ref[at, :].astype(wide)
        keys_ref[at, :] = piece.astype(low)
        keys_t_ref[:, at] = piece.T.astype(low)
        piece = v_ref[at, :].astype(wide)
        values_ref[at, :] = piece.astype(low)
        values_t_ref[:, at] = piece.T.astype(low)
    outer_ref[...] = do_ref[...].astype(wide).astype(low)

    class Unit:
        def __init__(self, row_start, rows, position_at, last_key, first, weight, head):
            self.at, self.position_at, self.rows = pl.ds(row_start, rows), position_at, rows
            self.head, self.weight, self.first = head, weight, first
            self.first_row = prompt_total + row_start
            if weight is not None:
                self.first_row = ctx_place * prompt_rows
            self.unmasked = 0 if weight is not None else prompt_total + row_start
            tiles = last_key // tile
            count = -(-last_key // SPAN)
            edges = [tile * (tiles * index // count) for index in range(count + 1)]
            self.spans = list(zip(edges[:-1], edges[1:]))
            self.tiles = range(0, last_key, piece_rows)
            self.scores, self.d_probs, self.raised, self.rounded, self.slopes = {}, {}, {}, {}, {}
            self.top = None

        def enter(self):
            lane = lax.broadcasted_iota(jnp.int32, (self.rows, 2 * HD), 1)
            mine = (lane >= self.head * HD) & (lane < (self.head + 1) * HD)
            queries, cotangent = queries_ref[self.position_at, :], outer_ref[self.at, :]
            self.q_head = jnp.where(mine, queries, jnp.zeros_like(queries))
            self.do_head = jnp.where(mine, cotangent, jnp.zeros_like(cotangent))
            for low_edge, high_edge in self.spans:
                at = pl.ds(low_edge, high_edge - low_edge)
                whole = matmul_bt(keys_ref[at, :], self.q_head)
                for start in range(low_edge, high_edge, piece_rows):
                    piece = whole[start - low_edge : start - low_edge + piece_rows]
                    if start + piece_rows > self.unmasked:
                        key_at = start + lax.broadcasted_iota(jnp.int32, piece.shape, 0)
                        row_at = lax.broadcasted_iota(jnp.int32, piece.shape, 1)
                        piece = jnp.where(key_at <= self.first_row + row_at, piece, masked_score)
                    self.scores[start] = piece
                    self.top = piece if self.top is None else jnp.maximum(self.top, piece)
                yield
                whole = matmul_bt(values_ref[at, :], self.do_head)
                for start in range(low_edge, high_edge, piece_rows):
                    self.d_probs[start] = whole[start - low_edge : start - low_edge + piece_rows]
                yield

        def soften(self):
            top = jnp.max(self.top, axis=0, keepdims=True)
            total, delta = None, None
            for start in self.tiles:
                piece = jnp.exp(self.scores[start] - top)
                part = piece * self.d_probs[start]
                self.raised[start] = piece
                total = piece if total is None else total + piece
                delta = part if delta is None else delta + part
                yield
            inverse = 1.0 / jnp.sum(total, axis=0, keepdims=True)
            delta = jnp.sum(delta, axis=0, keepdims=True) * inverse
            for start in self.tiles:
                soft = self.raised[start] * inverse
                self.rounded[start] = soft.astype(low)
                self.slopes[start] = (soft * (self.d_probs[start] - delta)).astype(low)
                yield
            if self.weight is not None:
                self.q_head = (self.q_head.astype(wide) * self.weight).astype(low)
                self.do_head = (self.do_head.astype(wide) * self.weight).astype(low)

        def span_of(self, pieces, span):
            return jnp.concatenate([pieces[start] for start in range(*span, piece_rows)], axis=0)

        def leave(self, partner=None):
            head_at = pl.ds(self.head * HD, HD)
            self.out_t, self.dq_t = None, None
            for span in self.spans:
                at = pl.ds(span[0], span[1] - span[0])
                part = matmul(values_t_ref[head_at, at], self.span_of(self.rounded, span))
                self.out_t = part if self.out_t is None else self.out_t + part
                yield
                part = matmul(keys_t_ref[head_at, at], self.span_of(self.slopes, span))
                self.dq_t = part if self.dq_t is None else self.dq_t + part
                yield
            if partner is None:
                return
            both_do = jnp.concatenate([partner.do_head, self.do_head], axis=0)
            both_q = jnp.concatenate([partner.q_head, self.q_head], axis=0)
            for span in self.spans:
                at = pl.ds(span[0], span[1] - span[0])
                for total, name, right in (
                    (dv_sum, "rounded", both_do),
                    (dk_sum, "slopes", both_q),
                ):
                    left = [
                        unit.span_of(getattr(unit, name), span) for unit in (partner, self)
                    ]
                    part = matmul(jnp.concatenate(left, axis=1), right)
                    total[at, :] = part if self.first else total[at, :] + part
                    yield

    blocks = [
        (
            row_start,
            QUERY_TILE,
            pl.ds(prompt_total + row_start, QUERY_TILE),
            prompt_total + row_start + QUERY_TILE,
            None,
        )
        for row_start in reversed(range(0, length, QUERY_TILE))
    ]
    own_at = pl.ds(pl.multiple_of(ctx_place * prompt_rows, prompt_rows), prompt_rows)
    blocks.append((length, prompt_rows, own_at, prompt_total, first_member))
    units = []
    for index, (row_start, rows, position_at, last_key, weight) in enumerate(blocks):
        for head in range(2):
            first = index == 0
            units.append(Unit(row_start, rows, position_at, last_key, first, weight, head))

    def close(index):
        if index % 2 == 0:
            return
        pair = units[index - 1 : index + 1]
        at, position_at = pair[0].at, pair[0].position_at
        o_ref[at, :] = jnp.concatenate([unit.out_t for unit in pair], axis=0).T.astype(o_ref.dtype)
        d_queries = jnp.concatenate([unit.dq_t for unit in pair], axis=0).T * score_scale
        turn = [table[position_at, :] for table in (cos_ref, low_ref, high_ref)]
        dq_ref[at, :] = pair_turn_back(d_queries, *turn).astype(dq_ref.dtype)

    for _ in units[0].enter():
        pass
    def leaving(index):
        unit = units[index]
        partner = units[index - 1] if unit.head == 1 else None
        return unit.leave(partner), (4 if partner else 2) * len(unit.spans)

    for index, unit in enumerate(units):
        side, side_count = [], 0
        if index > 0:
            generator, count = leaving(index - 1)
            side.append(generator)
            side_count += count
        if index + 1 < len(units):
            side.append(units[index + 1].enter())
            side_count += 2 * len(units[index + 1].spans)
        together(unit.soften(), 2 * len(unit.tiles), chain(*side), side_count)
        if index > 0:
            close(index - 1)
    for _ in leaving(len(units) - 1)[0]:
        pass
    close(len(units) - 1)

    prompt_at = pl.ds(0, prompt_total)
    kvp_ref[0] = dk_sum[prompt_at, :].astype(kvp_ref.dtype)
    kvp_ref[1] = dv_sum[prompt_at, :].astype(kvp_ref.dtype)
    own_at = pl.ds(prompt_total, length)
    turned_back = pair_turn_back(
        dk_sum[own_at, :], cos_ref[own_at, :], low_ref[own_at, :], high_ref[own_at, :]
    )
    dk_ref[...] = turned_back.astype(dk_ref.dtype)
    dv_ref[...] = dv_sum[own_at, :].astype(dv_ref.dtype)

    @pl.when(step == last_step)
    def _():
        for _, action in sorted(late, key=lambda item: item[0]):
            action()
        for array in arrays:
            if not array.resident:
                array.own().wait()
            array.finish()
        for level in range(-1, levels):
            for copy in stores(level):
                copy.wait()
        mine, owned = ids_ref[0], ad_slots.shape[1]
        chosen_ref[...] = ad_slots[mine // owned, mine % owned]


def turn_tables(count):
    half_rot = ROT // 2
    place = np.arange(half_rot, dtype=np.float32)
    frequency = np.float32(10000.0) ** (np.float32(-2.0) * place / np.float32(ROT))
    angles = np.arange(count, dtype=np.float32)[:, None] * frequency[None, :]
    cosine, sine_part = np.cos(angles), np.sin(angles)
    rest = np.zeros((count, HD - ROT), np.float32)
    gap = np.zeros((count, half_rot), np.float32)

    def pair(parts):
        return np.concatenate(parts + parts, axis=1).astype(np.float32)

    return (
        pair([cosine, cosine, rest + 1.0]),
        pair([-sine_part, gap, rest]),
        pair([gap, sine_part, rest]),
    )


def attention(ids, qkv, d_attended, w_up, w_down, low_sets, length):
    slots = lax.axis_size("fsdp")
    row_count = d_attended.shape[0]
    prompt_rows = row_count - length
    key_count = qkv.shape[0]
    prompt_total = key_count - length
    wide = 2 * HD
    low = jnp.bfloat16
    resident = key_count <= 2048

    def column(rows, start=0):
        return pl.BlockSpec((rows, wide), lambda pair: (0, start // wide + pair))

    down_shape = (slots,) + w_down.shape
    table = pl.BlockSpec((key_count, wide), lambda pair: (0, 0))
    anywhere = pl.BlockSpec(memory_space=pl.ANY)
    area = row_count * key_count * 0.75
    return pl.pallas_call(
        functools.partial(attention_kernel, length, prompt_total, prompt_rows),
        grid=(H // 2,),
        in_specs=[
            pl.BlockSpec(memory_space=pltpu.SMEM),
            column(key_count),
            column(key_count, D),
            column(key_count, 2 * D),
            column(row_count),
            table,
            table,
            table,
            anywhere,
            anywhere,
            anywhere,
        ],
        out_specs=[
            column(row_count),
            column(row_count),
            column(length),
            column(length),
            pl.BlockSpec((2, prompt_total, wide), lambda pair: (0, 0, pair)),
            anywhere,
            anywhere,
            pl.BlockSpec((R, WTOT - 6 * D), lambda pair: (0, 0)),
        ],
        out_shape=[
            jax.ShapeDtypeStruct((row_count, D), low),
            jax.ShapeDtypeStruct((row_count, D), low),
            jax.ShapeDtypeStruct((length, D), low),
            jax.ShapeDtypeStruct((length, D), low),
            jax.ShapeDtypeStruct((2, prompt_total, D), low),
            jax.ShapeDtypeStruct((slots,) + w_up.shape, low),
            jax.ShapeDtypeStruct(down_shape, low),
            jax.ShapeDtypeStruct((R, WTOT - 6 * D), low),
        ],
        scratch_shapes=[
            pltpu.VMEM((slots,) + low_sets.shape[:2] + (WTOT - 6 * D,), low),
            pltpu.VMEM((slots,) + w_up.shape if resident else (16, 128), low),
            pltpu.VMEM(down_shape if resident else (16, 128), low),
            pltpu.VMEM((key_count, wide), low),
            pltpu.VMEM((key_count, wide), low),
            pltpu.VMEM((key_count, wide), low),
            pltpu.VMEM((row_count, wide), low),
            pltpu.VMEM((wide, key_count), low),
            pltpu.VMEM((wide, key_count), low),
            pltpu.VMEM((key_count, wide), jnp.float32),
            pltpu.VMEM((key_count, wide), jnp.float32),
        ]
        + relay_sems(3, slots)
        + [pltpu.SemaphoreType.DMA((2, slots))],
        compiler_params=pltpu.CompilerParams(
            collective_id=2, has_side_effects=True, vmem_limit_bytes=VMEM_BYTES
        ),
        cost_estimate=pl.CostEstimate(
            flops=int(12 * area * D), bytes_accessed=32 * 1024 * 1024, transcendentals=int(area * H)
        ),
    )(ids, qkv, qkv, qkv, d_attended, *turn_tables(key_count), w_up, w_down, low_sets)


def mlp_kernel(
    length,
    a_ref,
    g_ref,
    up_ref,
    down_ref,
    a_up_ref,
    b_up_ref,
    a_down_ref,
    b_down_ref,
    bias_ref,
    kvp_ref,
    ids_ref,
    cos_ref,
    low_ref,
    high_ref,
    out_ref,
    d_in_ref,
    grads_ref,
    share_ref,
    ids_out,
    mid_up,
    d_mid_down,
    mid_down_sum,
    d_mid_up_sum,
    first,
    first_sum,
    second,
    third,
    id_tiles,
    a,
    g,
    w_up,
    w_down,
    own_sem,
    load_sems,
    *sems,
):
    step = pl.program_id(0)
    last_step = pl.num_programs(0) - 1
    members, prompt_total, part = first.shape
    places, prompt_rows, _ = second.shape
    ctx, me = lax.axis_index("ctx"), lax.axis_index("fsdp")
    halves = members // 2

    def prompt_part(place):
        columns = pl.ds(pl.multiple_of((place % halves) * part, part), part)
        return kvp_ref.at[place // halves, :, columns]

    def owned_rows(place):
        return first_sum.at[pl.ds(pl.multiple_of(place * prompt_rows, prompt_rows), prompt_rows)]

    over_members = Trade("fsdp", members, prompt_part, first, sems[0:2])
    over_places = Trade("ctx", places, owned_rows, second, sems[2:4])
    to_members = Trade("fsdp", members, lambda place: third.at[me], third, sems[4:6])
    id_trade = Trade("ctx", places, lambda place: id_tiles.at[ctx], id_tiles, sems[6:8])
    own_part = pltpu.make_async_copy(prompt_part(me), first.at[me], own_sem)
    loads = [
        pltpu.make_async_copy(a_ref, a, load_sems.at[0]),
        pltpu.make_async_copy(g_ref, g, load_sems.at[1]),
    ]

    @pl.when(step == 0)
    def _():
        for load in loads:
            load.start()
        own_part.start()
        id_tiles[ctx] = jnp.full(id_tiles.shape[1:], ids_ref[0].astype(jnp.float32))
        greet_all(
            [(ctx, flip(me, offset)) for offset in range(1, members)]
            + [(flip(ctx, offset), me) for offset in range(1, places)]
        )
        over_members.start()
        id_trade.start()

    @pl.when(step == last_step // 2 + 1)
    def _():
        own_part.wait()
        over_members.wait()
        total = first[0].astype(jnp.float32)
        for member in range(1, members):
            total += first[member].astype(jnp.float32)
        first_sum[...] = total.astype(jnp.bfloat16)
        over_places.start()

    @pl.when(step == last_step - 1)
    def _():
        over_places.wait()
        second[ctx] = owned_rows(ctx)[...]
        total = second[0].astype(jnp.float32)
        for place in range(1, places):
            total += second[place].astype(jnp.float32)
        is_key = me < halves
        own_at = pl.ds(pl.multiple_of(ctx * prompt_rows, prompt_rows), prompt_rows)
        cosine = jnp.where(is_key, cos_ref[own_at, :], 1.0)
        low_sine = jnp.where(is_key, low_ref[own_at, :], 0.0)
        high_sine = jnp.where(is_key, high_ref[own_at, :], 0.0)
        for lane in range(0, part, 2 * HD):
            third[me, :, lane : lane + 2 * HD] = pair_turn_back(
                total[:, lane : lane + 2 * HD], cosine, low_sine, high_sine
            ).astype(jnp.bfloat16)
        to_members.start()

    rows = a.shape[0]
    slots, wide, share = down_ref.shape
    low = jnp.bfloat16
    chunk = min(256, wide)
    parts = range(0, wide, chunk)
    tiles = [pl.ds(start, min(MLP_ROWS, rows - start)) for start in range(0, rows, MLP_ROWS)]

    def masked(values):
        row = lax.broadcasted_iota(jnp.int32, values.shape, 0)
        return jnp.where(row < length, values, 0.0).astype(low)

    @pl.when(step == 0)
    def _():
        for load in loads:
            load.wait()
        mid_up[...] = masked(matmul_bt(a[...], a_up_ref[...]))
        d_mid_down[...] = masked(matmul_bt(g[...], b_down_ref[...]))
        mid_down_sum[...] = jnp.zeros_like(mid_down_sum)
        d_mid_up_sum[...] = jnp.zeros_like(d_mid_up_sum)
        out_ref[...] = jnp.zeros_like(out_ref)
        d_in_ref[...] = jnp.zeros_like(d_in_ref)

    w_up[...] = up_ref[0].astype(jnp.float32).astype(low)
    for slot in range(slots):
        piece = down_ref[slot].astype(jnp.float32).astype(low)
        w_down[:, slot * share : (slot + 1) * share] = piece
    b_up, a_down = b_up_ref[...], a_down_ref[...]
    bias = bias_ref[...]

    class Unit:
        def __init__(self, at):
            self.at = at
            self.up, self.d_hidden, self.hidden, self.d_up = [], [], [], []

        def enter(self):
            for start in parts:
                lanes = slice(start, start + chunk)
                up = matmul(a[self.at, :], w_up[:, lanes])
                self.up.append(up + matmul(mid_up[self.at, :], b_up[:, lanes]) + bias[:, lanes])
                yield
                d_hidden = matmul_bt(g[self.at, :], w_down[lanes, :])
                self.d_hidden.append(d_hidden + matmul(d_mid_down[self.at, :], a_down[:, lanes]))
                yield

        def bend(self):
            for up, d_hidden in zip(self.up, self.d_hidden):
                height = up.shape[0]
                edges = [0, height // 32 * 16 + height % 32, height]
                hidden, d_up = [], []
                for lane in range(0, chunk, 128):
                    hidden_rows, d_rows = [], []
                    for low_edge, high_edge in zip(edges[:-1], edges[1:]):
                        u = up[low_edge:high_edge, lane : lane + 128]
                        cdf = 0.5 + 0.5 * lax.erf(u * (0.5**0.5))
                        density = jnp.exp(-0.5 * (u * u)) * ((2.0 * math.pi) ** -0.5)
                        hidden_rows.append((u * cdf).astype(low))
                        d_piece = d_hidden[low_edge:high_edge, lane : lane + 128]
                        d_rows.append((d_piece * (cdf + u * density)).astype(low))
                        yield
                    hidden.append(jnp.concatenate(hidden_rows, axis=0))
                    d_up.append(jnp.concatenate(d_rows, axis=0))
                self.hidden.append(jnp.concatenate(hidden, axis=1))
                self.d_up.append(jnp.concatenate(d_up, axis=1))

        def leave(self):
            at = self.at
            for column in range(0, D, 256):
                lanes = slice(column, column + 256)
                total = out_ref[at, lanes]
                for start, hidden in zip(parts, self.hidden):
                    total += matmul(hidden, w_down[start : start + chunk, lanes])
                out_ref[at, lanes] = total
                yield
                total = d_in_ref[at, lanes]
                for start, d_up in zip(parts, self.d_up):
                    total += matmul_bt(d_up, w_up[lanes, start : start + chunk])
                d_in_ref[at, lanes] = total
                yield
            self.grads = []
            middle, d_middle = mid_down_sum[at, :], d_mid_up_sum[at, :]
            for start, hidden, d_up in zip(parts, self.hidden, self.d_up):
                middle += matmul_bt(hidden, a_down[:, start : start + chunk])
                d_middle += matmul_bt(d_up, b_up[:, start : start + chunk])
                self.grads.append(
                    (matmul_at(mid_up[at, :], d_up), matmul_at(d_mid_down[at, :], hidden))
                )
                yield
            mid_down_sum[at, :] = middle
            d_mid_up_sum[at, :] = d_middle

    units = [Unit(at) for at in tiles]
    enters, leaves, bends = 2 * len(parts), 8 + len(parts), 2 * len(parts) * (chunk // 128)
    for _ in units[0].enter():
        pass
    for index, unit in enumerate(units):
        side, side_count = [], 0
        if index > 0:
            side.append(units[index - 1].leave())
            side_count += leaves
        if index + 1 < len(units):
            side.append(units[index + 1].enter())
            side_count += enters
        together(unit.bend(), bends, chain(*side), side_count)
    for _ in units[-1].leave():
        pass
    grad_b_up = jnp.concatenate(
        [sum(unit.grads[index][0] for unit in units) for index in range(len(parts))], axis=1
    )
    grad_a_down = jnp.concatenate(
        [sum(unit.grads[index][1] for unit in units) for index in range(len(parts))], axis=1
    )
    for start, value in ((D, grad_b_up), (D + FF, grad_a_down)):
        columns = pl.ds(pl.multiple_of(start + step * wide, wide), wide)
        grads_ref[:, columns] = value.astype(jnp.bfloat16)

    @pl.when(step == last_step)
    def _():
        mid_down = masked(mid_down_sum[...])
        d_mid_up = masked(d_mid_up_sum[...])
        out_ref[...] += matmul(mid_down, b_down_ref[...])
        d_in_ref[...] += matmul(d_mid_up, a_up_ref[...])
        grads_ref[:, :D] = matmul_at(d_mid_up, a[...]).astype(jnp.bfloat16)
        grads_ref[:, D + 2 * FF :] = matmul_at(mid_down, g[...]).astype(jnp.bfloat16)
        to_members.wait()
        id_trade.wait()
        share_ref[...] = third[...]
        ids_out[...] = id_tiles[...]
        for trade in (over_members, over_places, to_members, id_trade):
            trade.finish()


def mlp(mlp_in, grad_rows, up_slots, down_slots, chosen, frozen_bias, kvp, ids, length):
    rows = mlp_in.shape[0]
    prompt_total, prompt_rows = kvp.shape[1], rows - length
    places = lax.axis_size("ctx")
    slots, _, up_share = up_slots.shape
    down_share = down_slots.shape[2]
    wide = math.gcd(up_share, 512)
    per = up_share // wide

    def whole(shape):
        return pl.BlockSpec(shape, lambda step: (0,) * len(shape))

    def columns(start, width):
        return pl.BlockSpec((R, width), lambda step: (0, start // width))

    def moving(height, start):
        return pl.BlockSpec((height, wide), lambda step: (0, start // wide + step))

    return pl.pallas_call(
        functools.partial(mlp_kernel, length),
        grid=(FF // wide,),
        in_specs=[
            pl.BlockSpec(memory_space=pl.ANY),
            pl.BlockSpec(memory_space=pl.ANY),
            pl.BlockSpec((1, D, wide), lambda step: (step // per, 0, step % per)),
            pl.BlockSpec((slots, wide, down_share), lambda step: (0, step, 0)),
            columns(0, D),
            moving(R, D),
            moving(R, D + FF),
            columns(D + 2 * FF, D),
            moving(1, 4 * D),
            pl.BlockSpec(memory_space=pl.ANY),
            pl.BlockSpec(memory_space=pltpu.SMEM),
        ]
        + [whole((prompt_total, 2 * HD))] * 3,
        out_specs=[
            whole((rows, D)),
            whole((rows, D)),
            whole((R, 2 * D + 2 * FF)),
            whole((slots, prompt_rows, 2 * D // slots)),
            whole((places, 8, 2 * HD)),
        ],
        out_shape=[
            jax.ShapeDtypeStruct((rows, D), jnp.float32),
            jax.ShapeDtypeStruct((rows, D), jnp.float32),
            jax.ShapeDtypeStruct((R, 2 * D + 2 * FF), jnp.bfloat16),
            jax.ShapeDtypeStruct((slots, prompt_rows, 2 * D // slots), jnp.bfloat16),
            jax.ShapeDtypeStruct((places, 8, 2 * HD), jnp.float32),
        ],
        scratch_shapes=[
            pltpu.VMEM((rows, R), jnp.bfloat16),
            pltpu.VMEM((rows, R), jnp.bfloat16),
            pltpu.VMEM((rows, R), jnp.float32),
            pltpu.VMEM((rows, R), jnp.float32),
            pltpu.VMEM((slots, prompt_total, 2 * D // slots), jnp.bfloat16),
            pltpu.VMEM((prompt_total, 2 * D // slots), jnp.bfloat16),
            pltpu.VMEM((places, prompt_rows, 2 * D // slots), jnp.bfloat16),
            pltpu.VMEM((slots, prompt_rows, 2 * D // slots), jnp.bfloat16),
            pltpu.VMEM((places, 8, 2 * HD), jnp.float32),
            pltpu.VMEM((rows, D), jnp.bfloat16),
            pltpu.VMEM((rows, D), jnp.bfloat16),
            pltpu.VMEM((D, wide), jnp.bfloat16),
            pltpu.VMEM((wide, D), jnp.bfloat16),
            pltpu.SemaphoreType.DMA,
            pltpu.SemaphoreType.DMA((2,)),
        ]
        + trade_sems(slots)
        + trade_sems(places)
        + trade_sems(slots)
        + trade_sems(places),
        compiler_params=pltpu.CompilerParams(
            collective_id=3, has_side_effects=True, vmem_limit_bytes=VMEM_BYTES
        ),
        cost_estimate=pl.CostEstimate(
            flops=8 * rows * D * FF,
            bytes_accessed=30 * 1024 * 1024,
            transcendentals=2 * rows * FF,
        ),
    )(
        mlp_in,
        grad_rows,
        up_slots,
        down_slots,
        chosen,
        chosen,
        chosen,
        chosen,
        frozen_bias[None],
        kvp,
        ids,
        *turn_tables(prompt_total),
    )


def tail_kernel(
    length,
    x_ref,
    xp_ref,
    g_ref,
    ob_ref,
    dq_ref,
    dk_ref,
    dv_ref,
    share_ref,
    a1_ref,
    mlp_ref,
    d_mlp_ref,
    wq_ref,
    wo_ref,
    picked,
    mid_qkv,
    d_mid_out,
    back_ref,
    ids_ref,
    bias_ref,
    gain_ref,
    cont_out,
    prompt_out,
    cont_grad,
    prompt_grad,
    sums_ref,
    norm_ref,
    x,
    g,
    ob,
    dqkv,
    a1,
    result,
    d_rows,
    wq,
    wo,
    mid_out,
    d_mid_qkv,
    grads,
    first,
    bins,
    second,
    full,
    norm_members,
    norm_places,
    load_sems,
    store_sems,
    *sems,
):
    rows = x.shape[0]
    prompt_rows = rows - length
    places, members, owned = full.shape[0], second.shape[0], full.shape[1]
    width = first.shape[2]
    part = 2 * D // members
    slots, _, share = wq.shape
    out_share = wo.shape[2]
    ctx, me = lax.axis_index("ctx"), lax.axis_index("fsdp")
    parity, line, lines = ctx % 2, ctx // 2, places // 2
    sibling = ctx + 1 - 2 * parity
    own_rows, prompt_at = pl.ds(0, length), pl.ds(length, prompt_rows)

    front_places = 6 * D // width
    pairs = [
        (back_ref, grads.at[:, pl.ds(6 * D, WTOT - 6 * D)]),
        (dq_ref, dqkv.at[:, pl.ds(0, D)]),
        (dk_ref, dqkv.at[own_rows, pl.ds(D, D)]),
        (dv_ref, dqkv.at[own_rows, pl.ds(2 * D, D)]),
        (a1_ref.at[pl.ds(a1_ref.shape[0] - length, length)], a1),
        (ob_ref, ob),
        (g_ref, g),
        (wo_ref, wo),
        (x_ref, x.at[own_rows]),
        (xp_ref, x.at[prompt_at]),
        (mlp_ref, result),
        (wq_ref, wq),
        (d_mlp_ref, d_rows),
    ] + [
        (share_ref.at[slot], dqkv.at[prompt_at, pl.ds(D + slot * part, part)])
        for slot in range(members)
    ]
    loads = [
        pltpu.make_async_copy(source, target, load_sems.at[index])
        for index, (source, target) in enumerate(pairs)
    ]
    for load in loads:
        load.start()

    def grad_part(place):
        return grads.at[:, pl.ds(pl.multiple_of(place * width, width), width)]

    def line_place(offset, side):
        return flip(line, offset) * 2 + side

    over_places = Trade("ctx", places, grad_part, first, sems[0:2])
    over_members = Trade(
        "fsdp", members, lambda place: bins.at[pl.ds(place * owned, owned)], second, sems[2:4]
    )
    norm_a = Trade("fsdp", members, lambda place: norm_members.at[me], norm_members, sems[4:6])
    norm_b = Trade("ctx", places, lambda place: norm_places.at[ctx], norm_places, sems[6:8])
    line_sems, gift_sems = sems[8:10], sems[10:12]

    def line_send(offset):
        part_ref = full.at[ctx]
        return remote_copy(
            part_ref, part_ref, line_sems, offset, (line_place(offset, parity), me)
        )

    def line_landed(offset):
        part_ref = full.at[line_place(offset, parity)]
        return remote_copy(
            part_ref, part_ref, line_sems, offset, (line_place(offset, parity), me)
        )

    def gift(offset, taken=False):
        side = 1 - parity if taken else parity
        part_ref = full.at[line_place(offset, side)]
        return remote_copy(part_ref, part_ref, gift_sems, offset, (sibling, me))

    greet_all(
        [(ctx, flip(me, offset)) for offset in range(1, members)]
        + [(flip(ctx, offset), me) for offset in range(1, places)]
    )

    def send_grads(front):
        for offset in reversed(range(1, places)):
            is_front = flip(ctx, offset) < front_places

            @pl.when(is_front if front else jnp.logical_not(is_front))
            def _():
                over_places.send(offset).start()

    loads[0].wait()
    send_grads(False)
    for load in loads[1:7]:
        load.wait()
    low = jnp.bfloat16
    d_mid_qkv[prompt_at, :] = jnp.zeros((prompt_rows, R), low)
    mid_out[prompt_at, :] = jnp.zeros((prompt_rows, R), low)
    tile = ROW_TILE
    grad_parts = [None] * 4
    for start in range(0, length, tile):
        at = pl.ds(start, tile)
        d_middle = matmul_bt(dqkv[at, :], picked[:, D : 4 * D]).astype(low)
        middle = matmul_bt(ob[at, :], picked[:, 4 * D : 5 * D]).astype(low)
        d_mid_qkv[at, :] = d_middle
        mid_out[at, :] = middle
        parts = (
            matmul_at(d_middle, a1[at, :]),
            matmul_at(mid_qkv[at, :], dqkv[at, :]),
            matmul_at(d_mid_out[at, :], ob[at, :]),
            matmul_at(middle, g[at, :]),
        )
        grad_parts = [
            new if old is None else old + new for old, new in zip(grad_parts, parts)
        ]
    for start, value in zip((0, D, 4 * D, 5 * D), grad_parts):
        grads[:, start : start + value.shape[1]] = value.astype(low)
    send_grads(True)
    for load in loads[7:11]:
        load.wait()
    tiles = [(start, min(OUT_TILE, rows - start)) for start in range(0, rows, OUT_TILE)]
    def out_rows(start, size):
        at = pl.ds(start, size)
        adapted = matmul(mid_out[at, :], picked[:, 5 * D : 6 * D])
        for slot in range(slots):
            lanes = slice(slot * out_share, (slot + 1) * out_share)
            first_bias = bias_ref[:, 3 * D + slot * out_share : 3 * D + (slot + 1) * out_share]
            second_start = 4 * D + FF + slot * out_share
            second_bias = bias_ref[:, second_start : second_start + out_share]
            result[at, lanes] += (
                x[at, lanes].astype(jnp.float32)
                + matmul(ob[at, :], wo[slot])
                + adapted[:, lanes]
                + first_bias
                + second_bias
            )

    def back_rows(start, size):
        at = pl.ds(start, size)
        d_attn_in = matmul(d_mid_qkv[at, :], picked[:, :D])
        for slot in range(slots):
            d_attn_in += matmul_bt(dqkv[at, slot * share : (slot + 1) * share], wq[slot])
        for row in range(0, size, 16):
            row_at = pl.ds(start + row, 16)
            values = x[row_at, :].astype(jnp.float32)
            centered = values - jnp.mean(values, axis=-1, keepdims=True)
            variance = jnp.mean(centered * centered, axis=-1, keepdims=True)
            scale = lax.rsqrt(variance + 1e-05)
            unit = centered * scale
            d_unit = d_attn_in[row : row + 16] * gain_ref[0:1, :]
            d_unit += d_rows[row_at, :] * gain_ref[1:2, :]
            mean_d = jnp.mean(d_unit, axis=-1, keepdims=True)
            mean_du = jnp.mean(d_unit * unit, axis=-1, keepdims=True)
            d_rows[row_at, :] = g[row_at, :].astype(jnp.float32) + scale * (
                d_unit - mean_d - unit * mean_du
            )

    half = len(tiles) // 2
    for start, size in tiles[:half]:
        out_rows(start, size)

    over_places.wait()
    first[ctx] = grad_part(ctx)[...]
    for index in range(members * owned):
        total = None
        for place in range(places):
            matches = ids_ref[place, 0:1, 0:1] == float(index)
            piece = jnp.where(matches, first[place].astype(jnp.float32), 0.0)
            total = piece if total is None else total + piece
        bins[index] = total.astype(low)
    over_members.start()

    for start, size in tiles[half:]:
        out_rows(start, size)
    stores = [
        pltpu.make_async_copy(result.at[own_rows], cont_out, store_sems.at[0]),
        pltpu.make_async_copy(result.at[prompt_at], prompt_out, store_sems.at[1]),
    ]
    for store in stores:
        store.start()
    for load in loads[11:]:
        load.wait()

    over_members.wait()
    second[me] = bins[pl.ds(me * owned, owned)]
    total = second[0].astype(jnp.float32)
    for member in range(1, members):
        total += second[member].astype(jnp.float32)
    full[ctx] = total.astype(low)
    for offset in reversed(range(1, lines)):
        line_send(offset).start()
    gift(0).start()
    norm_members[me] = jnp.full(norm_members.shape[1:], jnp.sum(total * total))
    norm_a.start()

    for start, size in tiles[:1]:
        back_rows(start, size)
    norm_a.wait()
    square = norm_members[0]
    for member in range(1, members):
        square = square + norm_members[member]
    norm_places[ctx] = square
    norm_b.start()
    for start, size in tiles[1 : half + 1]:
        back_rows(start, size)
    for offset in reversed(range(1, lines)):
        line_landed(offset).wait_recv()
        gift(offset).start()
    for start, size in tiles[half + 1 :]:
        back_rows(start, size)
    stores += [
        pltpu.make_async_copy(d_rows.at[own_rows], cont_grad, store_sems.at[2]),
        pltpu.make_async_copy(d_rows.at[prompt_at], prompt_grad, store_sems.at[3]),
    ]
    for store in stores[2:]:
        store.start()
    norm_b.wait()
    square = norm_places[0]
    for place in range(1, places):
        square = square + norm_places[place]
    norm_ref[...] = jnp.sqrt(square)
    for offset in range(lines):
        gift(offset, taken=True).wait_recv()
    sums_ref[...] = full[...]
    for trade in (over_places, over_members, norm_a, norm_b):
        trade.finish()
    for offset in range(1, lines):
        line_send(offset).wait_send()
    for offset in range(lines):
        gift(offset).wait_send()
    for store in stores:
        store.wait()


def tail(
    x_cont,
    x_prompt,
    grad_rows,
    attended,
    dq_rows,
    dk_own,
    dv_own,
    prompt_share,
    attn_in,
    mlp_out,
    d_mlp_in,
    qkv_slots,
    out_slots,
    picked,
    mid_qkv,
    d_mid_out,
    back_grads,
    id_tiles,
    frozen_bias,
    norm_gain,
    owned,
):
    rows, length, prompt_rows = attended.shape[0], x_cont.shape[0], x_prompt.shape[0]
    places, members = lax.axis_size("ctx"), lax.axis_size("fsdp")
    width = WTOT // places
    low, wide = jnp.bfloat16, jnp.float32
    anywhere = pl.BlockSpec(memory_space=pl.ANY)
    on_chip = pl.BlockSpec(memory_space=pltpu.VMEM)
    return pl.pallas_call(
        functools.partial(tail_kernel, length),
        in_specs=[anywhere] * 13 + [on_chip] * 3 + [anywhere] + [on_chip] * 3,
        out_specs=[anywhere] * 4 + [on_chip] * 2,
        out_shape=[
            jax.ShapeDtypeStruct((length, D), wide),
            jax.ShapeDtypeStruct((prompt_rows, D), wide),
            jax.ShapeDtypeStruct((length, D), wide),
            jax.ShapeDtypeStruct((prompt_rows, D), wide),
            jax.ShapeDtypeStruct((places, owned, R, width), low),
            jax.ShapeDtypeStruct((8, 2 * HD), wide),
        ],
        scratch_shapes=[
            pltpu.VMEM((rows, D), low),
            pltpu.VMEM((rows, D), low),
            pltpu.VMEM((rows, D), low),
            pltpu.VMEM((rows, 3 * D), low),
            pltpu.VMEM((length, D), low),
            pltpu.VMEM((rows, D), wide),
            pltpu.VMEM((rows, D), wide),
            pltpu.VMEM(qkv_slots.shape, low),
            pltpu.VMEM(out_slots.shape, low),
            pltpu.VMEM((rows, R), low),
            pltpu.VMEM((rows, R), low),
            pltpu.VMEM((R, WTOT), low),
            pltpu.VMEM((places, R, width), low),
            pltpu.VMEM((members * owned, R, width), low),
            pltpu.VMEM((members, owned, R, width), low),
            pltpu.VMEM((places, owned, R, width), low),
            pltpu.VMEM((members, 8, 2 * HD), wide),
            pltpu.VMEM((places, 8, 2 * HD), wide),
            pltpu.SemaphoreType.DMA((13 + members,)),
            pltpu.SemaphoreType.DMA((4,)),
        ]
        + trade_sems(places)
        + trade_sems(members)
        + trade_sems(members)
        + trade_sems(places)
        + [pltpu.SemaphoreType.DMA((places // 2,)) for _ in range(4)],
        compiler_params=pltpu.CompilerParams(
            collective_id=4, has_side_effects=True, vmem_limit_bytes=VMEM_BYTES
        ),
        cost_estimate=pl.CostEstimate(
            flops=2 * rows * D * 4 * D, bytes_accessed=50 * 1024 * 1024, transcendentals=rows
        ),
    )(
        x_cont,
        x_prompt,
        grad_rows,
        attended,
        dq_rows,
        dk_own,
        dv_own,
        prompt_share,
        attn_in,
        mlp_out,
        d_mlp_in,
        qkv_slots,
        out_slots,
        picked,
        mid_qkv,
        d_mid_out,
        back_grads,
        id_tiles,
        frozen_bias[None],
        norm_gain,
    )


def update_kernel(
    sums_ref,
    norm_ref,
    sets_ref,
    first_ref,
    second_ref,
    rate_ref,
    cont_out_ref,
    cont_grad_ref,
    prompt_out_ref,
    prompt_grad_ref,
    new_sets,
    new_first,
    new_second,
    low_sets,
    cont_out,
    cont_grad,
    prompt_out,
    prompt_grad,
    norm_out,
):
    cont_out[...] = cont_out_ref[...]
    cont_grad[...] = cont_grad_ref[...]
    prompt_out[...] = prompt_out_ref[...]
    prompt_grad[...] = prompt_grad_ref[...]
    norm_out[0] = norm_ref[0, 0]
    limit = 0.1 * math.sqrt(SETS * R * WTOT)
    norm = norm_ref[0:1, 0:1]
    ratio = limit / jnp.maximum(norm, limit)
    rate = rate_ref[...]
    for index in range(sets_ref.shape[0]):
        clipped = sums_ref[0, index].astype(jnp.float32) * ratio
        first = beta_one * first_ref[index] + (1.0 - beta_one) * clipped
        second = beta_two * second_ref[index] + (1.0 - beta_two) * clipped * clipped
        corrected_first = first / (1.0 - beta_one**STEP)
        corrected_second = second / (1.0 - beta_two**STEP)
        old = sets_ref[index]
        new = old - rate * (
            corrected_first / (jnp.sqrt(corrected_second) + adam_eps) + weight_decay * old
        )
        new_first[index] = first
        new_second[index] = second
        new_sets[index] = new
        low_sets[index] = new.astype(jnp.bfloat16)


def update(sums, norm, adapters, first_moment, second_moment, rows_out):
    places, owned, _, width = sums.shape
    rates = np.where(up_columns(), rate_up, rate_down).astype(np.float32)[None]
    length, prompt_rows = rows_out[0].shape[0], rows_out[2].shape[0]

    def columns():
        return pl.BlockSpec((owned, R, width), lambda place: (0, 0, place))

    def shaped(kind):
        return jax.ShapeDtypeStruct(adapters.shape, kind)

    moving = [pl.BlockSpec((length // places, D), lambda place: (place, 0))] * 2
    moving += [pl.BlockSpec((prompt_rows, D), lambda place: (0, 0))] * 2
    return pl.pallas_call(
        update_kernel,
        grid=(places,),
        in_specs=[
            pl.BlockSpec((1, owned, R, width), lambda place: (place, 0, 0, 0)),
            pl.BlockSpec((8, 2 * HD), lambda place: (0, 0)),
            columns(),
            columns(),
            columns(),
            pl.BlockSpec((1, width), lambda place: (0, place)),
        ]
        + moving,
        out_specs=[columns()] * 4 + moving + [pl.BlockSpec(memory_space=pltpu.SMEM)],
        out_shape=[shaped(jnp.float32)] * 3
        + [shaped(jnp.bfloat16)]
        + [jax.ShapeDtypeStruct(row.shape, jnp.float32) for row in rows_out]
        + [jax.ShapeDtypeStruct((1,), jnp.float32)],
        compiler_params=pltpu.CompilerParams(vmem_limit_bytes=VMEM_BYTES),
    )(sums, norm, adapters, first_moment, second_moment, rates, *rows_out)


def per_device(
    x_prompt,
    x_cont,
    dy_prompt,
    dy_cont,
    adapter_ids,
    w_qkv,
    w_out,
    w_up,
    w_down,
    frozen_bias,
    norm_gain,
    norm_shift,
    adapters,
    first_moment,
    second_moment,
):
    length = x_cont.shape[1]
    (
        qkv,
        attn_in,
        mlp_in,
        d_attended,
        grad_rows,
        qkv_slots,
        out_slots,
        low_sets,
        picked,
        mid_qkv,
        d_mid_out,
    ) = front(
        adapter_ids,
        x_cont[0],
        x_prompt,
        dy_cont[0],
        dy_prompt,
        w_qkv,
        w_out,
        adapters,
        frozen_bias[None],
        norm_gain,
        norm_shift,
    )
    attended, dq_rows, dk_own, dv_own, kv_prompt, up_slots, down_slots, chosen = attention(
        adapter_ids, qkv, d_attended, w_up, w_down, low_sets, length
    )
    mlp_out, d_mlp_in, back_grads, prompt_share, id_tiles = mlp(
        mlp_in,
        grad_rows,
        up_slots,
        down_slots,
        chosen,
        frozen_bias,
        kv_prompt,
        adapter_ids,
        length,
    )
    cont_out, prompt_out, cont_grad, prompt_grad, sums, norm = tail(
        x_cont[0],
        x_prompt,
        grad_rows,
        attended,
        dq_rows,
        dk_own,
        dv_own,
        prompt_share,
        attn_in,
        mlp_out,
        d_mlp_in,
        qkv_slots,
        out_slots,
        picked,
        mid_qkv,
        d_mid_out,
        back_grads,
        id_tiles,
        frozen_bias,
        norm_gain,
        adapters.shape[0],
    )
    new_sets, new_first, new_second, low_new, cont_out, cont_grad, prompt_out, prompt_grad, norm = (
        update(
            sums,
            norm,
            adapters,
            first_moment,
            second_moment,
            (cont_out, cont_grad, prompt_out, prompt_grad),
        )
    )
    return (
        prompt_out,
        prompt_grad,
        cont_out[None],
        cont_grad[None],
        norm.reshape(()),
        new_sets,
        new_first,
        new_second,
        low_new,
    )


def solution(mesh):
    in_specs = (
        P("ctx", None),
        P(("ctx", "fsdp"), None, None),
        P("ctx", None),
        P(("ctx", "fsdp"), None, None),
        P(("ctx", "fsdp")),
        P(None, "fsdp"),
        P(None, "fsdp"),
        P(None, "fsdp"),
        P(None, "fsdp"),
        P(),
        P(),
        P(),
        P("fsdp", None, None),
        P("fsdp", None, None),
        P("fsdp", None, None),
    )
    out_specs = (
        P("ctx", None),
        P("ctx", None),
        P(("ctx", "fsdp"), None, None),
        P(("ctx", "fsdp"), None, None),
        P(),
        P("fsdp", None, None),
        P("fsdp", None, None),
        P("fsdp", None, None),
        P("fsdp", None, None),
    )
    return jax.shard_map(
        per_device, mesh=mesh, in_specs=in_specs, out_specs=out_specs, check_vma=False
    )
```
